256 devices in a mesh: grp: 16 (over x, y), dev: 16 (over z, core).
Axes of the slice: x: 4, y: 4, z: 8, core: 2. Of those that a mesh axis runs over, the one named last changes fastest.
Arguments:
- features: bfloat16 [2048, 8, 8, 512], P(('grp', 'dev')), may hold values from -6 to 6
- cotangent: bfloat16 [2048, 8, 8, 512], P(('grp', 'dev')), may hold values from -6 to 6
- timesteps: int32 [2048], P(('grp', 'dev')), may hold values from 0 to 999
- face_links: int32 [2048, 6], P(('grp', 'dev')), may hold values from -1 to 39, as said below
- face_sources: int32 [256, 16, 2], P(('grp', 'dev')), may hold values from -1 to 47, as said below
- coarse_targets: int32 [2048], P(('grp', 'dev')), may hold values from 0 to 15, as said below
- coarse_places: int32 [256, 16, 1], P(('grp', 'dev')), may hold values from -1 to 63, as said below
- time_weight: float32 [64, 128], replicated, may hold values from -0.75 to 0.75
- fine_weight: bfloat16 [7, 64, 64], replicated, may hold values from -0.25 to 0.25
- down_weight: bfloat16 [64, 128], replicated, may hold values from -2 to 2
- coarse_weight: bfloat16 [7, 128, 128], replicated, may hold values from -0.1875 to 0.1875
- up_weight: bfloat16 [128, 64], replicated, may hold values from -1 to 1
Outputs:
- mixed_out: bfloat16 [2048, 8, 8, 512], P(('grp', 'dev'))
- input_grad: bfloat16 [2048, 8, 8, 512], P(('grp', 'dev'))
- fine_grad: float32 [7, 64, 64], replicated
- down_grad: float32 [64, 128], replicated
- coarse_grad: float32 [7, 128, 128], replicated
- up_grad: float32 [128, 64], replicated
- time_grad: float32 [64, 128], replicated
The draws below stay inside these ranges and needn't reach their ends.
Inputs may be any that keep to these rules, and one draw needn't show every extreme that they name: `face_links`: -1 is no neighbour; below 8 a brick of the same device; else a received slot as in the reference program; each received slot is named once; on every device the last peer of its group, and some other, fill all 2 slots. `face_sources`: -1 marks an unused slot; a used slot names brick * 6 + side of the providing device. `coarse_targets`: each brick names one slot, each slot at most one brick; some owners of each group receive all 1 slots from every device of the group. `coarse_places`: -1 exactly for slots that no brick names; used positions are distinct on each owner.
All inputs are finite; a program needn't handle non-finite values.
Results may differ from the reference program's by a relative error of at most 0.014.
Values may be sent and summed in bfloat16 or wider, within the bound.
A program may use at most 128 MiB of HBM per device.

```python
import math
import jax
import jax.numpy as jnp
from jax import lax

CHANNELS = 64
COARSE_CH = 128
GROUPS = 32
BRICK_DEV = 8
COARSE_DEV = 1
FACE_SLOTS = 2
COARSE_SLOTS = 1
BRICKS = 2048
N_GRP = 16
N_DEV = 16
DEVICES = 256


def halo_tables(key):
    key = jax.random.fold_in(key, 11)
    slot_total = N_DEV * FACE_SLOTS
    pair_total = BRICK_DEV * 6

    def one_device(device_key):
        key_list = jax.random.split(device_key, 5)
        counts = jax.random.randint(key_list[0], (N_DEV,), 1, FACE_SLOTS + 1)
        fullest = jax.random.randint(key_list[1], (), 0, N_DEV)
        counts = counts.at[fullest].set(FACE_SLOTS).at[N_DEV - 1].set(FACE_SLOTS)
        valid_slot = (jnp.arange(FACE_SLOTS)[None, :] < counts[:, None]).reshape(-1)
        slot_rank = jnp.cumsum(valid_slot.astype(jnp.int32)) - 1
        used_total = jnp.sum(valid_slot.astype(jnp.int32))
        pair_order = jax.random.permutation(key_list[2], pair_total)
        first_position = jnp.argsort(pair_order, stable=True)
        held_pair = pair_order[used_total - 1]
        pair_order = pair_order.at[first_position[4]].set(held_pair).at[used_total - 1].set(4)
        position = jnp.argsort(pair_order, stable=True)
        slot_by_rank = jnp.argsort(jnp.where(valid_slot, 0, 1), stable=True)
        local_limit = used_total + (pair_total - used_total) // 2
        others = jax.random.randint(key_list[3], (pair_total,), 1, BRICK_DEV)
        local_pick = (jnp.arange(pair_total) // 6 + others) % BRICK_DEV
        remote_code = BRICK_DEV + slot_by_rank[jnp.minimum(position, slot_total - 1)]
        link_codes = jnp.where(position < used_total, remote_code, jnp.where(position < local_limit, local_pick, -1))
        slot_pair = pair_order[jnp.clip(slot_rank, 0, pair_total - 1)]
        side_index = slot_pair % 6
        opposite_side = side_index + 1 - 2 * (side_index % 2)
        sender_brick = jax.random.randint(key_list[4], (slot_total,), 0, BRICK_DEV)
        sender_brick = sender_brick.at[slot_total - 1].set(BRICK_DEV - 1)
        slot_codes = jnp.where(valid_slot, sender_brick * 6 + opposite_side, -1)
        return (link_codes.reshape(BRICK_DEV, 6).astype(jnp.int32), slot_codes.reshape(N_DEV, FACE_SLOTS).astype(jnp.int32))
    device_keys = jax.random.split(key, DEVICES)
    link_codes, slot_codes = jax.vmap(one_device)(device_keys)
    sources = slot_codes.reshape(N_GRP, N_DEV, N_DEV, FACE_SLOTS).swapaxes(1, 2).reshape(DEVICES, N_DEV, FACE_SLOTS)
    return (link_codes.reshape(BRICKS, 6), sources)


def coarse_tables(key):
    key = jax.random.fold_in(key, 23)
    slot_total = N_DEV * COARSE_SLOTS
    hot_count = max(N_DEV // 4, 1)

    def one_group(group_key):
        key_list = jax.random.split(group_key, N_DEV + 2)
        ranking = jax.random.permutation(key_list[0], N_DEV)
        hot_peer = ranking < hot_count

        def one_source(source_key):
            part_keys = jax.random.split(source_key, 2)
            noise_draw = jax.random.randint(part_keys[0], (slot_total,), 0, 1 << 16)
            slot_peer = jnp.arange(slot_total) // COARSE_SLOTS
            rank_score = (noise_draw + jnp.where(hot_peer[slot_peer], 0, 1 << 17)) * slot_total + jnp.arange(slot_total)
            chosen = jnp.argsort(rank_score, stable=True)[:BRICK_DEV].astype(jnp.int32)
            bricks = jax.random.permutation(part_keys[1], BRICK_DEV)
            targets = jnp.zeros((BRICK_DEV,), jnp.int32).at[bricks].set(chosen)
            selected = jnp.zeros((slot_total,), jnp.int32).at[chosen].set(1)
            return (targets, selected.reshape(N_DEV, COARSE_SLOTS))
        targets, selected = jax.vmap(one_source)(key_list[1:N_DEV + 1])
        received = jnp.swapaxes(selected, 0, 1)

        def one_owner(owner_key, mark_table):
            free_spots = jax.random.permutation(owner_key, COARSE_DEV * 64)[:slot_total]
            return jnp.where(mark_table.reshape(-1) > 0, free_spots, -1).reshape(N_DEV, COARSE_SLOTS).astype(jnp.int32)
        owner_keys = jax.random.split(key_list[N_DEV + 1], N_DEV)
        places = jax.vmap(one_owner)(owner_keys, received)
        return (targets, places)
    group_keys = jax.random.split(key, N_GRP)
    targets, places = jax.vmap(one_group)(group_keys)
    return (targets.reshape(BRICKS), places.reshape(DEVICES, N_DEV, COARSE_SLOTS))


def draw_face_links(key, part):
    return halo_tables(key)[0]


def draw_face_sources(key, part):
    return halo_tables(key)[1]


def draw_coarse_targets(key, part):
    return coarse_tables(key)[0]


def draw_coarse_places(key, part):
    return coarse_tables(key)[1]


def touch_ends(entries, key, least, high):
    index_at = [jax.random.randint(jax.random.fold_in(key, axis), (), 0, length) for axis, length in enumerate(entries.shape)]
    main_axis = entries.shape.index(max(entries.shape))
    next_to = index_at[:main_axis] + [(index_at[main_axis] + 1) % entries.shape[main_axis]] + index_at[main_axis + 1:]
    return entries.at[tuple(index_at)].set(least).at[tuple(next_to)].set(high)


def block_scale(own_key, shape, cuts, low, top_value):
    level, own = 1.0, jax.random.fold_in(own_key, 6)
    for dim, blocks in cuts:
        heights = jnp.exp(jax.random.uniform(jax.random.fold_in(own, dim), (blocks,), jnp.float32, low / len(cuts), top_value / len(cuts)))
        level = level * jnp.repeat(heights, shape[dim] // blocks).reshape([-1 if axis == dim else 1 for axis in range(len(shape))])
    return level


def scatter_about(key, dims, scale, bound, cuts=(), kind=jnp.bfloat16):
    entries = scale * jax.random.normal(key, dims, jnp.float32)
    if cuts:
        entries = entries * block_scale(key, dims, cuts, -0.22, 0.18)
    return jnp.clip(entries, -bound, bound).astype(kind)


def setup_inputs(seed: int = 0) -> dict:
    splits = jax.random.split(jax.random.key(seed), 13)
    features = scatter_about(splits[0], (BRICKS, 8, 8, 8 * CHANNELS), 1.0, 6.0, ((0, 256),))
    cotangent = scatter_about(splits[1], (BRICKS, 8, 8, 8 * CHANNELS), 1.0, 6.0, ((0, 256),))
    timesteps = touch_ends(jax.random.randint(splits[2], (BRICKS,), 0, 1000), jax.random.fold_in(splits[2], 1), 0, 999).astype(jnp.int32)
    face_links = draw_face_links(jax.random.fold_in(splits[12], 71), 0)
    face_sources = draw_face_sources(jax.random.fold_in(splits[12], 71), 0)
    coarse_targets = draw_coarse_targets(jax.random.fold_in(splits[12], 71), 0)
    coarse_places = draw_coarse_places(jax.random.fold_in(splits[12], 71), 0)
    time_weight = scatter_about(splits[7], (CHANNELS, 2 * CHANNELS), CHANNELS ** -0.5, 0.75, (), jnp.float32)
    fine_weight = scatter_about(splits[8], (7, CHANNELS, CHANNELS), (7 * CHANNELS) ** -0.5, 0.25)
    down_weight = scatter_about(splits[9], (CHANNELS, COARSE_CH), (CHANNELS // 8) ** -0.5, 2.0)
    coarse_weight = scatter_about(splits[10], (7, COARSE_CH, COARSE_CH), (7 * COARSE_CH) ** -0.5, 0.1875)
    up_weight = scatter_about(splits[11], (COARSE_CH, CHANNELS), (COARSE_CH // 4) ** -0.5, 1.0)
    return {"features": features, "cotangent": cotangent, "timesteps": timesteps, "face_links": face_links, "face_sources": face_sources, "coarse_targets": coarse_targets, "coarse_places": coarse_places, "time_weight": time_weight, "fine_weight": fine_weight, "down_weight": down_weight, "coarse_weight": coarse_weight, "up_weight": up_weight}


OPPOSITE = (1, 0, 3, 2, 5, 4)
EPSILON = 1e-05

def brick_view(packed):
    return packed.reshape(packed.shape[0], 8, 8, 8, packed.shape[-1] // 8)

def time_embedding(step_ids, channels):
    half_width = channels // 2
    frequency = jnp.exp(-math.log(10000.0) * jnp.arange(half_width).astype(jnp.float32) / half_width)
    angles = step_ids.astype(jnp.float32)[:, None] * frequency[None, :]
    return jnp.concatenate([jnp.cos(angles), jnp.sin(angles)], axis=1)

def activate(packed, step_ids, time_weight, groups):
    volume = brick_view(packed).astype(jnp.float32)
    brick_count = volume.shape[0]
    channels = volume.shape[-1]
    grouped = volume.reshape(brick_count, 512, groups, channels // groups)
    centre_mean = lax.optimization_barrier(jnp.mean(grouped, axis=(1, 3), keepdims=True))
    spread = lax.optimization_barrier(jnp.mean(jnp.square(grouped - centre_mean), axis=(1, 3), keepdims=True))
    inverse = lax.rsqrt(spread + EPSILON)
    normed = ((grouped - centre_mean) * inverse).reshape(brick_count, 8, 8, 8, channels)
    embedding = time_embedding(step_ids, channels)
    modulate = jnp.dot(embedding, time_weight, precision=lax.Precision.HIGHEST)
    scale_term = modulate[:, :channels][:, None, None, None, :]
    shift_term = modulate[:, channels:][:, None, None, None, :]
    before = normed * (1.0 + scale_term) + shift_term
    return (before, normed, inverse, embedding, scale_term)

def face_table(volume):
    layers = [volume[:, 0], volume[:, 7], volume[:, :, 0], volume[:, :, 7], volume[:, :, :, 0], volume[:, :, :, 7]]
    return jnp.stack(layers, axis=1)

def add_faces(volume, layers):
    volume = volume.at[:, 0].add(layers[:, 0])
    volume = volume.at[:, 7].add(layers[:, 1])
    volume = volume.at[:, :, 0].add(layers[:, 2])
    volume = volume.at[:, :, 7].add(layers[:, 3])
    volume = volume.at[:, :, :, 0].add(layers[:, 4])
    volume = volume.at[:, :, :, 7].add(layers[:, 5])
    return volume

def padded_volume(volume, layers):
    brick_count = volume.shape[0]
    channels = volume.shape[-1]
    padded = jnp.zeros((brick_count, 10, 10, 10, channels), volume.dtype)
    padded = padded.at[:, 1:9, 1:9, 1:9].set(volume)
    padded = padded.at[:, 0, 1:9, 1:9].set(layers[:, 0])
    padded = padded.at[:, 9, 1:9, 1:9].set(layers[:, 1])
    padded = padded.at[:, 1:9, 0, 1:9].set(layers[:, 2])
    padded = padded.at[:, 1:9, 9, 1:9].set(layers[:, 3])
    padded = padded.at[:, 1:9, 1:9, 0].set(layers[:, 4])
    padded = padded.at[:, 1:9, 1:9, 9].set(layers[:, 5])
    return padded

def tap_stack(padded, direction_sign):
    pieces = [padded[:, 1:9, 1:9, 1:9]]
    for direction in range(6):
        offset = 1 + direction_sign * (2 * (direction % 2) - 1)
        starts = [1, 1, 1]
        starts[direction // 2] = offset
        pieces.append(padded[:, starts[0]:starts[0] + 8, starts[1]:starts[1] + 8, starts[2]:starts[2] + 8])
    return jnp.concatenate(pieces, axis=-1)

def pick_rows(values, indices):
    zero_row = jnp.zeros((1,) + values.shape[1:], values.dtype)
    return jnp.concatenate([values, zero_row], axis=0)[indices]

def slot_bricks(targets, slot_count):
    brick_count = targets.shape[0]
    return jnp.full((slot_count,), brick_count, jnp.int32).at[targets].set(jnp.arange(brick_count).astype(jnp.int32))

def place_slots(places, place_count):
    slot_count = places.size
    flat_places = places.reshape(-1)
    target = jnp.where(flat_places < 0, place_count, flat_places)
    filled = jnp.full((place_count + 1,), slot_count, jnp.int32).at[target].set(jnp.arange(slot_count).astype(jnp.int32))
    return filled[:place_count]

def places_to_grid(placed, coarse_count):
    channels = placed.shape[-1]
    shaped = placed.reshape(coarse_count, 4, 4, 4, 2, 2, 2, channels)
    return shaped.transpose(0, 1, 4, 2, 5, 3, 6, 7).reshape(coarse_count, 8, 8, 8, channels)

def grid_to_places(volume):
    coarse_count = volume.shape[0]
    channels = volume.shape[-1]
    shaped = volume.reshape(coarse_count, 4, 2, 4, 2, 4, 2, channels)
    return shaped.transpose(0, 1, 3, 5, 2, 4, 6, 7).reshape(coarse_count * 64, 8, channels)

def pool_bricks(volume):
    brick_count = volume.shape[0]
    channels = volume.shape[-1]
    shaped = volume.reshape(brick_count, 2, 4, 2, 4, 2, 4, channels)
    return lax.optimization_barrier(jnp.mean(shaped, axis=(2, 4, 6))).reshape(brick_count, 8, channels)

def spread_bricks(values):
    brick_count = values.shape[0]
    channels = values.shape[-1]
    shaped = values.reshape(brick_count, 2, 1, 2, 1, 2, 1, channels)
    return jnp.broadcast_to(shaped, (brick_count, 2, 4, 2, 4, 2, 4, channels)).reshape(brick_count, 8, 8, 8, channels)

def gather_halo(face_rows, received, links):
    brick_count = links.shape[0]
    zero_row = jnp.zeros((1,) + face_rows.shape[1:], face_rows.dtype)
    every_face = jnp.concatenate([face_rows, received, zero_row], axis=0)
    opposite = jnp.array(OPPOSITE, jnp.int32)[None, :]
    local_index = links * 6 + opposite
    remote_index = brick_count * 6 + links - brick_count
    empty_index = every_face.shape[0] - 1
    indices = jnp.where(links < 0, empty_index, jnp.where(links < brick_count, local_index, remote_index))
    return every_face[indices]

def coarse_forward(incoming, places, down_weight, coarse_weight, coarse_count):
    channels = down_weight.shape[0]
    coarse_width = down_weight.shape[1]
    slot_of_place = place_slots(places, coarse_count * 64)
    pooled_places = pick_rows(incoming, slot_of_place).reshape(coarse_count * 64, 8, channels)
    flat_pooled = places_to_grid(pooled_places, coarse_count).reshape(-1, channels)
    coarse_pre = jnp.dot(flat_pooled, down_weight, preferred_element_type=jnp.float32)
    coarse_act = jax.nn.silu(coarse_pre).astype(jnp.bfloat16)
    act_grid = coarse_act.reshape(coarse_count, 8, 8, 8, coarse_width)
    empty_faces = jnp.zeros((coarse_count, 6, 8, 8, coarse_width), jnp.bfloat16)
    coarse_stack = tap_stack(padded_volume(act_grid, empty_faces), 1).reshape(-1, 7 * coarse_width)
    coarse_out = jnp.dot(coarse_stack, coarse_weight.reshape(7 * coarse_width, coarse_width), preferred_element_type=jnp.float32).astype(jnp.bfloat16)
    return (flat_pooled, coarse_pre, coarse_stack, coarse_out)

def coarse_send(coarse_out, places, coarse_count):
    coarse_width = coarse_out.shape[-1]
    coarse_rows = grid_to_places(coarse_out.reshape(coarse_count, 8, 8, 8, coarse_width)).reshape(coarse_count * 64, 8 * coarse_width)
    return pick_rows(coarse_rows, jnp.where(places < 0, coarse_count * 64, places))

def coarse_backward(incoming_grad, places, flat_pooled, coarse_pre, coarse_stack, up_weight, down_weight, coarse_weight, coarse_count):
    channels = down_weight.shape[0]
    coarse_width = down_weight.shape[1]
    slot_of_place = place_slots(places, coarse_count * 64)
    grad_places = pick_rows(incoming_grad, slot_of_place).reshape(coarse_count * 64, 8, channels)
    grad_grid = places_to_grid(grad_places, coarse_count).reshape(-1, channels)
    grad_out = jnp.dot(grad_grid, up_weight.astype(jnp.float32).T, precision=lax.Precision.HIGHEST)
    coarse_grad = lax.dot_general(coarse_stack.astype(jnp.float32), grad_out, (((0,), (0,)), ((), ())), precision=lax.Precision.HIGHEST).reshape(7, coarse_width, coarse_width)
    empty_faces = jnp.zeros((coarse_count, 6, 8, 8, coarse_width), jnp.float32)
    grad_stack = tap_stack(padded_volume(grad_out.reshape(coarse_count, 8, 8, 8, coarse_width), empty_faces), -1).reshape(-1, 7 * coarse_width)
    flipped = coarse_weight.astype(jnp.float32).transpose(0, 2, 1).reshape(7 * coarse_width, coarse_width)
    grad_act = jnp.dot(grad_stack, flipped, precision=lax.Precision.HIGHEST)
    sigmoid_term = jax.nn.sigmoid(coarse_pre)
    grad_pre = grad_act * sigmoid_term * (1.0 + coarse_pre * (1.0 - sigmoid_term))
    down_grad = jnp.dot(flat_pooled.astype(jnp.float32).T, grad_pre, precision=lax.Precision.HIGHEST)
    grad_pooled = jnp.dot(grad_pre, down_weight.astype(jnp.float32).T, precision=lax.Precision.HIGHEST)
    back_rows = grid_to_places(grad_pooled.reshape(coarse_count, 8, 8, 8, channels)).reshape(coarse_count * 64, 8 * channels)
    return (pick_rows(back_rows, jnp.where(places < 0, coarse_count * 64, places)), coarse_grad, down_grad)

def rim_gradients(grad_view, fine_weight):
    brick_count = grad_view.shape[0]
    channels = grad_view.shape[-1]
    grad_faces = face_table(grad_view)
    rim_list = []
    for direction in range(6):
        grad_layer = grad_faces[:, direction].reshape(brick_count * 64, channels)
        product = jnp.dot(grad_layer, fine_weight[direction + 1].T, preferred_element_type=jnp.float32)
        rim_list.append(product.reshape(brick_count, 8, 8 * channels))
    return jnp.stack(rim_list, axis=1).reshape(brick_count * 6, 8, 8 * channels)

def local_face_grads(rim_rows, links):
    brick_count = links.shape[0]
    opposite = jnp.array(OPPOSITE, jnp.int32)[None, :]
    is_local = (links >= 0) & (links < brick_count)
    target = jnp.where(is_local, links * 6 + opposite, brick_count * 6).reshape(-1)
    empty_table = jnp.zeros((brick_count * 6 + 1,) + rim_rows.shape[1:], jnp.float32)
    return empty_table.at[target].add(rim_rows)

def slot_pairs(links, slot_count):
    brick_count = links.shape[0]
    remote = jnp.where(links >= brick_count, links - brick_count, slot_count).reshape(-1)
    filled = jnp.full((slot_count + 1,), brick_count * 6, jnp.int32).at[remote].set(jnp.arange(brick_count * 6).astype(jnp.int32))
    return filled[:slot_count]

def transposed_conv(grad_view, fine_weight):
    brick_count = grad_view.shape[0]
    channels = grad_view.shape[-1]
    empty_faces = jnp.zeros((brick_count, 6, 8, 8, channels), grad_view.dtype)
    grad_stack = tap_stack(padded_volume(grad_view, empty_faces), -1).reshape(brick_count * 512, 7 * channels)
    flipped = fine_weight.transpose(0, 2, 1).reshape(7 * channels, channels)
    return jnp.dot(grad_stack, flipped, preferred_element_type=jnp.float32).reshape(brick_count, 8, 8, 8, channels)

def finish_backward(grad_active, before, normed, inverse, embedding, scale_term, grad_view, groups):
    brick_count = before.shape[0]
    channels = before.shape[-1]
    sigmoid_term = jax.nn.sigmoid(before)
    grad_before = grad_active * sigmoid_term * (1.0 + before * (1.0 - sigmoid_term))
    grad_scale = lax.optimization_barrier(jnp.sum(grad_before * normed, axis=(1, 2, 3)))
    grad_shift = lax.optimization_barrier(jnp.sum(grad_before, axis=(1, 2, 3)))
    time_grad = jnp.dot(embedding.T, jnp.concatenate([grad_scale, grad_shift], axis=1), precision=lax.Precision.HIGHEST)
    grad_normed = (grad_before * (1.0 + scale_term)).reshape(brick_count, 512, groups, channels // groups)
    grouped_norm = normed.reshape(brick_count, 512, groups, channels // groups)
    centred = grad_normed - lax.optimization_barrier(jnp.mean(grad_normed, axis=(1, 3), keepdims=True))
    grad_input = inverse * (centred - grouped_norm * lax.optimization_barrier(jnp.mean(grad_normed * grouped_norm, axis=(1, 3), keepdims=True)))
    grad_total = grad_view.astype(jnp.float32) + grad_input.reshape(brick_count, 8, 8, 8, channels)
    return (grad_total.astype(jnp.bfloat16).reshape(brick_count, 8, 8, 8 * channels), time_grad)

def swap_peers(buffer):
    shaped = buffer.reshape((N_GRP, N_DEV, N_DEV) + buffer.shape[2:])
    return jnp.swapaxes(shaped, 1, 2).reshape(buffer.shape)

def reference(features, cotangent, timesteps, face_links, face_sources, coarse_targets, coarse_places, time_weight, fine_weight, down_weight, coarse_weight, up_weight):
    device_total = N_GRP * N_DEV
    channels = CHANNELS
    slot_total = N_DEV * COARSE_SLOTS
    face_total = N_DEV * FACE_SLOTS
    feature_table = features.reshape(device_total, BRICK_DEV, 8, 8, 8 * channels)
    grad_table = cotangent.reshape(device_total, BRICK_DEV, 8, 8, 8 * channels)
    step_table = timesteps.reshape(device_total, BRICK_DEV)
    link_table = face_links.reshape(device_total, BRICK_DEV, 6)
    target_table = coarse_targets.reshape(device_total, BRICK_DEV)

    def send_section(inputs):
        packed, step_ids, sources, targets = inputs
        before = activate(packed, step_ids, time_weight, GROUPS)[0]
        active = jax.nn.silu(before).astype(jnp.bfloat16)
        face_rows = face_table(active).reshape(BRICK_DEV * 6, 8, 8 * channels)
        outgoing = pick_rows(face_rows, jnp.where(sources < 0, BRICK_DEV * 6, sources))
        pooled = pool_bricks(active.astype(jnp.float32)).astype(jnp.bfloat16)
        pooled_out = pick_rows(pooled.reshape(BRICK_DEV, 8 * channels), slot_bricks(targets, slot_total))
        return (outgoing, pooled_out.reshape(N_DEV, COARSE_SLOTS, 8 * channels))
    outgoing, pooled_out = lax.map(send_section, (feature_table, step_table, face_sources, target_table))
    arrived_all = swap_peers(outgoing)
    pooled_in = swap_peers(pooled_out)

    def owner_section(inputs):
        incoming, places = inputs
        coarse_out = coarse_forward(incoming.reshape(slot_total, 8 * channels), places, down_weight, coarse_weight, COARSE_DEV)[3]
        return coarse_send(coarse_out, places, COARSE_DEV)
    back_in = swap_peers(lax.map(owner_section, (pooled_in, coarse_places)))

    def fine_section(inputs):
        packed, grad_packed, step_ids, links, targets, arrived, back_rows = inputs
        before = activate(packed, step_ids, time_weight, GROUPS)[0]
        active = jax.nn.silu(before).astype(jnp.bfloat16)
        face_rows = face_table(active).reshape(BRICK_DEV * 6, 8, 8 * channels)
        halo_layers = gather_halo(face_rows, arrived.reshape(-1, 8, 8 * channels), links).reshape(BRICK_DEV, 6, 8, 8, channels)
        full_stack = tap_stack(padded_volume(active, halo_layers), 1).reshape(BRICK_DEV * 512, 7 * channels)
        conv_out = jnp.dot(full_stack, fine_weight.reshape(7 * channels, channels), preferred_element_type=jnp.float32).reshape(BRICK_DEV, 8, 8, 8, channels)
        coarse_values = back_rows.reshape(slot_total, 8, COARSE_CH)[targets]
        upward = jnp.dot(coarse_values.reshape(BRICK_DEV * 8, COARSE_CH), up_weight, preferred_element_type=jnp.float32).reshape(BRICK_DEV, 8, channels)
        result = brick_view(packed).astype(jnp.float32) + conv_out + spread_bricks(upward)
        mixed_out = result.astype(jnp.bfloat16).reshape(packed.shape)
        grad_view = brick_view(grad_packed)
        grad_up = lax.optimization_barrier(jnp.sum(grad_view.astype(jnp.float32).reshape(BRICK_DEV, 2, 4, 2, 4, 2, 4, channels), axis=(2, 4, 6))).reshape(BRICK_DEV, 8, channels)
        up_grad = jnp.dot(coarse_values.reshape(-1, COARSE_CH).astype(jnp.float32).T, grad_up.reshape(-1, channels), precision=lax.Precision.HIGHEST)
        grad_send = pick_rows(grad_up.reshape(BRICK_DEV, 8 * channels), slot_bricks(targets, slot_total)).reshape(N_DEV, COARSE_SLOTS, 8 * channels)
        fine_grad = lax.dot_general(full_stack, grad_view.reshape(-1, channels), (((0,), (0,)), ((), ())), preferred_element_type=jnp.float32).reshape(7, channels, channels)
        rim_rows = rim_gradients(grad_view, fine_weight)
        returned = pick_rows(rim_rows, slot_pairs(links, face_total)).reshape(N_DEV, FACE_SLOTS, 8, 8 * channels)
        return (mixed_out, grad_send, returned, fine_grad, up_grad)
    mixed_all, grad_send, returned, fine_grads, up_grads = lax.map(fine_section, (feature_table, grad_table, step_table, link_table, target_table, arrived_all, back_in))
    grad_arrive = swap_peers(grad_send)

    def owner_back(inputs):
        incoming, grad_in, places = inputs
        flat_pooled, coarse_pre, coarse_stack, coarse_out = coarse_forward(incoming.reshape(slot_total, 8 * channels), places, down_weight, coarse_weight, COARSE_DEV)
        return coarse_backward(grad_in.reshape(slot_total, 8 * channels), places, flat_pooled, coarse_pre, coarse_stack, up_weight, down_weight, coarse_weight, COARSE_DEV)
    grad_back, coarse_grads, down_grads = lax.map(owner_back, (pooled_in, grad_arrive, coarse_places))
    pooled_back = swap_peers(grad_back)
    faces_back = swap_peers(returned)

    def final_section(inputs):
        packed, grad_packed, step_ids, links, sources, targets, pooled_rows, face_rows_back = inputs
        before, normed, inverse, embedding, scale_term = activate(packed, step_ids, time_weight, GROUPS)
        grad_view = brick_view(grad_packed)
        grad_active = transposed_conv(grad_view, fine_weight)
        face_grad = local_face_grads(rim_gradients(grad_view, fine_weight), links)
        flat_sources = sources.reshape(-1)
        source_target = jnp.where(flat_sources < 0, BRICK_DEV * 6, flat_sources)
        face_grad = face_grad.at[source_target].add(face_rows_back.reshape(-1, 8, 8 * channels))
        pooled_grad = pooled_rows.reshape(slot_total, 8, channels)[targets]
        grad_active = add_faces(grad_active, face_grad[:BRICK_DEV * 6].reshape(BRICK_DEV, 6, 8, 8, channels))
        grad_active = grad_active + spread_bricks(pooled_grad) / 64.0
        return finish_backward(grad_active, before, normed, inverse, embedding, scale_term, grad_view, GROUPS)
    input_all, time_grads = lax.map(final_section, (feature_table, grad_table, step_table, link_table, face_sources, target_table, pooled_back, faces_back))
    mixed_out = mixed_all.reshape(features.shape)
    input_grad = input_all.reshape(features.shape)
    return (mixed_out, input_grad, lax.optimization_barrier(jnp.sum(fine_grads, axis=0)), lax.optimization_barrier(jnp.sum(down_grads, axis=0)), lax.optimization_barrier(jnp.sum(coarse_grads, axis=0)), lax.optimization_barrier(jnp.sum(up_grads, axis=0)), lax.optimization_barrier(jnp.sum(time_grads, axis=0)))
```

```python
import functools
import math

import jax
import jax.numpy as jnp
import numpy as np
from jax import lax
from jax.experimental import pallas as pl
from jax.experimental.pallas import tpu as pltpu
from jax.sharding import PartitionSpec as P

EPSILON = 1e-05
F32 = jnp.float32
BF16 = jnp.bfloat16
BRICKS = 8
ROWS = 512
LANES = 512
SLOT_ROWS = 16
PART_ROWS = 1280
UNITS = 10


def iota(shape, axis):
    return lax.broadcasted_iota(jnp.int32, shape, axis)


def dot(a, b):
    return jnp.dot(a, b, preferred_element_type=F32)


def dot_nt(a, b):
    return lax.dot_general(a, b, (((1,), (1,)), ((), ())), preferred_element_type=F32)


def dot_tn(a, b):
    return lax.dot_general(a, b, (((0,), (0,)), ((), ())), preferred_element_type=F32)


def one_hot(condition):
    return jnp.where(condition, 1.0, 0.0).astype(BF16)


def lanes_four(v):
    return jnp.concatenate([v, v, v, v], axis=1)


def fold_lanes(v):
    s = (v[:, 0:128] + v[:, 128:256]) + (v[:, 256:384] + v[:, 384:512])
    return s + pltpu.roll(s, 64, 1)


def group_mean(sums):
    s = fold_lanes(sums)
    lane = iota(s.shape, 1)
    pair = jnp.where((lane & 1) == 0, pltpu.roll(s, 127, 1), pltpu.roll(s, 1, 1))
    return lanes_four((s + pair) * (1.0 / 1024.0))


def brick_sum(v):
    return jnp.sum(v.reshape(BRICKS, 64, LANES), axis=1)


def per_brick(v):
    return v[:, None, :]


def face_index(brick, side, r):
    base = brick * 64
    xy = jnp.where(
        side < 0.5,
        base + r,
        jnp.where(
            side < 1.5,
            base + 56 + r,
            jnp.where(side < 2.5, base + 8 * r, base + 8 * r + 7),
        ),
    )
    zz = 512 + brick * 8 + r + jnp.where(side > 4.5, 64, 0)
    return jnp.where(side < 3.5, xy, zz)


def shift_rows(v, amount):
    return pltpu.roll(v, amount % v.shape[0], 0)


def z_table(v, mask, select):
    i, j = iota((128, LANES), 0), iota((128, LANES), 1)
    low = one_hot(i == (j & 63))
    high = one_hot(i - 64 == (j & 63))
    first = jnp.where(mask, dot(v[:, 0:128], low), 0.0).astype(BF16)
    last = jnp.where(mask, dot(v[:, 384:512], high), 0.0).astype(BF16)
    return dot(select, first).astype(BF16), dot(select, last).astype(BF16)


def diagonal_sum(blocks, low_shift, high_shift, count):
    even = odd = None
    for z in range(count):
        zr, zc = z + low_shift, z + high_shift
        if not (0 <= zr < count and 0 <= zc < count):
            continue
        piece = blocks[64 * zr : 64 * zr + 64, 128 * (zc // 2) : 128 * (zc // 2) + 128]
        if zc % 2 == 0:
            even = piece if even is None else even + piece
        else:
            odd = piece if odd is None else odd + piece
    return even + pltpu.roll(odd, 64, 1)


def kernel(
    n_grp,
    n_dev,
    features_ref,
    cotangent_ref,
    steps_ref,
    links_ref,
    sources_ref,
    targets_ref,
    places_ref,
    time_weight_ref,
    fine_weight_ref,
    down_weight_ref,
    coarse_weight_ref,
    up_weight_ref,
    frequency_ref,
    mixed_ref,
    input_grad_ref,
    fine_grad_ref,
    down_grad_ref,
    coarse_grad_ref,
    up_grad_ref,
    time_grad_ref,
    small_out,
    small_in,
    face_out,
    face_in,
    rim_out,
    rim_in,
    back_out,
    back_in,
    part_out,
    part_in,
    unit_out,
    unit_in,
    sum_out,
    sum_in,
    whole,
    time_out,
    time_in,
    time_mid,
    time_whole,
    hot_halo,
    hot_out,
    table,
    normed_ref,
    slope_ref,
    conv_ref,
    grad_ref,
    weight_ref,
    band_ref,
    send_sems,
    recv_sems,
):
    grp = lax.axis_index("grp")
    dev = lax.axis_index("dev")
    units = UNITS
    unit_rows = PART_ROWS // n_grp // units
    owners = min(n_grp, 8)
    owner_rows = 64 // owners

    def entry_signal():
        barrier = pltpu.get_barrier_semaphore()

        def to_dev(j, carry):
            pl.semaphore_signal(
                barrier,
                inc=1,
                device_id={"grp": grp, "dev": lax.rem(dev + j, n_dev)},
                device_id_type=pl.DeviceIdType.MESH,
            )
            return carry

        def to_grp(j, carry):
            pl.semaphore_signal(
                barrier,
                inc=1,
                device_id={"grp": lax.rem(grp + j, n_grp), "dev": dev},
                device_id_type=pl.DeviceIdType.MESH,
            )
            return carry

        lax.fori_loop(1, n_dev, to_dev, 0)
        lax.fori_loop(1, n_grp, to_grp, 0)

    def remote(src, dst, index, along, peer):
        target = {"grp": grp, "dev": peer} if along == "dev" else {"grp": peer, "dev": dev}
        return pltpu.make_async_remote_copy(
            src_ref=src,
            dst_ref=dst,
            send_sem=send_sems.at[index],
            recv_sem=recv_sems.at[index],
            device_id=target,
            device_id_type=pl.DeviceIdType.MESH,
        )

    def position(along):
        return (dev, n_dev) if along == "dev" else (grp, n_grp)

    def exchange(src, dst, index, along):
        me, count = position(along)

        def step(j, carry):
            p = lax.rem(me + j, count)
            remote(src.at[p], dst.at[me], index, along, p).start()
            return carry

        lax.fori_loop(1, count, step, 0)

    def wait_arrived(dst, blocks, index, along):
        me, count = position(along)
        if blocks > 0:
            part = dst.at[pl.ds(0, blocks)]
            remote(part, part, index, along, lax.rem(me + 1, count)).wait_recv()

    def wait_sent(src, blocks, index, along):
        me, count = position(along)
        if blocks > 0:
            part = src.at[pl.ds(0, blocks)]
            remote(part, part, index, along, lax.rem(me + 1, count)).wait_send()

    entry_signal()

    row = iota((ROWS, LANES), 0)
    lane = iota((ROWS, LANES), 1)
    y_mask = (lane >> 6) == (row & 7)

    def spread_index(shape):
        return iota(shape, 0), iota(shape, 1)

    i, j = spread_index((n_dev, n_dev * SLOT_ROWS))
    sources = sources_ref[0].astype(F32)
    chosen = jnp.where(((j >> 3) & 1) == 0, sources[:, 0:1], sources[:, 1:2])
    code = jnp.sum(jnp.where((j >> 4) == i, chosen, 0.0), axis=0, keepdims=True)
    brick = jnp.zeros_like(code)
    for m in range(1, BRICKS):
        brick = brick + jnp.where(code > 6.0 * m - 0.5, 1.0, 0.0)
    r = (iota(code.shape, 1) & 7).astype(F32)
    out_index = jnp.where(code < -0.5, -1.0, face_index(brick, code - 6.0 * brick, r))
    out_index = out_index.astype(jnp.int32)
    hot_out[...] = one_hot(iota((640, n_dev * SLOT_ROWS), 0) == out_index)

    i, j = spread_index((BRICKS, 384))
    links = links_ref[...].astype(F32)
    link = jnp.zeros((BRICKS, 384), F32)
    for k in range(6):
        link = link + jnp.where((j >> 6) == k, links[:, k : k + 1], 0.0)
    link = jnp.sum(jnp.where(((j >> 3) & 7) == i, link, 0.0), axis=0, keepdims=True)
    k_row = iota((1, 384), 1) >> 6
    side = (k_row + 1 - 2 * (k_row & 1)).astype(F32)
    r = (iota((1, 384), 1) & 7).astype(F32)
    halo_index = jnp.where(
        link < -0.5,
        -1.0,
        jnp.where(link < 7.5, face_index(link, side, r), 640 + (link - 8.0) * 8 + r),
    ).astype(jnp.int32)
    hot_halo[...] = one_hot(iota((640 + n_dev * SLOT_ROWS, 384), 0) == halo_index)

    i, j = spread_index((64, BRICKS))
    targets = targets_ref[...].astype(F32).reshape(1, BRICKS)
    target = jnp.sum(jnp.where((i >> 3) == j, targets, 0.0), axis=1, keepdims=True)
    child = (iota((64, 1), 0) & 7).astype(F32)
    target_code = (target * 16 + child).astype(jnp.int32)
    slot_lane = iota((64, n_dev * SLOT_ROWS), 1)
    hot_target = one_hot(slot_lane == target_code)
    hot_target_grad = one_hot(slot_lane == target_code + 8)

    i, j = spread_index((64, ROWS))
    pool = one_hot(
        ((i >> 3) == (j >> 6))
        & (((i >> 2) & 1) == ((j >> 5) & 1))
        & (((i >> 1) & 1) == ((j >> 2) & 1))
    )
    i, j = spread_index((64, LANES))
    half_mask = (i & 1) == (j >> 8)
    select_x = one_hot(i == (j >> 3))
    i, j = spread_index((ROWS, 64))
    unpool = one_hot(
        ((j >> 3) == (i >> 6))
        & (((j >> 2) & 1) == ((i >> 5) & 1))
        & (((j >> 1) & 1) == ((i >> 2) & 1))
    )
    repeat_y = one_hot(j == (i >> 3))
    repeat_x = one_hot(j == ((i >> 6) * 8 + (i & 7)))
    low_half = iota((64, 128), 1) < 64

    features = features_ref[...].astype(F32).reshape(ROWS, LANES)
    f3 = features.reshape(BRICKS, 64, LANES)
    centred = f3 - per_brick(group_mean(jnp.sum(f3, axis=1)))
    variance = group_mean(jnp.sum(centred * centred, axis=1))
    inverse = lax.rsqrt(variance + EPSILON)
    normed = (centred * per_brick(inverse)).reshape(ROWS, LANES)
    normed_ref[...] = normed
    i, j = spread_index((BRICKS, BRICKS))
    steps = steps_ref[...].astype(F32).reshape(1, BRICKS)
    step_column = jnp.sum(jnp.where(i == j, steps, 0.0), axis=1, keepdims=True)
    angles = step_column * frequency_ref[...]
    embedding = jnp.where(iota((BRICKS, 64), 1) < 32, jnp.cos(angles), jnp.sin(angles))
    modulate = jnp.dot(
        embedding,
        time_weight_ref[...],
        precision=lax.Precision.HIGHEST,
        preferred_element_type=F32,
    )
    swapped = pltpu.roll(modulate, 64, 1)
    low_b = iota((BRICKS, 128), 1) < 64
    scale = lanes_four(jnp.where(low_b, modulate, swapped))
    shift = lanes_four(jnp.where(low_b, swapped, modulate))
    gain = 1.0 + scale
    before = (
        normed.reshape(BRICKS, 64, LANES) * per_brick(gain) + per_brick(shift)
    ).reshape(ROWS, LANES)
    sigmoid = 1.0 / (1.0 + jnp.exp(-before))
    slope_ref[...] = sigmoid * (1.0 + before * (1.0 - sigmoid))
    active = (before * sigmoid).astype(BF16)
    table[0:512, :] = active

    grad = cotangent_ref[...].astype(F32).reshape(ROWS, LANES)
    grad_b = grad.astype(BF16)
    pooled = fold_lanes(jnp.where(half_mask, dot(pool, active), 0.0)) * (1.0 / 64.0)
    grad_up = fold_lanes(jnp.where(half_mask, dot(pool, grad_b), 0.0))
    small = jnp.where(low_half, pooled, grad_up).astype(BF16)
    small_out[...] = dot_tn(hot_target, small).astype(BF16).reshape(n_dev, SLOT_ROWS, 128)
    small_in[dev] = small_out[dev]
    barrier = pltpu.get_barrier_semaphore()
    pl.semaphore_wait(barrier, n_dev - 1 + n_grp - 1)
    exchange(small_out, small_in, 0, "dev")

    z_first, z_last = z_table(active, y_mask, select_x)
    table[512:576, :] = z_first
    table[576:640, :] = z_last
    face_out[...] = (
        dot_tn(hot_out[...], table[...]).astype(BF16).reshape(n_dev, SLOT_ROWS, LANES)
    )
    face_in[dev] = face_out[dev]
    exchange(face_out, face_in, 1, "dev")

    i, j = spread_index((64, LANES))
    wide = dot(fine_weight_ref[...].reshape(448, 64), one_hot(i == (j & 63)))
    weight_ref[...] = wide
    i, j = spread_index((256, 256))
    block = (i >> 6) == (j >> 6)
    for k in range(6):
        piece = weight_ref[64 * (k + 1) : 64 * (k + 2), 0:256]
        band_ref[256 * k : 256 * (k + 1), :] = jnp.where(
            block, jnp.concatenate([piece] * 4, axis=0), 0.0
        ).astype(BF16)
    z_step = (lane >> 6) - (row >> 6)
    middle = jnp.where(
        z_step == 0,
        jnp.concatenate([weight_ref[0:64, :]] * 8, axis=0),
        jnp.where(
            z_step == 1,
            jnp.concatenate([weight_ref[320:384, :]] * 8, axis=0),
            jnp.where(
                z_step == -1, jnp.concatenate([weight_ref[384:448, :]] * 8, axis=0), 0.0
            ),
        ),
    ).astype(BF16)

    i, j = spread_index((64, ROWS))
    g4 = grad.reshape(BRICKS, 8, 8, LANES)
    grad_z = z_table(grad_b, y_mask, select_x)
    layers = [
        g4[:, 0].reshape(64, LANES).astype(BF16),
        g4[:, 7].reshape(64, LANES).astype(BF16),
        dot(one_hot(j == i * 8), grad_b).astype(BF16),
        dot(one_hot(j == i * 8 + 7), grad_b).astype(BF16),
        grad_z[0],
        grad_z[1],
    ]
    rims = []
    for k in range(6):
        band = band_ref[256 * k : 256 * (k + 1), :]
        rims.append(
            jnp.concatenate(
                [dot_nt(layers[k][:, 0:256], band), dot_nt(layers[k][:, 256:512], band)], axis=1
            ).astype(BF16)
        )
    rim = jnp.concatenate(rims, axis=0)
    rim_out[...] = (
        dot(hot_halo[640 : 640 + n_dev * SLOT_ROWS, :], rim)
        .astype(BF16)
        .reshape(n_dev, SLOT_ROWS, LANES)
    )
    rim_in[dev] = rim_out[dev]
    exchange(rim_out, rim_in, 2, "dev")

    x_at, y_at = (row >> 3) & 7, row & 7

    def shifted(v, k, edge):
        amount, at, end = ((8, x_at, 0), (-8, x_at, 7), (1, y_at, 0), (-1, y_at, 7))[k]
        return jnp.where(at == end, edge, shift_rows(v, amount))

    total = dot_nt(grad_b, middle)
    left, right = total[:, 0:256], total[:, 256:512]
    for k in range(4):
        moved = shifted(grad, k ^ 1, 0.0).astype(BF16)
        band = band_ref[256 * k : 256 * (k + 1), :]
        left = left + dot_nt(moved[:, 0:256], band)
        right = right + dot_nt(moved[:, 256:512], band)
    total = jnp.concatenate([left, right], axis=1)
    total = total + dot(hot_halo[0:512, :], rim)
    z_rows = dot(hot_halo[512:640, :], rim)
    grad_ref[...] = total

    active_f = active.astype(F32)
    conv_ref[...] = dot(active, middle)
    grad_t = grad.T.astype(BF16)
    center = dot(grad_t, active)

    wait_arrived(small_in, n_dev - 1, 0, "dev")
    i, j = spread_index((n_dev, n_dev * SLOT_ROWS))
    places = places_ref[0].astype(F32)
    place = jnp.sum(jnp.where((j >> 4) == i, places, 0.0), axis=0, keepdims=True)
    j = iota((1, n_dev * SLOT_ROWS), 1)
    place_code = (place * 8 + (j & 7).astype(F32)).astype(jnp.int32)
    i = iota((ROWS, 1), 0)
    voxel_code = (
        ((i >> 7) * 16 + ((i >> 4) & 3) * 4 + ((i >> 1) & 3)) * 8
        + ((i >> 6) & 1) * 4
        + ((i >> 3) & 1) * 2
        + (i & 1)
    )
    first_kind = (j & 8) == 0
    hot_place = one_hot(voxel_code == jnp.where(first_kind, place_code, -1))
    hot_place_grad = one_hot(voxel_code == jnp.where(first_kind, -1, place_code))
    grid = dot(hot_place, small_in[...].reshape(n_dev * SLOT_ROWS, 128)).astype(BF16)
    down = jnp.concatenate([down_weight_ref[...], jnp.zeros((64, 128), BF16)], axis=0)
    i, j = spread_index((64, 128))
    up = dot(up_weight_ref[...], one_hot(j - 64 == i)).astype(BF16)
    coarse_pre = dot(grid, down)
    coarse_sig = 1.0 / (1.0 + jnp.exp(-coarse_pre))
    coarse_act = coarse_pre * coarse_sig
    row_c = iota((ROWS, 128), 0)
    at_c = (row_c >> 6, (row_c >> 3) & 7, row_c & 7)

    def coarse_shifted(v, k):
        amount = (64, -64, 8, -8, 1, -1)[k]
        return jnp.where(at_c[k // 2] == 7 * (k % 2), 0.0, shift_rows(v, amount))

    coarse_act_f = coarse_act.astype(BF16).astype(F32)
    stack = jnp.concatenate(
        [coarse_act_f.astype(BF16)]
        + [coarse_shifted(coarse_act_f, k).astype(BF16) for k in range(6)],
        axis=1,
    )
    coarse_out = dot(stack, coarse_weight_ref[...].reshape(896, 128)).astype(BF16)
    grad_out = dot_nt(grid, up)
    grad_out_b = grad_out.astype(BF16)
    grad_act = dot_nt(grad_out_b, coarse_weight_ref[0])
    for k in range(6):
        grad_act = grad_act + dot_nt(
            coarse_shifted(grad_out, k ^ 1).astype(BF16), coarse_weight_ref[k + 1]
        )
    grad_pre = grad_act * coarse_sig * (1.0 + coarse_pre * (1.0 - coarse_sig))
    grad_pre = grad_pre.astype(BF16)
    grad_pooled = dot_nt(grad_pre, down).astype(BF16)
    back_out[...] = (
        (dot_tn(hot_place, coarse_out) + dot_tn(hot_place_grad, grad_pooled))
        .astype(BF16)
        .reshape(n_dev, SLOT_ROWS, 128)
    )
    back_in[dev] = back_out[dev]
    exchange(back_out, back_in, 3, "dev")
    coarse_grad = dot_tn(stack, grad_out_b)
    down_grad = dot_tn(grid, grad_pre)
    up_grad = dot_tn(coarse_out, grid)
    up_rows = jnp.where(low_half, pltpu.roll(up_grad[0:64], 64, 1), up_grad[64:128])

    wait_arrived(face_in, n_dev - 1, 1, "dev")
    halo = dot_tn(hot_halo[0:640, :], table[...]) + dot_tn(
        hot_halo[640 : 640 + n_dev * SLOT_ROWS, :],
        face_in[...].reshape(n_dev * SLOT_ROWS, LANES),
    )
    halo = halo.astype(BF16)
    tap_grads = [diagonal_sum(center, 0, 0, 8)]
    conv = conv_ref[...]
    left, right = conv[:, 0:256], conv[:, 256:512]
    for k in range(4):
        repeat = repeat_x if k < 2 else repeat_y
        moved = shifted(active_f, k, dot(repeat, halo[64 * k : 64 * k + 64])).astype(BF16)
        band = band_ref[256 * k : 256 * (k + 1), :]
        left = left + dot(moved[:, 0:256], band)
        right = right + dot(moved[:, 256:512], band)
        tap_grads.append(
            diagonal_sum(dot(grad_t[0:256], moved[:, 0:256]), 0, 0, 4)
            + diagonal_sum(dot(grad_t[256:512], moved[:, 256:512]), 0, 0, 4)
        )
    layer = jnp.where(y_mask, dot(repeat_y, halo[256:320]), 0.0).astype(BF16)
    tail = jnp.concatenate(
        [jnp.where(low_half, weight_ref[320:384, 0:128], 0.0).astype(BF16)] * 8, axis=0
    )
    left = jnp.concatenate([left[:, 0:128] + dot(layer, tail), left[:, 128:256]], axis=1)
    tap_grads.append(
        diagonal_sum(center, 0, -1, 8) + fold_lanes(dot(grad_t[0:64], layer))
    )
    layer = jnp.where(y_mask, dot(repeat_y, halo[320:384]), 0.0).astype(BF16)
    tail = jnp.concatenate(
        [jnp.where(low_half, 0.0, weight_ref[384:448, 0:128]).astype(BF16)] * 8, axis=0
    )
    right = jnp.concatenate([right[:, 0:128], right[:, 128:256] + dot(layer, tail)], axis=1)
    tap_grads.append(
        diagonal_sum(center, 0, 1, 8) + fold_lanes(dot(grad_t[448:512], layer))
    )
    conv_ref[...] = jnp.concatenate([left, right], axis=1)

    fine_rows = []
    for t in range(4):
        low = tap_grads[t].T[0:64]
        high = tap_grads[t + 4].T[0:64] if t < 3 else jnp.zeros_like(low)
        fine_rows.append(jnp.concatenate([low, high], axis=1))
    part = jnp.concatenate([coarse_grad, down_grad[0:64], up_rows] + fine_rows, axis=0)
    part_out[...] = part.astype(BF16).reshape(n_grp, PART_ROWS // n_grp, 128)
    part_in[grp] = part_out[grp]
    exchange(part_out, part_in, 4, "grp")

    wait_arrived(back_in, n_dev - 1, 3, "dev")
    back = back_in[...].reshape(n_dev * SLOT_ROWS, 128)
    coarse_values = dot(hot_target, back).astype(BF16)
    i, j = spread_index((64, LANES))
    up_wide = dot(up_weight_ref[...], one_hot(i == (j & 63))).astype(BF16)
    upward = jnp.where(half_mask, dot(coarse_values, up_wide), 0.0)
    upward_high = upward.astype(BF16)
    upward_low = (upward - upward_high.astype(F32)).astype(BF16)
    upward = dot(unpool, upward_high) + dot(unpool, upward_low)
    features = features_ref[...].astype(F32).reshape(ROWS, LANES)
    mixed = features + conv_ref[...] + upward
    mixed_ref[...] = mixed.reshape(BRICKS, 8, 8, LANES).astype(BF16)

    wait_arrived(part_in, n_grp - 1, 4, "grp")
    own = part_in[0].astype(F32)
    for p in range(1, n_grp):
        own = own + part_in[p].astype(F32)
    unit_out[...] = own.reshape(units, unit_rows, 128)

    def to_owner(j, carry):
        p = lax.rem(dev + j, n_dev)

        @pl.when(p < units)
        def _():
            remote(unit_out.at[p], unit_in.at[dev], 5, "dev", p).start()

        return carry

    lax.fori_loop(1, n_dev, to_owner, 0)

    back_grad = dot(hot_target_grad, back).astype(BF16)
    i, j = spread_index((128, LANES))
    back_wide = jnp.where(half_mask, dot(back_grad, one_hot(i == (j & 63))), 0.0)
    total = grad_ref[...] + dot(unpool, (back_wide * (1.0 / 64.0)).astype(BF16))
    wait_arrived(rim_in, n_dev - 1, 2, "dev")
    rim_back = rim_in[...].reshape(n_dev * SLOT_ROWS, LANES)
    total = total + dot(hot_out[0:512, :], rim_back)
    z_rows = (z_rows + dot(hot_out[512:640, :], rim_back)).astype(BF16)
    low_rows = lane[:, 0:128] < 64
    first = fold_lanes(jnp.where(y_mask, dot(repeat_y, z_rows[0:64]), 0.0))
    last = fold_lanes(jnp.where(y_mask, dot(repeat_y, z_rows[64:128]), 0.0))
    total = jnp.concatenate(
        [
            total[:, 0:128] + jnp.where(low_rows, first, 0.0),
            total[:, 128:384],
            total[:, 384:512] + jnp.where(low_rows, 0.0, last),
        ],
        axis=1,
    )
    normed = normed_ref[...]
    grad_before = total * slope_ref[...]
    grad_scale = fold_lanes(brick_sum(grad_before * normed))
    grad_shift = fold_lanes(brick_sum(grad_before))
    time_grad = lax.dot_general(
        embedding,
        jnp.where(low_b, grad_scale, grad_shift),
        (((0,), (0,)), ((), ())),
        precision=lax.Precision.HIGHEST,
        preferred_element_type=F32,
    )
    time_out[...] = time_grad.reshape(owners, owner_rows, 128)

    def to_time_owner(j, carry):
        p = lax.rem(grp + j, n_grp)

        @pl.when(p < owners)
        def _():
            remote(time_out.at[p], time_in.at[grp], 8, "grp", p).start()

        return carry

    lax.fori_loop(1, n_grp, to_time_owner, 0)

    @pl.when(dev < units)
    def _():
        unit_in[dev] = unit_out[dev]
        wait_arrived(unit_in, n_dev - 1, 5, "dev")
        mine = unit_in[0]
        for p in range(1, n_dev):
            mine = mine + unit_in[p]
        sum_out[...] = mine
        sum_in[dev] = mine

        def to_all(j, carry):
            p = lax.rem(dev + j, n_dev)
            remote(sum_out, sum_in.at[dev], 6, "dev", p).start()
            return carry

        lax.fori_loop(1, n_dev, to_all, 0)

    g3 = grad_before.reshape(BRICKS, 64, LANES) * per_brick(gain)
    n3 = normed.reshape(BRICKS, 64, LANES)
    mean_g = group_mean(jnp.sum(g3, axis=1))
    mean_gn = group_mean(jnp.sum(g3 * n3, axis=1))
    result = per_brick(inverse) * (g3 - per_brick(mean_g) - n3 * per_brick(mean_gn))
    grad = cotangent_ref[...].astype(F32).reshape(ROWS, LANES)
    result = grad + result.reshape(ROWS, LANES)
    input_grad_ref[...] = result.reshape(BRICKS, 8, 8, LANES).astype(BF16)

    @pl.when(grp < owners)
    def _():
        time_in[grp] = time_out[grp]
        wait_arrived(time_in, n_grp - 1, 8, "grp")
        mine = time_in[0]
        for p in range(1, n_grp):
            mine = mine + time_in[p]
        time_mid[dev] = mine

        def to_all(j, carry):
            p = lax.rem(dev + j, n_dev)
            remote(time_mid.at[dev], time_mid.at[dev], 9, "dev", p).start()
            return carry

        lax.fori_loop(1, n_dev, to_all, 0)

    @pl.when(dev < units)
    def _():
        wait_arrived(sum_in, units - 1, 6, "dev")

    @pl.when(dev >= units)
    def _():
        wait_arrived(sum_in, units, 6, "dev")

    whole[grp] = sum_in[...].reshape(units * unit_rows, 128).astype(BF16)

    def to_all(j, carry):
        p = lax.rem(grp + j, n_grp)
        remote(whole.at[grp], whole.at[grp], 7, "grp", p).start()
        return carry

    lax.fori_loop(1, n_grp, to_all, 0)

    @pl.when(grp < owners)
    def _():
        wait_arrived(time_mid, n_dev - 1, 9, "dev")
        mine = time_mid[0]
        for p in range(1, n_dev):
            mine = mine + time_mid[p]
        time_whole[grp] = mine

        def to_all(j, carry):
            p = lax.rem(grp + j, n_grp)
            remote(time_whole.at[grp], time_whole.at[grp], 10, "grp", p).start()
            return carry

        lax.fori_loop(1, n_grp, to_all, 0)

    wait_arrived(whole, n_grp - 1, 7, "grp")
    sums = whole[...].reshape(PART_ROWS, 128).astype(F32)
    coarse_grad_ref[...] = sums[0:896].reshape(7, 128, 128)
    down_grad_ref[...] = sums[896:960]
    up_grad_ref[0:64, :] = sums[960:1024, 0:64]
    up_grad_ref[64:128, :] = pltpu.roll(sums[960:1024], 64, 1)[:, 0:64]
    for t in range(4):
        piece = sums[1024 + 64 * t : 1088 + 64 * t]
        fine_grad_ref[t] = piece[:, 0:64]
        if t < 3:
            fine_grad_ref[t + 4] = pltpu.roll(piece, 64, 1)[:, 0:64]

    @pl.when(grp < owners)
    def _():
        wait_arrived(time_whole, owners - 1, 10, "grp")

    @pl.when(grp >= owners)
    def _():
        wait_arrived(time_whole, owners, 10, "grp")

    time_grad_ref[...] = time_whole[...].reshape(64, 128)

    wait_sent(small_out, n_dev - 1, 0, "dev")
    wait_sent(face_out, n_dev - 1, 1, "dev")
    wait_sent(rim_out, n_dev - 1, 2, "dev")
    wait_sent(back_out, n_dev - 1, 3, "dev")
    wait_sent(part_out, n_grp - 1, 4, "grp")
    wait_sent(whole, n_grp - 1, 7, "grp")

    @pl.when(dev < units)
    def _():
        wait_sent(unit_out, units - 1, 5, "dev")
        wait_sent(unit_in, n_dev - 1, 6, "dev")

    @pl.when(dev >= units)
    def _():
        wait_sent(unit_out, units, 5, "dev")

    @pl.when(grp < owners)
    def _():
        wait_sent(time_out, owners - 1, 8, "grp")
        wait_sent(time_mid, n_dev - 1, 9, "dev")
        wait_sent(time_in, n_grp - 1, 10, "grp")

    @pl.when(grp >= owners)
    def _():
        wait_sent(time_out, owners, 8, "grp")


def body(n_grp, n_dev, *args):
    half = 32
    frequency = np.exp(-math.log(10000.0) * np.arange(half) / half).astype(np.float32)
    frequency = jnp.asarray(np.concatenate([frequency, frequency])[None, :])
    chunk = PART_ROWS // n_grp
    units, unit_rows = UNITS, chunk // UNITS
    owners = min(n_grp, 8)
    owner_rows = 64 // owners
    vmem = pl.BlockSpec(memory_space=pltpu.VMEM)
    packed = jax.ShapeDtypeStruct((BRICKS, 8, 8, LANES), BF16)
    slots = (n_dev, SLOT_ROWS)
    return pl.pallas_call(
        functools.partial(kernel, n_grp, n_dev),
        out_shape=(
            packed,
            packed,
            jax.ShapeDtypeStruct((7, 64, 64), F32),
            jax.ShapeDtypeStruct((64, 128), F32),
            jax.ShapeDtypeStruct((7, 128, 128), F32),
            jax.ShapeDtypeStruct((128, 64), F32),
            jax.ShapeDtypeStruct((64, 128), F32),
        ),
        in_specs=[vmem] * 13,
        out_specs=(vmem,) * 7,
        scratch_shapes=[
            pltpu.VMEM(slots + (128,), BF16),
            pltpu.VMEM(slots + (128,), BF16),
            pltpu.VMEM(slots + (LANES,), BF16),
            pltpu.VMEM(slots + (LANES,), BF16),
            pltpu.VMEM(slots + (LANES,), BF16),
            pltpu.VMEM(slots + (LANES,), BF16),
            pltpu.VMEM(slots + (128,), BF16),
            pltpu.VMEM(slots + (128,), BF16),
            pltpu.VMEM((n_grp, chunk, 128), BF16),
            pltpu.VMEM((n_grp, chunk, 128), BF16),
            pltpu.VMEM((units, unit_rows, 128), F32),
            pltpu.VMEM((n_dev, unit_rows, 128), F32),
            pltpu.VMEM((unit_rows, 128), F32),
            pltpu.VMEM((units, unit_rows, 128), F32),
            pltpu.VMEM((n_grp, chunk, 128), BF16),
            pltpu.VMEM((owners, owner_rows, 128), F32),
            pltpu.VMEM((n_grp, owner_rows, 128), F32),
            pltpu.VMEM((n_dev, owner_rows, 128), F32),
            pltpu.VMEM((owners, owner_rows, 128), F32),
            pltpu.VMEM((640 + n_dev * SLOT_ROWS, 384), BF16),
            pltpu.VMEM((640, n_dev * SLOT_ROWS), BF16),
            pltpu.VMEM((640, LANES), BF16),
            pltpu.VMEM((ROWS, LANES), F32),
            pltpu.VMEM((ROWS, LANES), F32),
            pltpu.VMEM((ROWS, LANES), F32),
            pltpu.VMEM((ROWS, LANES), F32),
            pltpu.VMEM((448, LANES), F32),
            pltpu.VMEM((1536, 256), BF16),
            pltpu.SemaphoreType.DMA((11,)),
            pltpu.SemaphoreType.DMA((11,)),
        ],
        compiler_params=pltpu.CompilerParams(
            collective_id=0, has_side_effects=True, vmem_limit_bytes=56 * 1024 * 1024
        ),
    )(*args, frequency)


def solution(mesh):
    split = ("grp", "dev")
    in_specs = (
        P(split, None, None, None),
        P(split, None, None, None),
        P(split),
        P(split, None),
        P(split, None, None),
        P(split),
        P(split, None, None),
        P(),
        P(),
        P(),
        P(),
        P(),
    )
    out_specs = (
        P(split, None, None, None),
        P(split, None, None, None),
        P(),
        P(),
        P(),
        P(),
        P(),
    )
    return jax.shard_map(
        functools.partial(body, mesh.shape["grp"], mesh.shape["dev"]),
        mesh=mesh,
        in_specs=in_specs,
        out_specs=out_specs,
        check_vma=False,
    )
```

```python
import functools
import math

import jax
import jax.numpy as jnp
import numpy as np
from jax import lax
from jax.experimental import pallas as pl
from jax.experimental.pallas import tpu as pltpu
from jax.sharding import PartitionSpec as P

EPSILON = 1e-05
F32 = jnp.float32
BF16 = jnp.bfloat16
BRICKS = 8
ROWS = 512
LANES = 512
SLOT_ROWS = 16
COARSE_ROWS = 1024
FINE_ROWS = 256


def iota(shape, axis):
    return lax.broadcasted_iota(jnp.int32, shape, axis)


def dot(a, b):
    return jnp.dot(a, b, preferred_element_type=F32)


def dot_nt(a, b):
    return lax.dot_general(a, b, (((1,), (1,)), ((), ())), preferred_element_type=F32)


def dot_tn(a, b):
    return lax.dot_general(a, b, (((0,), (0,)), ((), ())), preferred_element_type=F32)


def exact_dot(a, b):
    return jnp.dot(a, b, precision=lax.Precision.HIGHEST, preferred_element_type=F32)


def one_hot(condition):
    return jnp.where(condition, 1.0, 0.0).astype(BF16)


def lanes_four(v):
    return jnp.concatenate([v, v, v, v], axis=1)


def fold_lanes(v):
    s = (v[:, 0:128] + v[:, 128:256]) + (v[:, 256:384] + v[:, 384:512])
    return s + pltpu.roll(s, 64, 1)


def group_mean(sums):
    s = fold_lanes(sums)
    lane = iota(s.shape, 1)
    pair = jnp.where((lane & 1) == 0, pltpu.roll(s, 127, 1), pltpu.roll(s, 1, 1))
    return lanes_four((s + pair) * (1.0 / 1024.0))


def brick_sum(v):
    return jnp.sum(v.reshape(BRICKS, 64, LANES), axis=1)


def per_brick(v):
    return v[:, None, :]


def face_index(brick, side, r):
    base = brick * 64
    xy = jnp.where(
        side < 0.5,
        base + r,
        jnp.where(
            side < 1.5,
            base + 56 + r,
            jnp.where(side < 2.5, base + 8 * r, base + 8 * r + 7),
        ),
    )
    zz = 512 + brick * 8 + r + jnp.where(side > 4.5, 64, 0)
    return jnp.where(side < 3.5, xy, zz)


def shift_rows(v, amount):
    return pltpu.roll(v, amount % v.shape[0], 0)


def z_table(v, mask, select):
    i, j = iota((128, LANES), 0), iota((128, LANES), 1)
    low = one_hot(i == (j & 63))
    high = one_hot(i - 64 == (j & 63))
    first = jnp.where(mask, dot(v[:, 0:128], low), 0.0).astype(BF16)
    last = jnp.where(mask, dot(v[:, 384:512], high), 0.0).astype(BF16)
    return dot(select, first).astype(BF16), dot(select, last).astype(BF16)


def diagonal_sum(blocks, low_shift, high_shift, count):
    even = odd = None
    for z in range(count):
        zr, zc = z + low_shift, z + high_shift
        if not (0 <= zr < count and 0 <= zc < count):
            continue
        piece = blocks[64 * zr : 64 * zr + 64, 128 * (zc // 2) : 128 * (zc // 2) + 128]
        if zc % 2 == 0:
            even = piece if even is None else even + piece
        else:
            odd = piece if odd is None else odd + piece
    return even + pltpu.roll(odd, 64, 1)


def kernel(
    n_grp,
    n_dev,
    features_ref,
    cotangent_ref,
    steps_ref,
    links_ref,
    sources_ref,
    targets_ref,
    places_ref,
    time_weight_ref,
    fine_weight_ref,
    down_weight_ref,
    coarse_weight_ref,
    up_weight_ref,
    frequency_ref,
    mixed_ref,
    input_grad_ref,
    coarse_sum_ref,
    fine_sum_ref,
    time_sum_ref,
    small_out,
    small_in,
    face_out,
    face_in,
    rim_out,
    rim_in,
    back_out,
    back_in,
    pair_out,
    pair_in,
    coarse_out_ref,
    coarse_in,
    coarse_mid,
    coarse_all,
    fine_out,
    fine_in,
    fine_mid,
    fine_all,
    brick_all,
    time_all,
    mixed_held,
    input_grad_held,
    hot_halo,
    hot_out,
    table,
    normed_ref,
    slope_ref,
    conv_ref,
    grad_ref,
    weight_ref,
    band_ref,
    send_sems,
    recv_sems,
    copy_sems,
):
    grp = lax.axis_index("grp")
    dev = lax.axis_index("dev")
    chip = dev // 2
    core = dev % 2
    n_chip = n_dev // 2

    def entry_signal():
        barrier = pltpu.get_barrier_semaphore()

        def to_dev(j, carry):
            pl.semaphore_signal(
                barrier,
                inc=1,
                device_id={"grp": grp, "dev": lax.rem(dev + j, n_dev)},
                device_id_type=pl.DeviceIdType.MESH,
            )
            return carry

        def to_grp(j, carry):
            pl.semaphore_signal(
                barrier,
                inc=1,
                device_id={"grp": lax.rem(grp + j, n_grp), "dev": dev},
                device_id_type=pl.DeviceIdType.MESH,
            )
            return carry

        lax.fori_loop(1, n_dev, to_dev, 0)
        lax.fori_loop(1, n_grp, to_grp, 0)

    def remote(src, dst, index, along, peer):
        target = {"grp": grp, "dev": peer} if along == "dev" else {"grp": peer, "dev": dev}
        return pltpu.make_async_remote_copy(
            src_ref=src,
            dst_ref=dst,
            send_sem=send_sems.at[index],
            recv_sem=recv_sems.at[index],
            device_id=target,
            device_id_type=pl.DeviceIdType.MESH,
        )

    def ring(along):
        if along == "dev":
            return dev, n_dev, "dev", lambda p: p
        if along == "chip":
            return chip, n_chip, "dev", lambda p: 2 * p + core
        if along == "core":
            return core, 2, "dev", lambda p: 2 * chip + p
        return grp, n_grp, "grp", lambda p: p

    def exchange(src, dst, index, along):
        me, count, axis, device = ring(along)

        def step(j, carry):
            p = lax.rem(me + j, count)
            remote(src(p), dst, index, axis, device(p)).start()
            return carry

        lax.fori_loop(1, count, step, 0)

    def wait_arrived(part, index, along):
        me, count, axis, device = ring(along)
        if count > 1:
            remote(part, part, index, axis, device(lax.rem(me + 1, count))).wait_recv()

    def wait_sent(part, index, along):
        me, count, axis, device = ring(along)
        if count > 1:
            remote(part, part, index, axis, device(lax.rem(me + 1, count))).wait_send()

    def others(ref, count):
        return ref.at[pl.ds(0, max(count - 1, 1))]

    entry_signal()

    row = iota((ROWS, LANES), 0)
    lane = iota((ROWS, LANES), 1)
    y_mask = (lane >> 6) == (row & 7)

    def spread_index(shape):
        return iota(shape, 0), iota(shape, 1)

    i, j = spread_index((n_dev, n_dev * SLOT_ROWS))
    by_slot = (j >> 4) == i
    spread_slot = jnp.where(by_slot, 1.0, 0.0)
    sources = exact_dot(sources_ref[0].astype(F32), spread_slot)
    j = iota((1, n_dev * SLOT_ROWS), 1)
    code = jnp.where(((j >> 3) & 1) == 0, sources[0:1], sources[1:2])
    brick = jnp.zeros_like(code)
    for m in range(1, BRICKS):
        brick = brick + jnp.where(code > 6.0 * m - 0.5, 1.0, 0.0)
    r = (iota(code.shape, 1) & 7).astype(F32)
    out_index = jnp.where(code < -0.5, -1.0, face_index(brick, code - 6.0 * brick, r))
    out_index = out_index.astype(jnp.int32)
    hot_out[...] = one_hot(iota((640, n_dev * SLOT_ROWS), 0) == out_index)

    i, j = spread_index((BRICKS, 384))
    links = links_ref[...].astype(F32)
    link = jnp.zeros((BRICKS, 384), F32)
    for k in range(6):
        link = link + jnp.where((j >> 6) == k, links[:, k : k + 1], 0.0)
    link = jnp.sum(jnp.where(((j >> 3) & 7) == i, link, 0.0), axis=0, keepdims=True)
    k_row = iota((1, 384), 1) >> 6
    side = (k_row + 1 - 2 * (k_row & 1)).astype(F32)
    r = (iota((1, 384), 1) & 7).astype(F32)
    halo_index = jnp.where(
        link < -0.5,
        -1.0,
        jnp.where(link < 7.5, face_index(link, side, r), 640 + (link - 8.0) * 8 + r),
    ).astype(jnp.int32)
    hot_halo[...] = one_hot(iota((640 + n_dev * SLOT_ROWS, 384), 0) == halo_index)

    i, j = spread_index((64, BRICKS))
    targets = targets_ref[...].astype(F32).reshape(1, BRICKS)
    target = jnp.sum(jnp.where((i >> 3) == j, targets, 0.0), axis=1, keepdims=True)
    child = (iota((64, 1), 0) & 7).astype(F32)
    target_code = (target * 16 + child).astype(jnp.int32)
    slot_lane = iota((64, n_dev * SLOT_ROWS), 1)
    hot_target = one_hot(slot_lane == target_code)
    hot_target_grad = one_hot(slot_lane == target_code + 8)

    i, j = spread_index((64, ROWS))
    pool = one_hot(
        ((i >> 3) == (j >> 6))
        & (((i >> 2) & 1) == ((j >> 5) & 1))
        & (((i >> 1) & 1) == ((j >> 2) & 1))
    )
    i, j = spread_index((64, LANES))
    half_mask = (i & 1) == (j >> 8)
    select_x = one_hot(i == (j >> 3))
    i, j = spread_index((ROWS, 64))
    unpool = one_hot(
        ((j >> 3) == (i >> 6))
        & (((j >> 2) & 1) == ((i >> 5) & 1))
        & (((j >> 1) & 1) == ((i >> 2) & 1))
    )
    repeat_y = one_hot(j == (i >> 3))
    repeat_x = one_hot(j == ((i >> 6) * 8 + (i & 7)))
    low_half = iota((64, 128), 1) < 64

    features = features_ref[...].astype(F32).reshape(ROWS, LANES)
    f3 = features.reshape(BRICKS, 64, LANES)
    centred = f3 - per_brick(group_mean(jnp.sum(f3, axis=1)))
    variance = group_mean(jnp.sum(centred * centred, axis=1))
    inverse = lax.rsqrt(variance + EPSILON)
    normed = (centred * per_brick(inverse)).reshape(ROWS, LANES)
    normed_ref[...] = normed
    i, j = spread_index((BRICKS, BRICKS))
    steps = steps_ref[...].astype(F32).reshape(1, BRICKS)
    step_column = jnp.sum(jnp.where(i == j, steps, 0.0), axis=1, keepdims=True)
    angles = step_column * frequency_ref[...]
    embedding = jnp.where(iota((BRICKS, 64), 1) < 32, jnp.cos(angles), jnp.sin(angles))
    modulate = exact_dot(embedding, time_weight_ref[...])
    swapped = pltpu.roll(modulate, 64, 1)
    low_b = iota((BRICKS, 128), 1) < 64
    scale = lanes_four(jnp.where(low_b, modulate, swapped))
    shift = lanes_four(jnp.where(low_b, swapped, modulate))
    gain = 1.0 + scale
    before = (
        normed.reshape(BRICKS, 64, LANES) * per_brick(gain) + per_brick(shift)
    ).reshape(ROWS, LANES)
    sigmoid = 1.0 / (1.0 + jnp.exp(-before))
    slope_ref[...] = sigmoid * (1.0 + before * (1.0 - sigmoid))
    active = (before * sigmoid).astype(BF16)
    table[0:512, :] = active

    grad = cotangent_ref[...].astype(F32).reshape(ROWS, LANES)
    grad_b = grad.astype(BF16)
    pooled = fold_lanes(jnp.where(half_mask, dot(pool, active), 0.0)) * (1.0 / 64.0)
    grad_up = fold_lanes(jnp.where(half_mask, dot(pool, grad_b), 0.0))
    small = jnp.where(low_half, pooled, grad_up).astype(BF16)
    i, j = spread_index((BRICKS, 128))
    wide_embedding = jnp.concatenate([embedding, embedding], axis=1)
    rounded = wide_embedding.astype(BF16).astype(F32)
    rounded = jnp.where(j < 64, rounded, wide_embedding - rounded)
    rounded = jnp.concatenate([jnp.zeros((8, 128), F32), rounded] * n_dev, axis=0)
    small = dot_tn(hot_target, small) + rounded
    small_out[...] = small.astype(BF16).reshape(n_dev, SLOT_ROWS, 128)
    small_in[dev] = small_out[dev]
    barrier = pltpu.get_barrier_semaphore()
    pl.semaphore_wait(barrier, n_dev - 1 + n_grp - 1)
    exchange(lambda p: small_out.at[p], small_in.at[dev], 0, "dev")

    z_first, z_last = z_table(active, y_mask, select_x)
    table[512:576, :] = z_first
    table[576:640, :] = z_last
    face_out[...] = (
        dot_tn(hot_out[...], table[...]).astype(BF16).reshape(n_dev, SLOT_ROWS, LANES)
    )
    face_in[dev] = face_out[dev]
    exchange(lambda p: face_out.at[p], face_in.at[dev], 1, "dev")

    i, j = spread_index((64, LANES))
    wide = dot(fine_weight_ref[...].reshape(448, 64), one_hot(i == (j & 63)))
    weight_ref[...] = wide
    i, j = spread_index((256, 256))
    block = (i >> 6) == (j >> 6)
    for k in range(6):
        piece = weight_ref[64 * (k + 1) : 64 * (k + 2), 0:256]
        band_ref[256 * k : 256 * (k + 1), :] = jnp.where(
            block, jnp.concatenate([piece] * 4, axis=0), 0.0
        ).astype(BF16)
    z_step = (lane >> 6) - (row >> 6)
    middle = jnp.where(
        z_step == 0,
        jnp.concatenate([weight_ref[0:64, :]] * 8, axis=0),
        jnp.where(
            z_step == 1,
            jnp.concatenate([weight_ref[320:384, :]] * 8, axis=0),
            jnp.where(
                z_step == -1, jnp.concatenate([weight_ref[384:448, :]] * 8, axis=0), 0.0
            ),
        ),
    ).astype(BF16)

    i, j = spread_index((64, ROWS))
    g4 = grad.reshape(BRICKS, 8, 8, LANES)
    grad_z = z_table(grad_b, y_mask, select_x)
    layers = [
        g4[:, 0].reshape(64, LANES).astype(BF16),
        g4[:, 7].reshape(64, LANES).astype(BF16),
        dot(one_hot(j == i * 8), grad_b).astype(BF16),
        dot(one_hot(j == i * 8 + 7), grad_b).astype(BF16),
        grad_z[0],
        grad_z[1],
    ]
    rims = []
    for k in range(6):
        band = band_ref[256 * k : 256 * (k + 1), :]
        rims.append(
            jnp.concatenate(
                [dot_nt(layers[k][:, 0:256], band), dot_nt(layers[k][:, 256:512], band)], axis=1
            ).astype(BF16)
        )
    rim = jnp.concatenate(rims, axis=0)
    rim_out[...] = (
        dot(hot_halo[640 : 640 + n_dev * SLOT_ROWS, :], rim)
        .astype(BF16)
        .reshape(n_dev, SLOT_ROWS, LANES)
    )
    rim_in[dev] = rim_out[dev]
    exchange(lambda p: rim_out.at[p], rim_in.at[dev], 2, "dev")

    x_at, y_at = (row >> 3) & 7, row & 7

    def shifted(v, k, edge):
        amount, at, end = ((8, x_at, 0), (-8, x_at, 7), (1, y_at, 0), (-1, y_at, 7))[k]
        return jnp.where(at == end, edge, shift_rows(v, amount))

    total = dot_nt(grad_b, middle)
    left, right = total[:, 0:256], total[:, 256:512]
    for k in range(4):
        moved = shifted(grad, k ^ 1, 0.0).astype(BF16)
        band = band_ref[256 * k : 256 * (k + 1), :]
        left = left + dot_nt(moved[:, 0:256], band)
        right = right + dot_nt(moved[:, 256:512], band)
    total = jnp.concatenate([left, right], axis=1)
    total = total + dot(hot_halo[0:512, :], rim)
    z_rows = dot(hot_halo[512:640, :], rim)
    grad_ref[...] = total

    active_f = active.astype(F32)
    conv_ref[...] = dot(active, middle)
    grad_t = grad.T.astype(BF16)
    center = dot(grad_t, active)

    wait_arrived(others(small_in, n_dev), 0, "dev")
    place = exact_dot(places_ref[...].astype(F32), spread_slot)
    j = iota((1, n_dev * SLOT_ROWS), 1)
    place_code = (place * 8 + (j & 7).astype(F32)).astype(jnp.int32)
    i = iota((ROWS, 1), 0)
    voxel_code = (
        ((i >> 7) * 16 + ((i >> 4) & 3) * 4 + ((i >> 1) & 3)) * 8
        + ((i >> 6) & 1) * 4
        + ((i >> 3) & 1) * 2
        + (i & 1)
    )
    first_kind = (j & 8) == 0
    hot_place = one_hot(voxel_code == jnp.where(first_kind, place_code, -1))
    hot_place_grad = one_hot(voxel_code == jnp.where(first_kind, -1, place_code))
    grid = dot(hot_place, small_in[...].reshape(n_dev * SLOT_ROWS, 128)).astype(BF16)
    down = jnp.concatenate([down_weight_ref[...], jnp.zeros((64, 128), BF16)], axis=0)
    up = jnp.concatenate([jnp.zeros((64, 128), BF16), up_weight_ref[...]], axis=0)
    coarse_pre = dot(grid, down)
    coarse_sig = 1.0 / (1.0 + jnp.exp(-coarse_pre))
    coarse_act = coarse_pre * coarse_sig
    row_c = iota((ROWS, 128), 0)
    at_c = (row_c >> 6, (row_c >> 3) & 7, row_c & 7)

    def coarse_shifted(v, k):
        amount = (64, -64, 8, -8, 1, -1)[k]
        return jnp.where(at_c[k // 2] == 7 * (k % 2), 0.0, shift_rows(v, amount))

    coarse_act_f = coarse_act.astype(BF16).astype(F32)
    stack = jnp.concatenate(
        [coarse_act_f.astype(BF16)]
        + [coarse_shifted(coarse_act_f, k).astype(BF16) for k in range(6)],
        axis=1,
    )
    coarse_out = dot(stack, coarse_weight_ref[...].reshape(896, 128)).astype(BF16)
    grad_out = dot(grid, up)
    grad_out_b = grad_out.astype(BF16)
    grad_act = dot_nt(grad_out_b, coarse_weight_ref[0])
    for k in range(6):
        grad_act = grad_act + dot_nt(
            coarse_shifted(grad_out, k ^ 1).astype(BF16), coarse_weight_ref[k + 1]
        )
    grad_pre = grad_act * coarse_sig * (1.0 + coarse_pre * (1.0 - coarse_sig))
    grad_pre = grad_pre.astype(BF16)
    grad_pooled = dot_nt(grad_pre, down).astype(BF16)
    back_out[...] = (
        (dot_tn(hot_place, coarse_out) + dot_tn(hot_place_grad, grad_pooled))
        .astype(BF16)
        .reshape(n_dev, SLOT_ROWS, 128)
    )
    back_in[dev] = back_out[dev]
    exchange(lambda p: back_out.at[p], back_in.at[dev], 3, "dev")
    coarse_grad = dot_tn(stack, grad_out_b)
    down_grad = dot_tn(grid, grad_pre)
    up_grad = dot_tn(grid, coarse_out)

    part = jnp.concatenate([coarse_grad, down_grad[0:64], up_grad[64:128]], axis=0)
    pair_out[...] = part.astype(BF16).reshape(2, COARSE_ROWS // 2, 128)
    exchange(lambda p: pair_out.at[p], pair_in, 4, "core")

    wait_arrived(others(face_in, n_dev), 1, "dev")
    halo = dot_tn(hot_halo[0:640, :], table[...]) + dot_tn(
        hot_halo[640 : 640 + n_dev * SLOT_ROWS, :],
        face_in[...].reshape(n_dev * SLOT_ROWS, LANES),
    )
    halo = halo.astype(BF16)
    tap_grads = [diagonal_sum(center, 0, 0, 8)]
    taps = []
    for k in range(4):
        repeat = repeat_x if k < 2 else repeat_y
        moved = shifted(active_f, k, dot(repeat, halo[64 * k : 64 * k + 64])).astype(BF16)
        taps.append(moved)
        tap_grads.append(
            diagonal_sum(dot(grad_t[0:256], moved[:, 0:256]), 0, 0, 4)
            + diagonal_sum(dot(grad_t[256:512], moved[:, 256:512]), 0, 0, 4)
        )
    low_z = jnp.where(y_mask, dot(repeat_y, halo[256:320]), 0.0).astype(BF16)
    high_z = jnp.where(y_mask, dot(repeat_y, halo[320:384]), 0.0).astype(BF16)
    tap_grads.append(diagonal_sum(center, 0, -1, 8) + fold_lanes(dot(grad_t[0:64], low_z)))
    tap_grads.append(diagonal_sum(center, 0, 1, 8) + fold_lanes(dot(grad_t[448:512], high_z)))
    fine_rows = []
    for t in range(4):
        low = tap_grads[t].T[0:64]
        high = tap_grads[t + 4].T[0:64] if t < 3 else jnp.zeros_like(low)
        fine_rows.append(jnp.concatenate([low, high], axis=1))
    part = jnp.concatenate(fine_rows, axis=0)
    fine_out[...] = part.astype(BF16).reshape(n_grp, FINE_ROWS // n_grp, 128)
    fine_in[grp] = fine_out[grp]
    exchange(lambda p: fine_out.at[p], fine_in.at[grp], 9, "grp")

    wait_arrived(pair_in, 4, "core")
    part = pair_out[core].astype(F32) + pair_in[...].astype(F32)
    coarse_out_ref[...] = part.astype(BF16).reshape(n_grp, COARSE_ROWS // 2 // n_grp, 128)
    coarse_in[grp] = coarse_out_ref[grp]
    exchange(lambda p: coarse_out_ref.at[p], coarse_in.at[grp], 5, "grp")

    conv = conv_ref[...]
    left, right = conv[:, 0:256], conv[:, 256:512]
    for k in range(4):
        band = band_ref[256 * k : 256 * (k + 1), :]
        left = left + dot(taps[k][:, 0:256], band)
        right = right + dot(taps[k][:, 256:512], band)
    end = jnp.where(low_half, weight_ref[320:384, 0:128], 0.0).astype(BF16)
    first = dot(low_z, jnp.concatenate([end] * 8, axis=0))
    end = jnp.where(low_half, 0.0, weight_ref[384:448, 0:128]).astype(BF16)
    last = dot(high_z, jnp.concatenate([end] * 8, axis=0))
    conv_ref[...] = jnp.concatenate(
        [left[:, 0:128] + first, left[:, 128:256], right[:, 0:128], right[:, 128:256] + last],
        axis=1,
    )

    wait_arrived(others(coarse_in, n_grp), 5, "grp")
    part = coarse_in[0].astype(F32)
    for p in range(1, n_grp):
        part = part + coarse_in[p].astype(F32)
    coarse_mid[chip] = part.astype(BF16)
    exchange(lambda p: coarse_mid.at[chip], coarse_mid.at[chip], 6, "chip")

    wait_arrived(others(back_in, n_dev), 3, "dev")
    back = back_in[...].reshape(n_dev * SLOT_ROWS, 128)
    coarse_values = dot(hot_target, back).astype(BF16)
    i, j = spread_index((64, LANES))
    up_wide = dot_tn(up_weight_ref[...], one_hot(i == (j & 63))).astype(BF16)
    upward = jnp.where(half_mask, dot(coarse_values, up_wide), 0.0)
    upward_high = upward.astype(BF16)
    upward_low = (upward - upward_high.astype(F32)).astype(BF16)
    upward = dot(unpool, upward_high) + dot(unpool, upward_low)
    features = features_ref[...].astype(F32).reshape(ROWS, LANES)
    mixed = features + conv_ref[...] + upward
    mixed_held[...] = mixed.reshape(BRICKS, 8, 8, LANES).astype(BF16)
    mixed_copy = pltpu.make_async_copy(mixed_held, mixed_ref, copy_sems.at[0])
    mixed_copy.start()

    back_grad = dot(hot_target_grad, back).astype(BF16)
    i, j = spread_index((128, LANES))
    back_wide = jnp.where(half_mask, dot(back_grad, one_hot(i == (j & 63))), 0.0)
    total = grad_ref[...] + dot(unpool, (back_wide * (1.0 / 64.0)).astype(BF16))
    wait_arrived(others(rim_in, n_dev), 2, "dev")
    rim_back = rim_in[...].reshape(n_dev * SLOT_ROWS, LANES)
    total = total + dot(hot_out[0:512, :], rim_back)
    z_rows = (z_rows + dot(hot_out[512:640, :], rim_back)).astype(BF16)
    low_rows = lane[:, 0:128] < 64
    first = fold_lanes(jnp.where(y_mask, dot(repeat_y, z_rows[0:64]), 0.0))
    last = fold_lanes(jnp.where(y_mask, dot(repeat_y, z_rows[64:128]), 0.0))
    total = jnp.concatenate(
        [
            total[:, 0:128] + jnp.where(low_rows, first, 0.0),
            total[:, 128:384],
            total[:, 384:512] + jnp.where(low_rows, 0.0, last),
        ],
        axis=1,
    )
    normed = normed_ref[...]
    grad_before = total * slope_ref[...]
    grad_ref[...] = grad_before
    grad_scale = fold_lanes(brick_sum(grad_before * normed))
    grad_shift = fold_lanes(brick_sum(grad_before))
    brick_all[dev] = jnp.where(low_b, grad_scale, grad_shift)
    exchange(lambda p: brick_all.at[dev], brick_all.at[dev], 11, "dev")

    wait_arrived(others(fine_in, n_grp), 9, "grp")
    part = fine_in[0].astype(F32)
    for p in range(1, n_grp):
        part = part + fine_in[p].astype(F32)
    fine_mid[dev] = part.astype(BF16)
    exchange(lambda p: fine_mid.at[dev], fine_mid.at[dev], 10, "dev")

    wait_arrived(others(coarse_mid, n_chip), 6, "chip")
    part = coarse_mid[0].astype(F32)
    for p in range(1, n_chip):
        part = part + coarse_mid[p].astype(F32)
    coarse_all[core, grp] = part.astype(BF16)
    exchange(lambda p: coarse_all.at[core, grp], coarse_all.at[core, grp], 7, "grp")

    grad_before = grad_ref[...]
    g3 = grad_before.reshape(BRICKS, 64, LANES) * per_brick(gain)
    n3 = normed_ref[...].reshape(BRICKS, 64, LANES)
    mean_g = group_mean(jnp.sum(g3, axis=1))
    mean_gn = group_mean(jnp.sum(g3 * n3, axis=1))
    result = per_brick(inverse) * (g3 - per_brick(mean_g) - n3 * per_brick(mean_gn))
    grad = cotangent_ref[...].astype(F32).reshape(ROWS, LANES)
    result = grad + result.reshape(ROWS, LANES)
    input_grad_held[...] = result.reshape(BRICKS, 8, 8, LANES).astype(BF16)
    input_grad_copy = pltpu.make_async_copy(input_grad_held, input_grad_ref, copy_sems.at[1])
    input_grad_copy.start()

    wait_arrived(others(fine_mid, n_dev), 10, "dev")
    part = fine_mid[0].astype(F32)
    for p in range(1, n_dev):
        part = part + fine_mid[p].astype(F32)
    fine_all[grp] = part.astype(BF16)
    exchange(lambda p: fine_all.at[grp], fine_all.at[grp], 12, "grp")

    wait_arrived(others(brick_all, n_dev), 11, "dev")
    embeddings = small_in[...].astype(F32)[:, 8:16, :].reshape(n_dev * BRICKS, 128)
    embeddings = embeddings + pltpu.roll(embeddings, 64, 1)
    time_grad = lax.dot_general(
        embeddings,
        brick_all[...].reshape(n_dev * BRICKS, 128),
        (((0,), (0,)), ((), ())),
        precision=lax.Precision.HIGHEST,
        preferred_element_type=F32,
    )
    time_all[grp] = time_grad[0:64].astype(BF16)
    exchange(lambda p: time_all.at[grp], time_all.at[grp], 13, "grp")

    wait_arrived(others(coarse_all.at[0], n_grp), 7, "grp")
    exchange(lambda p: coarse_all.at[core], coarse_all.at[core], 8, "core")
    wait_arrived(others(fine_all, n_grp), 12, "grp")
    fine_sum_ref[...] = fine_all[...].reshape(FINE_ROWS, 128)
    wait_arrived(coarse_all.at[0], 8, "core")
    coarse_sum_ref[...] = coarse_all[...].reshape(COARSE_ROWS, 128)
    wait_arrived(others(time_all, n_grp), 13, "grp")
    part = time_all[0].astype(F32)
    for p in range(1, n_grp):
        part = part + time_all[p].astype(F32)
    time_sum_ref[...] = part

    wait_sent(others(small_out, n_dev), 0, "dev")
    wait_sent(others(face_out, n_dev), 1, "dev")
    wait_sent(others(rim_out, n_dev), 2, "dev")
    wait_sent(others(back_out, n_dev), 3, "dev")
    wait_sent(pair_in, 4, "core")
    wait_sent(others(coarse_out_ref, n_grp), 5, "grp")
    wait_sent(others(coarse_mid, n_chip), 6, "chip")
    wait_sent(others(coarse_all.at[0], n_grp), 7, "grp")
    wait_sent(coarse_all.at[0], 8, "core")
    wait_sent(others(fine_out, n_grp), 9, "grp")
    wait_sent(others(fine_mid, n_dev), 10, "dev")
    wait_sent(others(brick_all, n_dev), 11, "dev")
    wait_sent(others(fine_all, n_grp), 12, "grp")
    wait_sent(others(time_all, n_grp), 13, "grp")
    mixed_copy.wait()
    input_grad_copy.wait()


def finish(
    mixed_in,
    input_grad_in,
    coarse_sum_ref,
    fine_sum_ref,
    time_sum_ref,
    mixed_ref,
    input_grad_ref,
    fine_grad_ref,
    down_grad_ref,
    coarse_grad_ref,
    up_grad_ref,
    time_grad_ref,
):
    mixed_ref[...] = mixed_in[...]
    input_grad_ref[...] = input_grad_in[...]
    coarse_grad_ref[...] = coarse_sum_ref[0:896, :].astype(F32).reshape(7, 128, 128)
    down_grad_ref[...] = coarse_sum_ref[896:960, :].astype(F32)
    up_grad_ref[...] = coarse_sum_ref[960:1024, :].astype(F32)
    for t in range(4):
        piece = fine_sum_ref[64 * t : 64 * t + 64, :].astype(F32)
        fine_grad_ref[t] = piece[:, 0:64]
        if t < 3:
            fine_grad_ref[t + 4] = pltpu.roll(piece, 64, 1)[:, 0:64]
    time_grad_ref[...] = time_sum_ref[...]


def body(n_grp, n_dev, *args):
    half = 32
    frequency = np.exp(-math.log(10000.0) * np.arange(half) / half).astype(np.float32)
    frequency = jnp.asarray(np.concatenate([frequency, frequency])[None, :])
    args = list(args)
    args[4] = jnp.swapaxes(args[4], 1, 2)
    args[6] = args[6].reshape(1, n_dev)
    args[11] = args[11].T
    vmem = pl.BlockSpec(memory_space=pltpu.VMEM)
    free = pl.BlockSpec(memory_space=pl.ANY)
    packed = jax.ShapeDtypeStruct((BRICKS, 8, 8, LANES), BF16)
    slots = (n_dev, SLOT_ROWS)
    coarse_half = COARSE_ROWS // 2
    coarse_chunk = coarse_half // n_grp
    fine_chunk = FINE_ROWS // n_grp
    held = pl.pallas_call(
        functools.partial(kernel, n_grp, n_dev),
        out_shape=(
            packed,
            packed,
            jax.ShapeDtypeStruct((COARSE_ROWS, 128), BF16),
            jax.ShapeDtypeStruct((FINE_ROWS, 128), BF16),
            jax.ShapeDtypeStruct((64, 128), F32),
        ),
        in_specs=[vmem] * 13,
        out_specs=(free, free, vmem, vmem, vmem),
        scratch_shapes=[
            pltpu.VMEM(slots + (128,), BF16),
            pltpu.VMEM(slots + (128,), BF16),
            pltpu.VMEM(slots + (LANES,), BF16),
            pltpu.VMEM(slots + (LANES,), BF16),
            pltpu.VMEM(slots + (LANES,), BF16),
            pltpu.VMEM(slots + (LANES,), BF16),
            pltpu.VMEM(slots + (128,), BF16),
            pltpu.VMEM(slots + (128,), BF16),
            pltpu.VMEM((2, coarse_half, 128), BF16),
            pltpu.VMEM((coarse_half, 128), BF16),
            pltpu.VMEM((n_grp, coarse_chunk, 128), BF16),
            pltpu.VMEM((n_grp, coarse_chunk, 128), BF16),
            pltpu.VMEM((n_dev // 2, coarse_chunk, 128), BF16),
            pltpu.VMEM((2, n_grp, coarse_chunk, 128), BF16),
            pltpu.VMEM((n_grp, fine_chunk, 128), BF16),
            pltpu.VMEM((n_grp, fine_chunk, 128), BF16),
            pltpu.VMEM((n_dev, fine_chunk, 128), BF16),
            pltpu.VMEM((n_grp, fine_chunk, 128), BF16),
            pltpu.VMEM((n_dev, BRICKS, 128), F32),
            pltpu.VMEM((n_grp, 64, 128), BF16),
            pltpu.VMEM((BRICKS, 8, 8, LANES), BF16),
            pltpu.VMEM((BRICKS, 8, 8, LANES), BF16),
            pltpu.VMEM((640 + n_dev * SLOT_ROWS, 384), BF16),
            pltpu.VMEM((640, n_dev * SLOT_ROWS), BF16),
            pltpu.VMEM((640, LANES), BF16),
            pltpu.VMEM((ROWS, LANES), F32),
            pltpu.VMEM((ROWS, LANES), F32),
            pltpu.VMEM((ROWS, LANES), F32),
            pltpu.VMEM((ROWS, LANES), F32),
            pltpu.VMEM((448, LANES), F32),
            pltpu.VMEM((1536, 256), BF16),
            pltpu.SemaphoreType.DMA((14,)),
            pltpu.SemaphoreType.DMA((14,)),
            pltpu.SemaphoreType.DMA((2,)),
        ],
        compiler_params=pltpu.CompilerParams(
            collective_id=0, has_side_effects=True, vmem_limit_bytes=56 * 1024 * 1024
        ),
    )(*args, frequency)
    outs = pl.pallas_call(
        finish,
        out_shape=(
            packed,
            packed,
            jax.ShapeDtypeStruct((7, 64, 64), F32),
            jax.ShapeDtypeStruct((64, 128), F32),
            jax.ShapeDtypeStruct((7, 128, 128), F32),
            jax.ShapeDtypeStruct((64, 128), F32),
            jax.ShapeDtypeStruct((64, 128), F32),
        ),
        in_specs=[vmem] * 5,
        out_specs=(vmem,) * 7,
        compiler_params=pltpu.CompilerParams(vmem_limit_bytes=56 * 1024 * 1024),
    )(*held)
    return outs[0], outs[1], outs[2], outs[3], outs[4], outs[5].T, outs[6]


def solution(mesh):
    split = ("grp", "dev")
    in_specs = (
        P(split, None, None, None),
        P(split, None, None, None),
        P(split),
        P(split, None),
        P(split, None, None),
        P(split),
        P(split, None, None),
        P(),
        P(),
        P(),
        P(),
        P(),
    )
    out_specs = (
        P(split, None, None, None),
        P(split, None, None, None),
        P(),
        P(),
        P(),
        P(),
        P(),
    )
    return jax.shard_map(
        functools.partial(body, mesh.shape["grp"], mesh.shape["dev"]),
        mesh=mesh,
        in_specs=in_specs,
        out_specs=out_specs,
        check_vma=False,
    )
```

```python
import functools
import math

import jax
import jax.numpy as jnp
import numpy as np
from jax import lax
from jax.experimental import pallas as pl
from jax.experimental.pallas import tpu as pltpu
from jax.sharding import PartitionSpec as P

EPSILON = 1e-05
F32 = jnp.float32
BF16 = jnp.bfloat16
BRICKS = 8
ROWS = 512
LANES = 512
SLOT_ROWS = 16
COARSE_ROWS = 1024
FINE_ROWS = 256


def iota(shape, axis):
    return lax.broadcasted_iota(jnp.int32, shape, axis)


def dot(a, b):
    return jnp.dot(a, b, preferred_element_type=F32)


def dot_nt(a, b):
    return lax.dot_general(a, b, (((1,), (1,)), ((), ())), preferred_element_type=F32)


def dot_tn(a, b):
    return lax.dot_general(a, b, (((0,), (0,)), ((), ())), preferred_element_type=F32)


def exact_dot(a, b):
    return jnp.dot(a, b, precision=lax.Precision.HIGHEST, preferred_element_type=F32)


def one_hot(condition):
    return jnp.where(condition, 1.0, 0.0).astype(BF16)


def lanes_four(v):
    return jnp.concatenate([v, v, v, v], axis=1)


def fold_lanes(v):
    s = (v[:, 0:128] + v[:, 128:256]) + (v[:, 256:384] + v[:, 384:512])
    return s + pltpu.roll(s, 64, 1)


def group_mean(sums):
    s = fold_lanes(sums)
    lane = iota(s.shape, 1)
    pair = jnp.where((lane & 1) == 0, pltpu.roll(s, 127, 1), pltpu.roll(s, 1, 1))
    return lanes_four((s + pair) * (1.0 / 1024.0))


def brick_sum(v):
    return jnp.sum(v.reshape(BRICKS, 64, LANES), axis=1)


def per_brick(v):
    return v[:, None, :]


def face_index(brick, side, r):
    base = brick * 64
    xy = jnp.where(
        side < 0.5,
        base + r,
        jnp.where(
            side < 1.5,
            base + 56 + r,
            jnp.where(side < 2.5, base + 8 * r, base + 8 * r + 7),
        ),
    )
    zz = 512 + brick * 8 + r + jnp.where(side > 4.5, 64, 0)
    return jnp.where(side < 3.5, xy, zz)


def shift_rows(v, amount):
    return pltpu.roll(v, amount % v.shape[0], 0)


def z_table(v, mask, select):
    i, j = iota((128, LANES), 0), iota((128, LANES), 1)
    low = one_hot(i == (j & 63))
    high = one_hot(i - 64 == (j & 63))
    first = jnp.where(mask, dot(v[:, 0:128], low), 0.0).astype(BF16)
    last = jnp.where(mask, dot(v[:, 384:512], high), 0.0).astype(BF16)
    return dot(select, first).astype(BF16), dot(select, last).astype(BF16)


def diagonal_sum(blocks, low_shift, high_shift, count):
    even = odd = None
    for z in range(count):
        zr, zc = z + low_shift, z + high_shift
        if not (0 <= zr < count and 0 <= zc < count):
            continue
        piece = blocks[64 * zr : 64 * zr + 64, 128 * (zc // 2) : 128 * (zc // 2) + 128]
        if zc % 2 == 0:
            even = piece if even is None else even + piece
        else:
            odd = piece if odd is None else odd + piece
    return even + pltpu.roll(odd, 64, 1)


def kernel(
    n_grp,
    n_dev,
    features_far,
    cotangent_far,
    steps_far,
    links_far,
    sources_far,
    targets_far,
    places_far,
    time_weight_far,
    fine_weight_far,
    down_weight_far,
    coarse_weight_far,
    up_weight_far,
    frequency_far,
    mixed_ref,
    input_grad_ref,
    coarse_sum_ref,
    fine_sum_ref,
    time_sum_ref,
    small_out,
    small_in,
    face_out,
    face_in,
    layer_out,
    layer_in,
    back_out,
    back_in,
    coarse_part,
    coarse_in,
    coarse_mid,
    coarse_all,
    fine_out,
    fine_in,
    fine_mid,
    fine_all,
    brick_all,
    time_all,
    mixed_held,
    input_grad_held,
    hot_halo,
    hot_out,
    table,
    normed_ref,
    slope_ref,
    conv_ref,
    grad_ref,
    weight_ref,
    band_ref,
    send_sems,
    recv_sems,
    copy_sems,
    features_ref,
    cotangent_ref,
    steps_ref,
    links_ref,
    sources_ref,
    targets_ref,
    places_ref,
    time_weight_ref,
    fine_weight_ref,
    down_weight_ref,
    coarse_weight_ref,
    up_weight_ref,
    frequency_ref,
    load_sems,
):
    grp = lax.axis_index("grp")
    dev = lax.axis_index("dev")
    chip = dev // 2
    core = dev % 2
    n_chip = n_dev // 2
    coarse_chunk = COARSE_ROWS // 2 // n_grp

    rings = {
        "dev": (dev, n_dev, lambda p: (grp, p)),
        "chip": (chip, n_chip, lambda p: (grp, 2 * p + core)),
        "grp": (grp, n_grp, lambda p: (p, dev)),
        "cross": (grp, n_grp, lambda p: (p, 2 * chip + 1 - core)),
        "plane": (2 * grp + core, 2 * n_grp, lambda p: (p // 2, 2 * chip + p % 2)),
    }

    def device_at(along, p):
        grp_at, dev_at = rings[along][2](p)
        return {"grp": grp_at, "dev": dev_at}

    def entry_signal():
        barrier = pltpu.get_barrier_semaphore()
        for along in ("dev", "grp", "cross"):
            me, count, _ = rings[along]

            def step(j, carry, along=along, me=me, count=count):
                pl.semaphore_signal(
                    barrier,
                    inc=1,
                    device_id=device_at(along, lax.rem(me + j, count)),
                    device_id_type=pl.DeviceIdType.MESH,
                )
                return carry

            lax.fori_loop(1, count, step, 0)

    def entry_wait():
        pl.semaphore_wait(pltpu.get_barrier_semaphore(), n_dev - 1 + 2 * (n_grp - 1))

    def remote(src, dst, index, along, p):
        return pltpu.make_async_remote_copy(
            src_ref=src,
            dst_ref=dst,
            send_sem=send_sems.at[index],
            recv_sem=recv_sems.at[index],
            device_id=device_at(along, p),
            device_id_type=pl.DeviceIdType.MESH,
        )

    def exchange(src, dst, index, along):
        me, count, _ = rings[along]

        def step(j, carry):
            p = lax.rem(me + j, count)
            remote(src(p), dst, index, along, p).start()
            return carry

        lax.fori_loop(1, count, step, 0)

    def wait_arrived(part, index, along):
        me, count, _ = rings[along]
        if count > 1:
            remote(part, part, index, along, lax.rem(me + 1, count)).wait_recv()

    def wait_sent(part, index, along):
        me, count, _ = rings[along]
        if count > 1:
            remote(part, part, index, along, lax.rem(me + 1, count)).wait_send()

    def others(ref, count):
        return ref.at[pl.ds(0, max(count - 1, 1))]

    loads = [
        pltpu.make_async_copy(far, near, load_sems.at[index])
        for index, (far, near) in enumerate(
            (
                (features_far, features_ref),
                (cotangent_far, cotangent_ref),
                (steps_far, steps_ref),
                (links_far, links_ref),
                (sources_far, sources_ref),
                (targets_far, targets_ref),
                (places_far, places_ref),
                (time_weight_far, time_weight_ref),
                (fine_weight_far, fine_weight_ref),
                (down_weight_far, down_weight_ref),
                (coarse_weight_far, coarse_weight_ref),
                (up_weight_far, up_weight_ref),
                (frequency_far, frequency_ref),
            )
        )
    ]
    for load in loads:
        load.start()
    entry_signal()
    for load in loads:
        load.wait()

    row = iota((ROWS, LANES), 0)
    lane = iota((ROWS, LANES), 1)
    y_mask = (lane >> 6) == (row & 7)

    def spread_index(shape):
        return iota(shape, 0), iota(shape, 1)

    i, j = spread_index((n_dev, n_dev * SLOT_ROWS))
    by_slot = (j >> 4) == i
    spread_slot = jnp.where(by_slot, 1.0, 0.0)
    sources = exact_dot(sources_ref[0].astype(F32), spread_slot)
    j = iota((1, n_dev * SLOT_ROWS), 1)
    code = jnp.where(((j >> 3) & 1) == 0, sources[0:1], sources[1:2])
    brick = jnp.zeros_like(code)
    for m in range(1, BRICKS):
        brick = brick + jnp.where(code > 6.0 * m - 0.5, 1.0, 0.0)
    r = (iota(code.shape, 1) & 7).astype(F32)
    out_index = jnp.where(code < -0.5, -1.0, face_index(brick, code - 6.0 * brick, r))
    out_index = out_index.astype(jnp.int32)
    hot_out[...] = one_hot(iota((640, n_dev * SLOT_ROWS), 0) == out_index)

    i, j = spread_index((BRICKS, 384))
    links = links_ref[...].astype(F32)
    link = jnp.zeros((BRICKS, 384), F32)
    for k in range(6):
        link = link + jnp.where((j >> 6) == k, links[:, k : k + 1], 0.0)
    link = jnp.sum(jnp.where(((j >> 3) & 7) == i, link, 0.0), axis=0, keepdims=True)
    k_row = iota((1, 384), 1) >> 6
    side = (k_row + 1 - 2 * (k_row & 1)).astype(F32)
    r = (iota((1, 384), 1) & 7).astype(F32)
    halo_index = jnp.where(
        link < -0.5,
        -1.0,
        jnp.where(link < 7.5, face_index(link, side, r), 640 + (link - 8.0) * 8 + r),
    ).astype(jnp.int32)
    hot_halo[...] = one_hot(iota((640 + n_dev * SLOT_ROWS, 384), 0) == halo_index)

    i, j = spread_index((64, BRICKS))
    targets = targets_ref[...].astype(F32).reshape(1, BRICKS)
    target = jnp.sum(jnp.where((i >> 3) == j, targets, 0.0), axis=1, keepdims=True)
    child = (iota((64, 1), 0) & 7).astype(F32)
    target_code = (target * 16 + child).astype(jnp.int32)
    slot_lane = iota((64, n_dev * SLOT_ROWS), 1)
    hot_target = one_hot(slot_lane == target_code)
    hot_target_grad = one_hot(slot_lane == target_code + 8)

    i, j = spread_index((64, ROWS))
    pool = one_hot(
        ((i >> 3) == (j >> 6))
        & (((i >> 2) & 1) == ((j >> 5) & 1))
        & (((i >> 1) & 1) == ((j >> 2) & 1))
    )
    i, j = spread_index((64, LANES))
    half_mask = (i & 1) == (j >> 8)
    select_x = one_hot(i == (j >> 3))
    i, j = spread_index((ROWS, 64))
    unpool = one_hot(
        ((j >> 3) == (i >> 6))
        & (((j >> 2) & 1) == ((i >> 5) & 1))
        & (((j >> 1) & 1) == ((i >> 2) & 1))
    )
    repeat_y = one_hot(j == (i >> 3))
    repeat_x = one_hot(j == ((i >> 6) * 8 + (i & 7)))
    low_half = iota((64, 128), 1) < 64

    grad = cotangent_ref[...].astype(F32).reshape(ROWS, LANES)
    grad_b = grad.astype(BF16)
    i, j = spread_index((64, ROWS))
    g4 = grad.reshape(BRICKS, 8, 8, LANES)
    grad_z = z_table(grad_b, y_mask, select_x)
    layers = [
        g4[:, 0].reshape(64, LANES).astype(BF16),
        g4[:, 7].reshape(64, LANES).astype(BF16),
        dot(one_hot(j == i * 8), grad_b).astype(BF16),
        dot(one_hot(j == i * 8 + 7), grad_b).astype(BF16),
        grad_z[0],
        grad_z[1],
    ]
    hot_slots = hot_halo[640 : 640 + n_dev * SLOT_ROWS, :]
    layer_out[...] = (
        dot(hot_slots, jnp.concatenate(layers, axis=0))
        .astype(BF16)
        .reshape(n_dev, SLOT_ROWS, LANES)
    )
    layer_in[dev] = layer_out[dev]
    directions = dot(hot_slots, (iota((384, 128), 0) >> 6).astype(F32).astype(BF16))

    features = features_ref[...].astype(F32).reshape(ROWS, LANES)
    f3 = features.reshape(BRICKS, 64, LANES)
    centred = f3 - per_brick(group_mean(jnp.sum(f3, axis=1)))
    variance = group_mean(jnp.sum(centred * centred, axis=1))
    inverse = lax.rsqrt(variance + EPSILON)
    normed = (centred * per_brick(inverse)).reshape(ROWS, LANES)
    normed_ref[...] = normed
    i, j = spread_index((BRICKS, BRICKS))
    steps = steps_ref[...].astype(F32).reshape(1, BRICKS)
    step_column = jnp.sum(jnp.where(i == j, steps, 0.0), axis=1, keepdims=True)
    angles = step_column * frequency_ref[...]
    embedding = jnp.where(iota((BRICKS, 64), 1) < 32, jnp.cos(angles), jnp.sin(angles))
    modulate = exact_dot(embedding, time_weight_ref[...])
    swapped = pltpu.roll(modulate, 64, 1)
    low_b = iota((BRICKS, 128), 1) < 64
    scale = lanes_four(jnp.where(low_b, modulate, swapped))
    shift = lanes_four(jnp.where(low_b, swapped, modulate))
    gain = 1.0 + scale
    before = (
        normed.reshape(BRICKS, 64, LANES) * per_brick(gain) + per_brick(shift)
    ).reshape(ROWS, LANES)
    sigmoid = 1.0 / (1.0 + jnp.exp(-before))
    slope_ref[...] = sigmoid * (1.0 + before * (1.0 - sigmoid))
    active = (before * sigmoid).astype(BF16)
    table[0:512, :] = active

    pooled = fold_lanes(jnp.where(half_mask, dot(pool, active), 0.0)) * (1.0 / 64.0)
    grad_up = fold_lanes(jnp.where(half_mask, dot(pool, grad_b), 0.0))
    small = jnp.where(low_half, pooled, grad_up).astype(BF16)
    wide = jnp.concatenate([embedding, embedding], axis=1)
    wide = jnp.concatenate([jnp.zeros((8, 128), F32), wide] * n_dev, axis=0)
    i, j = spread_index((n_dev * SLOT_ROWS, 128))
    codes = jnp.where(j < 96, shift_rows(directions, 8), directions)
    codes = jnp.where((i & 8) == 8, codes, 0.0)
    small = dot_tn(hot_target, small) + jnp.where(j < 64, wide, codes)
    small_out[...] = small.astype(BF16).reshape(n_dev, SLOT_ROWS, 128)
    small_in[dev] = small_out[dev]

    entry_wait()
    exchange(lambda p: small_out.at[p], small_in.at[dev], 0, "dev")
    exchange(lambda p: layer_out.at[p], layer_in.at[dev], 2, "dev")

    z_first, z_last = z_table(active, y_mask, select_x)
    table[512:576, :] = z_first
    table[576:640, :] = z_last
    face_out[...] = (
        dot_tn(hot_out[...], table[...]).astype(BF16).reshape(n_dev, SLOT_ROWS, LANES)
    )
    face_in[dev] = face_out[dev]

    i, j = spread_index((64, LANES))
    wide = dot(fine_weight_ref[...].reshape(448, 64), one_hot(i == (j & 63)))
    weight_ref[...] = wide
    i, j = spread_index((256, 256))
    block = (i >> 6) == (j >> 6)
    for k in range(6):
        piece = weight_ref[64 * (k + 1) : 64 * (k + 2), 0:256]
        band_ref[256 * k : 256 * (k + 1), :] = jnp.where(
            block, jnp.concatenate([piece] * 4, axis=0), 0.0
        ).astype(BF16)
    z_step = (lane >> 6) - (row >> 6)
    middle = jnp.where(
        z_step == 0,
        jnp.concatenate([weight_ref[0:64, :]] * 8, axis=0),
        jnp.where(
            z_step == 1,
            jnp.concatenate([weight_ref[320:384, :]] * 8, axis=0),
            jnp.where(
                z_step == -1, jnp.concatenate([weight_ref[384:448, :]] * 8, axis=0), 0.0
            ),
        ),
    ).astype(BF16)

    def times_band(v, k):
        band = band_ref[256 * k : 256 * (k + 1), :]
        return jnp.concatenate([dot_nt(v[:, 0:256], band), dot_nt(v[:, 256:512], band)], axis=1)

    rim = jnp.concatenate([times_band(layers[k], k).astype(BF16) for k in range(6)], axis=0)

    x_at, y_at = (row >> 3) & 7, row & 7

    def shifted(v, k, edge):
        amount, at, end = ((8, x_at, 0), (-8, x_at, 7), (1, y_at, 0), (-1, y_at, 7))[k]
        return jnp.where(at == end, edge, shift_rows(v, amount))

    total = dot_nt(grad_b, middle)
    left, right = total[:, 0:256], total[:, 256:512]
    for k in range(4):
        moved = shifted(grad, k ^ 1, 0.0).astype(BF16)
        band = band_ref[256 * k : 256 * (k + 1), :]
        left = left + dot_nt(moved[:, 0:256], band)
        right = right + dot_nt(moved[:, 256:512], band)
    total = jnp.concatenate([left, right], axis=1)
    total = total + dot(hot_halo[0:512, :], rim)
    z_rows = dot(hot_halo[512:640, :], rim)
    grad_ref[...] = total

    active_f = active.astype(F32)
    halo = dot_tn(hot_halo[0:640, :], table[...]).astype(BF16)
    grad_t = grad.T.astype(BF16)
    center = dot(grad_t, active)
    conv = dot(active, middle)
    left, right = conv[:, 0:256], conv[:, 256:512]
    tap_grads = [diagonal_sum(center, 0, 0, 8)]
    for k in range(4):
        repeat = repeat_x if k < 2 else repeat_y
        moved = shifted(active_f, k, dot(repeat, halo[64 * k : 64 * k + 64])).astype(BF16)
        band = band_ref[256 * k : 256 * (k + 1), :]
        left = left + dot(moved[:, 0:256], band)
        right = right + dot(moved[:, 256:512], band)
        tap_grads.append(
            diagonal_sum(dot(grad_t[0:256], moved[:, 0:256]), 0, 0, 4)
            + diagonal_sum(dot(grad_t[256:512], moved[:, 256:512]), 0, 0, 4)
        )
    low_z = jnp.where(y_mask, dot(repeat_y, halo[256:320]), 0.0).astype(BF16)
    high_z = jnp.where(y_mask, dot(repeat_y, halo[320:384]), 0.0).astype(BF16)
    end = jnp.where(low_half, weight_ref[320:384, 0:128], 0.0).astype(BF16)
    first = dot(low_z, jnp.concatenate([end] * 8, axis=0))
    end = jnp.where(low_half, 0.0, weight_ref[384:448, 0:128]).astype(BF16)
    last = dot(high_z, jnp.concatenate([end] * 8, axis=0))
    conv_ref[...] = jnp.concatenate(
        [left[:, 0:128] + first, left[:, 128:256], right[:, 0:128], right[:, 128:256] + last],
        axis=1,
    )
    tap_grads.append(diagonal_sum(center, 0, -1, 8) + fold_lanes(dot(grad_t[0:64], low_z)))
    tap_grads.append(diagonal_sum(center, 0, 1, 8) + fold_lanes(dot(grad_t[448:512], high_z)))

    place = exact_dot(places_ref[...].astype(F32), spread_slot)
    j = iota((1, n_dev * SLOT_ROWS), 1)
    place_code = (place * 8 + (j & 7).astype(F32)).astype(jnp.int32)
    i = iota((ROWS, 1), 0)
    voxel_code = (
        ((i >> 7) * 16 + ((i >> 4) & 3) * 4 + ((i >> 1) & 3)) * 8
        + ((i >> 6) & 1) * 4
        + ((i >> 3) & 1) * 2
        + (i & 1)
    )
    first_kind = (j & 8) == 0
    hot_place = one_hot(voxel_code == jnp.where(first_kind, place_code, -1))
    hot_place_grad = one_hot(voxel_code == jnp.where(first_kind, -1, place_code))
    wait_arrived(others(small_in, n_dev), 0, "dev")
    grid = dot(hot_place, small_in[...].reshape(n_dev * SLOT_ROWS, 128)).astype(BF16)
    down = jnp.concatenate([down_weight_ref[...], jnp.zeros((64, 128), BF16)], axis=0)
    up = jnp.concatenate([jnp.zeros((64, 128), BF16), up_weight_ref[...]], axis=0)
    coarse_pre = dot(grid, down)
    coarse_sig = 1.0 / (1.0 + jnp.exp(-coarse_pre))
    coarse_act = coarse_pre * coarse_sig
    row_c = iota((ROWS, 128), 0)
    at_c = (row_c >> 6, (row_c >> 3) & 7, row_c & 7)

    def coarse_shifted(v, k):
        amount = (64, -64, 8, -8, 1, -1)[k]
        return jnp.where(at_c[k // 2] == 7 * (k % 2), 0.0, shift_rows(v, amount))

    coarse_act_f = coarse_act.astype(BF16).astype(F32)
    stack = jnp.concatenate(
        [coarse_act_f.astype(BF16)]
        + [coarse_shifted(coarse_act_f, k).astype(BF16) for k in range(6)],
        axis=1,
    )
    coarse_out = dot(stack, coarse_weight_ref[...].reshape(896, 128)).astype(BF16)
    grad_out = dot(grid, up)
    grad_out_b = grad_out.astype(BF16)
    grad_act = dot_nt(grad_out_b, coarse_weight_ref[0])
    for k in range(6):
        grad_act = grad_act + dot_nt(
            coarse_shifted(grad_out, k ^ 1).astype(BF16), coarse_weight_ref[k + 1]
        )
    grad_pre = grad_act * coarse_sig * (1.0 + coarse_pre * (1.0 - coarse_sig))
    grad_pre = grad_pre.astype(BF16)
    grad_pooled = dot_nt(grad_pre, down).astype(BF16)
    back_out[...] = (
        (dot_tn(hot_place, coarse_out) + dot_tn(hot_place_grad, grad_pooled))
        .astype(BF16)
        .reshape(n_dev, SLOT_ROWS, 128)
    )
    back_in[dev] = back_out[dev]
    exchange(lambda p: back_out.at[p], back_in.at[dev], 3, "dev")

    coarse_grad = dot_tn(stack, grad_out_b)
    down_grad = dot_tn(grid, grad_pre)
    up_grad = dot_tn(grid, coarse_out)
    part = jnp.concatenate([coarse_grad, down_grad[0:64], up_grad[64:128]], axis=0)
    coarse_part[...] = part.astype(BF16).reshape(2 * n_grp, coarse_chunk, 128)
    plane = rings["plane"][0]
    coarse_in[plane] = coarse_part[plane]
    exchange(lambda p: coarse_part.at[p], coarse_in.at[plane], 4, "plane")

    exchange(lambda p: face_out.at[p], face_in.at[dev], 1, "dev")

    wait_arrived(others(layer_in, n_dev), 2, "dev")
    came = layer_in[...].reshape(n_dev * SLOT_ROWS, LANES)
    came_f = came.astype(F32)
    came_t = came_f.T.astype(BF16)
    faces = face_out[...].reshape(n_dev * SLOT_ROWS, LANES).astype(F32)
    marks = small_in[...].reshape(n_dev * SLOT_ROWS, 128).astype(F32)
    odd_slot = (iota((n_dev * SLOT_ROWS, 1), 0) & 8) == 8
    way = jnp.where(odd_slot, marks[:, 96:97], shift_rows(marks, -8)[:, 64:65])
    for k in range(6):
        own_faces = jnp.where(way == float(k), faces, 0.0).astype(BF16)
        tap_grads[k + 1] = (
            tap_grads[k + 1]
            + diagonal_sum(dot(came_t[0:256], own_faces[:, 0:256]), 0, 0, 4)
            + diagonal_sum(dot(came_t[256:512], own_faces[:, 256:512]), 0, 0, 4)
        )
    fine_rows = []
    for t in range(4):
        low = tap_grads[t].T[0:64]
        high = tap_grads[t + 4].T[0:64] if t < 3 else jnp.zeros_like(low)
        fine_rows.append(jnp.concatenate([low, high], axis=1))
    part = jnp.concatenate(fine_rows, axis=0)
    fine_out[...] = part.astype(BF16).reshape(n_grp, FINE_ROWS // n_grp, 128)
    fine_in[grp] = fine_out[grp]
    exchange(lambda p: fine_out.at[p], fine_in.at[grp], 7, "grp")

    rim_back = jnp.zeros((n_dev * SLOT_ROWS, LANES), F32)
    for k in range(6):
        rim_back = rim_back + times_band(
            jnp.where(way == float(k), came_f, 0.0).astype(BF16), k
        )
    rim_back = rim_back.astype(BF16)
    total = grad_ref[...] + dot(hot_out[0:512, :], rim_back)
    z_rows = (z_rows + dot(hot_out[512:640, :], rim_back)).astype(BF16)
    low_rows = lane[:, 0:128] < 64
    first = fold_lanes(jnp.where(y_mask, dot(repeat_y, z_rows[0:64]), 0.0))
    last = fold_lanes(jnp.where(y_mask, dot(repeat_y, z_rows[64:128]), 0.0))
    grad_ref[...] = jnp.concatenate(
        [
            total[:, 0:128] + jnp.where(low_rows, first, 0.0),
            total[:, 128:384],
            total[:, 384:512] + jnp.where(low_rows, 0.0, last),
        ],
        axis=1,
    )

    wait_arrived(others(coarse_in, 2 * n_grp), 4, "plane")
    part = coarse_in[0].astype(F32)
    for p in range(1, 2 * n_grp):
        part = part + coarse_in[p].astype(F32)
    coarse_mid[chip] = part.astype(BF16)
    exchange(lambda p: coarse_mid.at[chip], coarse_mid.at[chip], 5, "chip")

    wait_arrived(others(back_in, n_dev), 3, "dev")
    back = back_in[...].reshape(n_dev * SLOT_ROWS, 128)
    back_grad = dot(hot_target_grad, back).astype(BF16)
    i, j = spread_index((128, LANES))
    back_wide = jnp.where(half_mask, dot(back_grad, one_hot(i == (j & 63))), 0.0)
    total = grad_ref[...] + dot(unpool, (back_wide * (1.0 / 64.0)).astype(BF16))
    normed = normed_ref[...]
    grad_before = total * slope_ref[...]
    grad_ref[...] = grad_before
    grad_scale = fold_lanes(brick_sum(grad_before * normed))
    grad_shift = fold_lanes(brick_sum(grad_before))
    brick_all[dev] = jnp.where(low_b, grad_scale, grad_shift)
    exchange(lambda p: brick_all.at[dev], brick_all.at[dev], 9, "dev")

    wait_arrived(others(fine_in, n_grp), 7, "grp")
    part = fine_in[0].astype(F32)
    for p in range(1, n_grp):
        part = part + fine_in[p].astype(F32)
    fine_mid[dev] = part.astype(BF16)
    exchange(lambda p: fine_mid.at[dev], fine_mid.at[dev], 8, "dev")

    grad_before = grad_ref[...]
    g3 = grad_before.reshape(BRICKS, 64, LANES) * per_brick(gain)
    n3 = normed_ref[...].reshape(BRICKS, 64, LANES)
    mean_g = group_mean(jnp.sum(g3, axis=1))
    mean_gn = group_mean(jnp.sum(g3 * n3, axis=1))
    result = per_brick(inverse) * (g3 - per_brick(mean_g) - n3 * per_brick(mean_gn))
    grad = cotangent_ref[...].astype(F32).reshape(ROWS, LANES)
    result = grad + result.reshape(ROWS, LANES)
    input_grad_held[...] = result.reshape(BRICKS, 8, 8, LANES).astype(BF16)
    input_grad_copy = pltpu.make_async_copy(input_grad_held, input_grad_ref, copy_sems.at[1])
    input_grad_copy.start()

    coarse_values = dot(hot_target, back).astype(BF16)
    i, j = spread_index((64, LANES))
    up_wide = dot_tn(up_weight_ref[...], one_hot(i == (j & 63))).astype(BF16)
    upward = jnp.where(half_mask, dot(coarse_values, up_wide), 0.0)
    upward_high = upward.astype(BF16)
    upward_low = (upward - upward_high.astype(F32)).astype(BF16)
    upward = dot(unpool, upward_high) + dot(unpool, upward_low)
    features = features_ref[...].astype(F32).reshape(ROWS, LANES)
    conv_ref[...] = features + conv_ref[...] + upward
    i, j = spread_index((ROWS, 256))
    x, y = (i >> 3) & 7, i & 7
    by_x = (j & 63) == ((i >> 6) * 8 + y)
    by_y = (j & 63) == (i >> 3)
    way = j >> 6
    edges = one_hot(
        ((way == 0) & (x == 0) & by_x)
        | ((way == 1) & (x == 7) & by_x)
        | ((way == 2) & (y == 0) & by_y)
        | ((way == 3) & (y == 7) & by_y)
    )

    wait_arrived(others(coarse_mid, n_chip), 5, "chip")
    part = coarse_mid[0].astype(F32)
    for p in range(1, n_chip):
        part = part + coarse_mid[p].astype(F32)
    coarse_all[plane] = part.astype(BF16)
    exchange(lambda p: coarse_all.at[plane], coarse_all.at[plane], 6, "plane")

    wait_arrived(others(brick_all, n_dev), 9, "dev")
    embeddings = small_in[...].astype(F32)[:, 8:16, :].reshape(n_dev * BRICKS, 128)
    time_grad = lax.dot_general(
        embeddings,
        brick_all[...].reshape(n_dev * BRICKS, 128),
        (((0,), (0,)), ((), ())),
        precision=lax.Precision.HIGHEST,
        preferred_element_type=F32,
    )
    time_all[grp] = time_grad[0:64].astype(BF16)
    exchange(lambda p: time_all.at[grp], time_all.at[grp], 11, "grp")

    wait_arrived(others(fine_mid, n_dev), 8, "dev")
    part = fine_mid[0].astype(F32)
    for p in range(1, n_dev):
        part = part + fine_mid[p].astype(F32)
    fine_all[grp] = part.astype(BF16)
    exchange(lambda p: fine_all.at[grp], fine_all.at[grp], 10, "grp")

    wait_arrived(others(face_in, n_dev), 1, "dev")
    halo = dot_tn(hot_halo[640 : 640 + n_dev * SLOT_ROWS, :], face_in[...].reshape(-1, LANES))
    halo = halo.astype(BF16)
    sides = []
    for k in range(6):
        band = band_ref[256 * k : 256 * (k + 1), :]
        piece = halo[64 * k : 64 * k + 64]
        sides.append(
            jnp.concatenate([dot(piece[:, 0:256], band), dot(piece[:, 256:512], band)], axis=1)
            .astype(BF16)
        )
    mixed = conv_ref[...] + dot(edges, jnp.concatenate(sides[0:4], axis=0))
    first = fold_lanes(jnp.where(y_mask, dot(repeat_y, sides[4]), 0.0))
    last = fold_lanes(jnp.where(y_mask, dot(repeat_y, sides[5]), 0.0))
    mixed = jnp.concatenate(
        [
            mixed[:, 0:128] + jnp.where(low_rows, first, 0.0),
            mixed[:, 128:384],
            mixed[:, 384:512] + jnp.where(low_rows, 0.0, last),
        ],
        axis=1,
    )
    mixed_held[...] = mixed.reshape(BRICKS, 8, 8, LANES).astype(BF16)
    mixed_copy = pltpu.make_async_copy(mixed_held, mixed_ref, copy_sems.at[0])
    mixed_copy.start()

    wait_arrived(others(coarse_all, 2 * n_grp), 6, "plane")
    coarse_sum_ref[...] = coarse_all[...].reshape(COARSE_ROWS, 128)
    wait_arrived(others(fine_all, n_grp), 10, "grp")
    fine_sum_ref[...] = fine_all[...].reshape(FINE_ROWS, 128)
    wait_arrived(others(time_all, n_grp), 11, "grp")
    part = time_all[0].astype(F32)
    for p in range(1, n_grp):
        part = part + time_all[p].astype(F32)
    time_sum_ref[...] = part

    wait_sent(others(small_out, n_dev), 0, "dev")
    wait_sent(others(face_out, n_dev), 1, "dev")
    wait_sent(others(layer_out, n_dev), 2, "dev")
    wait_sent(others(back_out, n_dev), 3, "dev")
    wait_sent(others(coarse_part, 2 * n_grp), 4, "plane")
    wait_sent(others(coarse_mid, n_chip), 5, "chip")
    wait_sent(others(coarse_all, 2 * n_grp), 6, "plane")
    wait_sent(others(fine_out, n_grp), 7, "grp")
    wait_sent(others(fine_mid, n_dev), 8, "dev")
    wait_sent(others(brick_all, n_dev), 9, "dev")
    wait_sent(others(fine_all, n_grp), 10, "grp")
    wait_sent(others(time_all, n_grp), 11, "grp")
    mixed_copy.wait()
    input_grad_copy.wait()


def finish(
    mixed_in,
    input_grad_in,
    coarse_sum_ref,
    fine_sum_ref,
    time_sum_ref,
    mixed_ref,
    input_grad_ref,
    fine_grad_ref,
    down_grad_ref,
    coarse_grad_ref,
    up_grad_ref,
    time_grad_ref,
):
    mixed_ref[...] = mixed_in[...]
    input_grad_ref[...] = input_grad_in[...]
    coarse_grad_ref[...] = coarse_sum_ref[0:896, :].astype(F32).reshape(7, 128, 128)
    down_grad_ref[...] = coarse_sum_ref[896:960, :].astype(F32)
    up_grad_ref[...] = coarse_sum_ref[960:1024, :].astype(F32)
    for t in range(4):
        piece = fine_sum_ref[64 * t : 64 * t + 64, :].astype(F32)
        fine_grad_ref[t] = piece[:, 0:64]
        if t < 3:
            fine_grad_ref[t + 4] = pltpu.roll(piece, 64, 1)[:, 0:64]
    time_grad_ref[...] = time_sum_ref[...]


def body(n_grp, n_dev, *args):
    half = 32
    frequency = np.exp(-math.log(10000.0) * np.arange(half) / half).astype(np.float32)
    frequency = jnp.asarray(np.concatenate([frequency, frequency])[None, :])
    args = list(args)
    args[4] = jnp.swapaxes(args[4], 1, 2)
    args[6] = args[6].reshape(1, n_dev)
    args[11] = args[11].T
    args.append(frequency)
    vmem = pl.BlockSpec(memory_space=pltpu.VMEM)
    free = pl.BlockSpec(memory_space=pl.ANY)
    packed = jax.ShapeDtypeStruct((BRICKS, 8, 8, LANES), BF16)
    slots = (n_dev, SLOT_ROWS)
    coarse_chunk = COARSE_ROWS // 2 // n_grp
    fine_chunk = FINE_ROWS // n_grp
    held = pl.pallas_call(
        functools.partial(kernel, n_grp, n_dev),
        out_shape=(
            packed,
            packed,
            jax.ShapeDtypeStruct((COARSE_ROWS, 128), BF16),
            jax.ShapeDtypeStruct((FINE_ROWS, 128), BF16),
            jax.ShapeDtypeStruct((64, 128), F32),
        ),
        in_specs=[free] * 13,
        out_specs=(free, free, vmem, vmem, vmem),
        scratch_shapes=[
            pltpu.VMEM(slots + (128,), BF16),
            pltpu.VMEM(slots + (128,), BF16),
            pltpu.VMEM(slots + (LANES,), BF16),
            pltpu.VMEM(slots + (LANES,), BF16),
            pltpu.VMEM(slots + (LANES,), BF16),
            pltpu.VMEM(slots + (LANES,), BF16),
            pltpu.VMEM(slots + (128,), BF16),
            pltpu.VMEM(slots + (128,), BF16),
            pltpu.VMEM((2 * n_grp, coarse_chunk, 128), BF16),
            pltpu.VMEM((2 * n_grp, coarse_chunk, 128), BF16),
            pltpu.VMEM((n_dev // 2, coarse_chunk, 128), BF16),
            pltpu.VMEM((2 * n_grp, coarse_chunk, 128), BF16),
            pltpu.VMEM((n_grp, fine_chunk, 128), BF16),
            pltpu.VMEM((n_grp, fine_chunk, 128), BF16),
            pltpu.VMEM((n_dev, fine_chunk, 128), BF16),
            pltpu.VMEM((n_grp, fine_chunk, 128), BF16),
            pltpu.VMEM((n_dev, BRICKS, 128), F32),
            pltpu.VMEM((n_grp, 64, 128), BF16),
            pltpu.VMEM((BRICKS, 8, 8, LANES), BF16),
            pltpu.VMEM((BRICKS, 8, 8, LANES), BF16),
            pltpu.VMEM((640 + n_dev * SLOT_ROWS, 384), BF16),
            pltpu.VMEM((640, n_dev * SLOT_ROWS), BF16),
            pltpu.VMEM((640, LANES), BF16),
            pltpu.VMEM((ROWS, LANES), F32),
            pltpu.VMEM((ROWS, LANES), F32),
            pltpu.VMEM((ROWS, LANES), F32),
            pltpu.VMEM((ROWS, LANES), F32),
            pltpu.VMEM((448, LANES), F32),
            pltpu.VMEM((1536, 256), BF16),
            pltpu.SemaphoreType.DMA((12,)),
            pltpu.SemaphoreType.DMA((12,)),
            pltpu.SemaphoreType.DMA((2,)),
        ]
        + [pltpu.VMEM(a.shape, a.dtype) for a in args]
        + [pltpu.SemaphoreType.DMA((13,))],
        compiler_params=pltpu.CompilerParams(
            collective_id=0, has_side_effects=True, vmem_limit_bytes=56 * 1024 * 1024
        ),
    )(*args)
    outs = pl.pallas_call(
        finish,
        out_shape=(
            packed,
            packed,
            jax.ShapeDtypeStruct((7, 64, 64), F32),
            jax.ShapeDtypeStruct((64, 128), F32),
            jax.ShapeDtypeStruct((7, 128, 128), F32),
            jax.ShapeDtypeStruct((64, 128), F32),
            jax.ShapeDtypeStruct((64, 128), F32),
        ),
        in_specs=[vmem] * 5,
        out_specs=(vmem,) * 7,
        compiler_params=pltpu.CompilerParams(vmem_limit_bytes=56 * 1024 * 1024),
    )(*held)
    return outs[0], outs[1], outs[2], outs[3], outs[4], outs[5].T, outs[6]


def solution(mesh):
    split = ("grp", "dev")
    in_specs = (
        P(split, None, None, None),
        P(split, None, None, None),
        P(split),
        P(split, None),
        P(split, None, None),
        P(split),
        P(split, None, None),
        P(),
        P(),
        P(),
        P(),
        P(),
    )
    out_specs = (
        P(split, None, None, None),
        P(split, None, None, None),
        P(),
        P(),
        P(),
        P(),
        P(),
    )
    return jax.shard_map(
        functools.partial(body, mesh.shape["grp"], mesh.shape["dev"]),
        mesh=mesh,
        in_specs=in_specs,
        out_specs=out_specs,
        check_vma=False,
    )
```

```python
import functools
import math

import jax
import jax.numpy as jnp
import numpy as np
from jax import lax
from jax.experimental import pallas as pl
from jax.experimental.pallas import tpu as pltpu
from jax.sharding import PartitionSpec as P

EPSILON = 1e-05
F32 = jnp.float32
BF16 = jnp.bfloat16
BRICKS = 8
ROWS = 512
LANES = 512
SLOT_ROWS = 16
COARSE_ROWS = 1024
FINE_ROWS = 256


def iota(shape, axis):
    return lax.broadcasted_iota(jnp.int32, shape, axis)


def dot(a, b):
    return jnp.dot(a, b, preferred_element_type=F32)


def dot_nt(a, b):
    return lax.dot_general(a, b, (((1,), (1,)), ((), ())), preferred_element_type=F32)


def dot_tn(a, b):
    return lax.dot_general(a, b, (((0,), (0,)), ((), ())), preferred_element_type=F32)


def exact_dot(a, b):
    return jnp.dot(a, b, precision=lax.Precision.HIGHEST, preferred_element_type=F32)


def one_hot(condition):
    return jnp.where(condition, 1.0, 0.0).astype(BF16)


def lanes_four(v):
    return jnp.concatenate([v, v, v, v], axis=1)


def fold_lanes(v):
    s = (v[:, 0:128] + v[:, 128:256]) + (v[:, 256:384] + v[:, 384:512])
    return s + pltpu.roll(s, 64, 1)


def group_mean(sums):
    s = fold_lanes(sums)
    lane = iota(s.shape, 1)
    pair = jnp.where((lane & 1) == 0, pltpu.roll(s, 127, 1), pltpu.roll(s, 1, 1))
    return lanes_four((s + pair) * (1.0 / 1024.0))


def brick_sum(v):
    return jnp.sum(v.reshape(BRICKS, 64, LANES), axis=1)


def per_brick(v):
    return v[:, None, :]


def face_index(brick, side, r):
    base = brick * 64
    xy = jnp.where(
        side < 0.5,
        base + r,
        jnp.where(
            side < 1.5,
            base + 56 + r,
            jnp.where(side < 2.5, base + 8 * r, base + 8 * r + 7),
        ),
    )
    zz = 512 + brick * 8 + r + jnp.where(side > 4.5, 64, 0)
    return jnp.where(side < 3.5, xy, zz)


def shift_rows(v, amount):
    return pltpu.roll(v, amount % v.shape[0], 0)


def z_table(v, mask, select):
    i, j = iota((128, LANES), 0), iota((128, LANES), 1)
    low = one_hot(i == (j & 63))
    high = one_hot(i - 64 == (j & 63))
    first = jnp.where(mask, dot(v[:, 0:128], low), 0.0).astype(BF16)
    last = jnp.where(mask, dot(v[:, 384:512], high), 0.0).astype(BF16)
    return dot(select, first).astype(BF16), dot(select, last).astype(BF16)


def diagonal_sum(blocks, low_shift, high_shift, count):
    even = odd = None
    for z in range(count):
        zr, zc = z + low_shift, z + high_shift
        if not (0 <= zr < count and 0 <= zc < count):
            continue
        piece = blocks[64 * zr : 64 * zr + 64, 128 * (zc // 2) : 128 * (zc // 2) + 128]
        if zc % 2 == 0:
            even = piece if even is None else even + piece
        else:
            odd = piece if odd is None else odd + piece
    return even + pltpu.roll(odd, 64, 1)


def kernel(
    n_grp,
    n_dev,
    features_far,
    cotangent_far,
    steps_far,
    links_far,
    sources_far,
    targets_far,
    places_far,
    time_weight_far,
    fine_weight_far,
    down_weight_far,
    coarse_weight_far,
    up_weight_far,
    frequency_far,
    mixed_ref,
    input_grad_ref,
    coarse_sum_ref,
    fine_sum_ref,
    time_sum_ref,
    small_out,
    small_in,
    face_out,
    face_in,
    layer_out,
    layer_in,
    back_out,
    back_in,
    coarse_part,
    coarse_in,
    coarse_mid,
    coarse_all,
    fine_out,
    fine_in,
    fine_mid,
    fine_all,
    brick_all,
    time_all,
    mixed_held,
    input_grad_held,
    own_faces,
    hot_halo,
    hot_out,
    table,
    normed_ref,
    slope_ref,
    conv_ref,
    grad_ref,
    weight_ref,
    band_ref,
    send_sems,
    recv_sems,
    copy_sems,
    features_ref,
    cotangent_ref,
    steps_ref,
    links_ref,
    sources_ref,
    targets_ref,
    places_ref,
    time_weight_ref,
    fine_weight_ref,
    down_weight_ref,
    coarse_weight_ref,
    up_weight_ref,
    frequency_ref,
    load_sems,
):
    grp = lax.axis_index("grp")
    dev = lax.axis_index("dev")
    chip = dev // 2
    core = dev % 2
    n_chip = n_dev // 2
    coarse_chunk = COARSE_ROWS // 2 // n_grp

    rings = {
        "dev": (dev, n_dev, lambda p: (grp, p)),
        "chip": (chip, n_chip, lambda p: (grp, 2 * p + core)),
        "grp": (grp, n_grp, lambda p: (p, dev)),
        "cross": (grp, n_grp, lambda p: (p, 2 * chip + 1 - core)),
        "plane": (2 * grp + core, 2 * n_grp, lambda p: (p // 2, 2 * chip + p % 2)),
    }

    def device_at(along, p):
        grp_at, dev_at = rings[along][2](p)
        return {"grp": grp_at, "dev": dev_at}

    def entry_signal():
        barrier = pltpu.get_barrier_semaphore()
        for along in ("dev", "grp", "cross"):
            me, count, _ = rings[along]

            def step(j, carry, along=along, me=me, count=count):
                pl.semaphore_signal(
                    barrier,
                    inc=1,
                    device_id=device_at(along, lax.rem(me + j, count)),
                    device_id_type=pl.DeviceIdType.MESH,
                )
                return carry

            lax.fori_loop(1, count, step, 0)

    def entry_wait():
        pl.semaphore_wait(pltpu.get_barrier_semaphore(), n_dev - 1 + 2 * (n_grp - 1))

    def remote(src, dst, index, along, p):
        return pltpu.make_async_remote_copy(
            src_ref=src,
            dst_ref=dst,
            send_sem=send_sems.at[index],
            recv_sem=recv_sems.at[index],
            device_id=device_at(along, p),
            device_id_type=pl.DeviceIdType.MESH,
        )

    def exchange(src, dst, index, along):
        me, count, _ = rings[along]

        def step(j, carry):
            p = lax.rem(me + j, count)
            remote(src(p), dst, index, along, p).start()
            return carry

        lax.fori_loop(1, count, step, 0)

    def wait_arrived(part, index, along):
        me, count, _ = rings[along]
        if count > 1:
            remote(part, part, index, along, lax.rem(me + 1, count)).wait_recv()

    def wait_sent(part, index, along):
        me, count, _ = rings[along]
        if count > 1:
            remote(part, part, index, along, lax.rem(me + 1, count)).wait_send()

    def others(ref, count):
        return ref.at[pl.ds(0, max(count - 1, 1))]

    loads = [
        pltpu.make_async_copy(far, near, load_sems.at[index])
        for index, (far, near) in enumerate(
            (
                (features_far, features_ref),
                (cotangent_far, cotangent_ref),
                (steps_far, steps_ref),
                (links_far, links_ref),
                (sources_far, sources_ref),
                (targets_far, targets_ref),
                (places_far, places_ref),
                (time_weight_far, time_weight_ref),
                (fine_weight_far, fine_weight_ref),
                (down_weight_far, down_weight_ref),
                (coarse_weight_far, coarse_weight_ref),
                (up_weight_far, up_weight_ref),
                (frequency_far, frequency_ref),
            )
        )
    ]
    for load in loads:
        load.start()
    entry_signal()
    for load in loads:
        load.wait()

    row = iota((ROWS, LANES), 0)
    lane = iota((ROWS, LANES), 1)
    y_mask = (lane >> 6) == (row & 7)

    def spread_index(shape):
        return iota(shape, 0), iota(shape, 1)

    i, j = spread_index((n_dev, n_dev * SLOT_ROWS))
    by_slot = (j >> 4) == i
    spread_slot = jnp.where(by_slot, 1.0, 0.0)
    sources = exact_dot(sources_ref[0].astype(F32), spread_slot)
    j = iota((1, n_dev * SLOT_ROWS), 1)
    code = jnp.where(((j >> 3) & 1) == 0, sources[0:1], sources[1:2])
    brick = jnp.zeros_like(code)
    for m in range(1, BRICKS):
        brick = brick + jnp.where(code > 6.0 * m - 0.5, 1.0, 0.0)
    r = (iota(code.shape, 1) & 7).astype(F32)
    out_index = jnp.where(code < -0.5, -1.0, face_index(brick, code - 6.0 * brick, r))
    out_index = out_index.astype(jnp.int32)
    hot_out[...] = one_hot(iota((640, n_dev * SLOT_ROWS), 0) == out_index)

    i, j = spread_index((BRICKS, 384))
    links = links_ref[...].astype(F32)
    link = jnp.zeros((BRICKS, 384), F32)
    for k in range(6):
        link = link + jnp.where((j >> 6) == k, links[:, k : k + 1], 0.0)
    link = jnp.sum(jnp.where(((j >> 3) & 7) == i, link, 0.0), axis=0, keepdims=True)
    k_row = iota((1, 384), 1) >> 6
    side = (k_row + 1 - 2 * (k_row & 1)).astype(F32)
    r = (iota((1, 384), 1) & 7).astype(F32)
    halo_index = jnp.where(
        link < -0.5,
        -1.0,
        jnp.where(link < 7.5, face_index(link, side, r), 640 + (link - 8.0) * 8 + r),
    ).astype(jnp.int32)
    hot_halo[...] = one_hot(iota((640 + n_dev * SLOT_ROWS, 384), 0) == halo_index)

    i, j = spread_index((64, BRICKS))
    targets = targets_ref[...].astype(F32).reshape(1, BRICKS)
    target = jnp.sum(jnp.where((i >> 3) == j, targets, 0.0), axis=1, keepdims=True)
    child = (iota((64, 1), 0) & 7).astype(F32)
    target_code = (target * 16 + child).astype(jnp.int32)
    slot_lane = iota((64, n_dev * SLOT_ROWS), 1)
    hot_target = one_hot(slot_lane == target_code)
    hot_target_grad = one_hot(slot_lane == target_code + 8)

    i, j = spread_index((64, ROWS))
    pool = one_hot(
        ((i >> 3) == (j >> 6))
        & (((i >> 2) & 1) == ((j >> 5) & 1))
        & (((i >> 1) & 1) == ((j >> 2) & 1))
    )
    i, j = spread_index((64, LANES))
    half_mask = (i & 1) == (j >> 8)
    select_x = one_hot(i == (j >> 3))
    i, j = spread_index((ROWS, 64))
    unpool = one_hot(
        ((j >> 3) == (i >> 6))
        & (((j >> 2) & 1) == ((i >> 5) & 1))
        & (((j >> 1) & 1) == ((i >> 2) & 1))
    )
    repeat_y = one_hot(j == (i >> 3))
    repeat_x = one_hot(j == ((i >> 6) * 8 + (i & 7)))
    low_half = iota((64, 128), 1) < 64

    grad = cotangent_ref[...].astype(F32).reshape(ROWS, LANES)
    grad_b = grad.astype(BF16)
    i, j = spread_index((64, ROWS))
    g4 = grad.reshape(BRICKS, 8, 8, LANES)
    grad_z = z_table(grad_b, y_mask, select_x)
    layers = [
        g4[:, 0].reshape(64, LANES).astype(BF16),
        g4[:, 7].reshape(64, LANES).astype(BF16),
        dot(one_hot(j == i * 8), grad_b).astype(BF16),
        dot(one_hot(j == i * 8 + 7), grad_b).astype(BF16),
        grad_z[0],
        grad_z[1],
    ]
    hot_slots = hot_halo[640 : 640 + n_dev * SLOT_ROWS, :]
    layer_out[...] = (
        dot(hot_slots, jnp.concatenate(layers, axis=0))
        .astype(BF16)
        .reshape(n_dev, SLOT_ROWS, LANES)
    )
    layer_in[dev] = layer_out[dev]
    directions = dot(hot_slots, (iota((384, 128), 0) >> 6).astype(F32).astype(BF16))

    features = features_ref[...].astype(F32).reshape(ROWS, LANES)
    f3 = features.reshape(BRICKS, 64, LANES)
    centred = f3 - per_brick(group_mean(jnp.sum(f3, axis=1)))
    variance = group_mean(jnp.sum(centred * centred, axis=1))
    inverse = lax.rsqrt(variance + EPSILON)
    normed = (centred * per_brick(inverse)).reshape(ROWS, LANES)
    normed_ref[...] = normed
    i, j = spread_index((BRICKS, BRICKS))
    steps = steps_ref[...].astype(F32).reshape(1, BRICKS)
    step_column = jnp.sum(jnp.where(i == j, steps, 0.0), axis=1, keepdims=True)
    angles = step_column * frequency_ref[...]
    embedding = jnp.where(iota((BRICKS, 64), 1) < 32, jnp.cos(angles), jnp.sin(angles))
    modulate = exact_dot(embedding, time_weight_ref[...])
    swapped = pltpu.roll(modulate, 64, 1)
    low_b = iota((BRICKS, 128), 1) < 64
    scale = lanes_four(jnp.where(low_b, modulate, swapped))
    shift = lanes_four(jnp.where(low_b, swapped, modulate))
    gain = 1.0 + scale
    before = (
        normed.reshape(BRICKS, 64, LANES) * per_brick(gain) + per_brick(shift)
    ).reshape(ROWS, LANES)
    sigmoid = 1.0 / (1.0 + jnp.exp(-before))
    slope_ref[...] = sigmoid * (1.0 + before * (1.0 - sigmoid))
    active = (before * sigmoid).astype(BF16)
    table[0:512, :] = active

    pooled = fold_lanes(jnp.where(half_mask, dot(pool, active), 0.0)) * (1.0 / 64.0)
    grad_up = fold_lanes(jnp.where(half_mask, dot(pool, grad_b), 0.0))
    small = jnp.where(low_half, pooled, grad_up).astype(BF16)
    wide = jnp.concatenate([embedding, embedding], axis=1)
    wide = jnp.concatenate([jnp.zeros((8, 128), F32), wide] * n_dev, axis=0)
    i, j = spread_index((n_dev * SLOT_ROWS, 128))
    codes = jnp.where(j < 96, shift_rows(directions, 8), directions)
    codes = jnp.where((i & 8) == 8, codes, 0.0)
    small = dot_tn(hot_target, small) + jnp.where(j < 64, wide, codes)
    small_out[...] = small.astype(BF16).reshape(n_dev, SLOT_ROWS, 128)
    small_in[dev] = small_out[dev]

    entry_wait()
    exchange(lambda p: small_out.at[p], small_in.at[dev], 0, "dev")
    exchange(lambda p: layer_out.at[p], layer_in.at[dev], 2, "dev")

    z_first, z_last = z_table(active, y_mask, select_x)
    table[512:576, :] = z_first
    table[576:640, :] = z_last
    face_out[...] = (
        dot_tn(hot_out[...], table[...]).astype(BF16).reshape(n_dev, SLOT_ROWS, LANES)
    )
    face_in[dev] = face_out[dev]

    i, j = spread_index((64, LANES))
    wide = dot(fine_weight_ref[...].reshape(448, 64), one_hot(i == (j & 63)))
    weight_ref[...] = wide
    i, j = spread_index((256, 256))
    block = (i >> 6) == (j >> 6)
    for k in range(6):
        piece = weight_ref[64 * (k + 1) : 64 * (k + 2), 0:256]
        band_ref[256 * k : 256 * (k + 1), :] = jnp.where(
            block, jnp.concatenate([piece] * 4, axis=0), 0.0
        ).astype(BF16)
    z_step = (lane >> 6) - (row >> 6)
    middle = jnp.where(
        z_step == 0,
        jnp.concatenate([weight_ref[0:64, :]] * 8, axis=0),
        jnp.where(
            z_step == 1,
            jnp.concatenate([weight_ref[320:384, :]] * 8, axis=0),
            jnp.where(
                z_step == -1, jnp.concatenate([weight_ref[384:448, :]] * 8, axis=0), 0.0
            ),
        ),
    ).astype(BF16)

    def times_band(v, k):
        band = band_ref[256 * k : 256 * (k + 1), :]
        return jnp.concatenate([dot_nt(v[:, 0:256], band), dot_nt(v[:, 256:512], band)], axis=1)

    rim = jnp.concatenate([times_band(layers[k], k).astype(BF16) for k in range(6)], axis=0)

    x_at, y_at = (row >> 3) & 7, row & 7

    def shifted(v, k, edge):
        amount, at, end = ((8, x_at, 0), (-8, x_at, 7), (1, y_at, 0), (-1, y_at, 7))[k]
        return jnp.where(at == end, edge, shift_rows(v, amount))

    total = dot_nt(grad_b, middle)
    left, right = total[:, 0:256], total[:, 256:512]
    for k in range(4):
        moved = shifted(grad, k ^ 1, 0.0).astype(BF16)
        band = band_ref[256 * k : 256 * (k + 1), :]
        left = left + dot_nt(moved[:, 0:256], band)
        right = right + dot_nt(moved[:, 256:512], band)
    total = jnp.concatenate([left, right], axis=1)
    total = total + dot(hot_halo[0:512, :], rim)
    z_rows = dot(hot_halo[512:640, :], rim)
    grad_ref[...] = total

    active_f = active.astype(F32)
    halo = dot_tn(hot_halo[0:640, :], table[...]).astype(BF16)
    grad_t = grad.T.astype(BF16)
    center = dot(grad_t, active)
    conv = dot(active, middle)
    left, right = conv[:, 0:256], conv[:, 256:512]
    tap_grads = [diagonal_sum(center, 0, 0, 8)]
    for k in range(4):
        repeat = repeat_x if k < 2 else repeat_y
        moved = shifted(active_f, k, dot(repeat, halo[64 * k : 64 * k + 64])).astype(BF16)
        band = band_ref[256 * k : 256 * (k + 1), :]
        left = left + dot(moved[:, 0:256], band)
        right = right + dot(moved[:, 256:512], band)
        tap_grads.append(
            diagonal_sum(dot(grad_t[0:256], moved[:, 0:256]), 0, 0, 4)
            + diagonal_sum(dot(grad_t[256:512], moved[:, 256:512]), 0, 0, 4)
        )
    low_z = jnp.where(y_mask, dot(repeat_y, halo[256:320]), 0.0).astype(BF16)
    high_z = jnp.where(y_mask, dot(repeat_y, halo[320:384]), 0.0).astype(BF16)
    end = jnp.where(low_half, weight_ref[320:384, 0:128], 0.0).astype(BF16)
    first = dot(low_z, jnp.concatenate([end] * 8, axis=0))
    end = jnp.where(low_half, 0.0, weight_ref[384:448, 0:128]).astype(BF16)
    last = dot(high_z, jnp.concatenate([end] * 8, axis=0))
    conv_ref[...] = jnp.concatenate(
        [left[:, 0:128] + first, left[:, 128:256], right[:, 0:128], right[:, 128:256] + last],
        axis=1,
    )
    tap_grads.append(diagonal_sum(center, 0, -1, 8) + fold_lanes(dot(grad_t[0:64], low_z)))
    tap_grads.append(diagonal_sum(center, 0, 1, 8) + fold_lanes(dot(grad_t[448:512], high_z)))

    place = exact_dot(places_ref[...].astype(F32), spread_slot)
    j = iota((1, n_dev * SLOT_ROWS), 1)
    place_code = (place * 8 + (j & 7).astype(F32)).astype(jnp.int32)
    i = iota((ROWS, 1), 0)
    voxel_code = (
        ((i >> 7) * 16 + ((i >> 4) & 3) * 4 + ((i >> 1) & 3)) * 8
        + ((i >> 6) & 1) * 4
        + ((i >> 3) & 1) * 2
        + (i & 1)
    )
    first_kind = (j & 8) == 0
    hot_place = one_hot(voxel_code == jnp.where(first_kind, place_code, -1))
    hot_place_grad = one_hot(voxel_code == jnp.where(first_kind, -1, place_code))
    wait_arrived(others(small_in, n_dev), 0, "dev")
    grid = dot(hot_place, small_in[...].reshape(n_dev * SLOT_ROWS, 128)).astype(BF16)
    down = jnp.concatenate([down_weight_ref[...], jnp.zeros((64, 128), BF16)], axis=0)
    up = jnp.concatenate([jnp.zeros((64, 128), BF16), up_weight_ref[...]], axis=0)
    coarse_pre = dot(grid, down)
    coarse_sig = 1.0 / (1.0 + jnp.exp(-coarse_pre))
    coarse_act = coarse_pre * coarse_sig
    row_c = iota((ROWS, 128), 0)
    at_c = (row_c >> 6, (row_c >> 3) & 7, row_c & 7)

    def coarse_shifted(v, k):
        amount = (64, -64, 8, -8, 1, -1)[k]
        return jnp.where(at_c[k // 2] == 7 * (k % 2), 0.0, shift_rows(v, amount))

    coarse_act_f = coarse_act.astype(BF16).astype(F32)
    stack = jnp.concatenate(
        [coarse_act_f.astype(BF16)]
        + [coarse_shifted(coarse_act_f, k).astype(BF16) for k in range(6)],
        axis=1,
    )
    coarse_out = dot(stack, coarse_weight_ref[...].reshape(896, 128)).astype(BF16)
    grad_out = dot(grid, up)
    grad_out_b = grad_out.astype(BF16)
    grad_act = dot_nt(grad_out_b, coarse_weight_ref[0])
    for k in range(6):
        grad_act = grad_act + dot_nt(
            coarse_shifted(grad_out, k ^ 1).astype(BF16), coarse_weight_ref[k + 1]
        )
    grad_pre = grad_act * coarse_sig * (1.0 + coarse_pre * (1.0 - coarse_sig))
    grad_pre = grad_pre.astype(BF16)
    grad_pooled = dot_nt(grad_pre, down).astype(BF16)
    back_out[...] = (
        (dot_tn(hot_place, coarse_out) + dot_tn(hot_place_grad, grad_pooled))
        .astype(BF16)
        .reshape(n_dev, SLOT_ROWS, 128)
    )
    back_in[dev] = back_out[dev]
    exchange(lambda p: back_out.at[p], back_in.at[dev], 3, "dev")

    coarse_grad = dot_tn(stack, grad_out_b)
    down_grad = dot_tn(grid, grad_pre)
    up_grad = dot_tn(grid, coarse_out)
    part = jnp.concatenate([coarse_grad, down_grad[0:64], up_grad[64:128]], axis=0)
    coarse_part[...] = part.astype(BF16).reshape(2 * n_grp, coarse_chunk, 128)
    plane = rings["plane"][0]
    coarse_in[plane] = coarse_part[plane]
    exchange(lambda p: coarse_part.at[p], coarse_in.at[plane], 4, "plane")

    exchange(lambda p: face_out.at[p], face_in.at[dev], 1, "dev")

    marks = small_in[...].reshape(n_dev * SLOT_ROWS, 128).astype(F32)
    odd_slot = (iota((n_dev * SLOT_ROWS, 1), 0) & 8) == 8
    way = jnp.where(odd_slot, marks[:, 96:97], shift_rows(marks, -8)[:, 64:65])
    way_row = jnp.broadcast_to(way, (n_dev * SLOT_ROWS, 128)).T[0:1]
    faces_t = face_out[...].reshape(n_dev * SLOT_ROWS, LANES).astype(F32).T
    for k in range(6):
        own_faces[LANES * k : LANES * (k + 1), :] = jnp.where(
            way_row == float(k), faces_t, 0.0
        ).astype(BF16)
    tap_grads = [jnp.concatenate([t, t], axis=0).T[0:64] for t in tap_grads]
    wait_arrived(others(layer_in, n_dev), 2, "dev")
    came = layer_in[...].reshape(n_dev * SLOT_ROWS, LANES)
    for k in range(6):
        base = LANES * k
        tap_grads[k + 1] = (
            tap_grads[k + 1]
            + diagonal_sum(dot(own_faces[base : base + 256, :], came[:, 0:256]), 0, 0, 4)
            + diagonal_sum(dot(own_faces[base + 256 : base + 512, :], came[:, 256:512]), 0, 0, 4)
        )
    fine_rows = []
    for t in range(4):
        high = pltpu.roll(tap_grads[t + 4], 64, 1) if t < 3 else 0.0
        fine_rows.append(jnp.where(low_half, tap_grads[t], high))
    part = jnp.concatenate(fine_rows, axis=0)
    fine_out[...] = part.astype(BF16).reshape(n_grp, FINE_ROWS // n_grp, 128)
    fine_in[grp] = fine_out[grp]
    exchange(lambda p: fine_out.at[p], fine_in.at[grp], 7, "grp")

    rim_back = times_band(came, 0)
    for k in range(1, 6):
        rim_back = jnp.where(way == float(k), times_band(came, k), rim_back)
    rim_back = rim_back.astype(BF16)
    total = grad_ref[...] + dot(hot_out[0:512, :], rim_back)
    z_rows = (z_rows + dot(hot_out[512:640, :], rim_back)).astype(BF16)
    low_rows = lane[:, 0:128] < 64
    first = fold_lanes(jnp.where(y_mask, dot(repeat_y, z_rows[0:64]), 0.0))
    last = fold_lanes(jnp.where(y_mask, dot(repeat_y, z_rows[64:128]), 0.0))
    grad_ref[...] = jnp.concatenate(
        [
            total[:, 0:128] + jnp.where(low_rows, first, 0.0),
            total[:, 128:384],
            total[:, 384:512] + jnp.where(low_rows, 0.0, last),
        ],
        axis=1,
    )

    wait_arrived(others(coarse_in, 2 * n_grp), 4, "plane")
    part = coarse_in[0].astype(F32)
    for p in range(1, 2 * n_grp):
        part = part + coarse_in[p].astype(F32)
    coarse_mid[chip] = part.astype(BF16)
    exchange(lambda p: coarse_mid.at[chip], coarse_mid.at[chip], 5, "chip")

    wait_arrived(others(back_in, n_dev), 3, "dev")
    back = back_in[...].reshape(n_dev * SLOT_ROWS, 128)
    back_grad = dot(hot_target_grad, back).astype(BF16)
    i, j = spread_index((128, LANES))
    back_wide = jnp.where(half_mask, dot(back_grad, one_hot(i == (j & 63))), 0.0)
    total = grad_ref[...] + dot(unpool, (back_wide * (1.0 / 64.0)).astype(BF16))
    normed = normed_ref[...]
    grad_before = total * slope_ref[...]
    grad_ref[...] = grad_before
    grad_scale = fold_lanes(brick_sum(grad_before * normed))
    grad_shift = fold_lanes(brick_sum(grad_before))
    brick_all[dev] = jnp.where(low_b, grad_scale, grad_shift)
    exchange(lambda p: brick_all.at[dev], brick_all.at[dev], 9, "dev")

    wait_arrived(others(fine_in, n_grp), 7, "grp")
    part = fine_in[0].astype(F32)
    for p in range(1, n_grp):
        part = part + fine_in[p].astype(F32)
    fine_mid[dev] = part.astype(BF16)
    exchange(lambda p: fine_mid.at[dev], fine_mid.at[dev], 8, "dev")

    grad_before = grad_ref[...]
    g3 = grad_before.reshape(BRICKS, 64, LANES) * per_brick(gain)
    n3 = normed_ref[...].reshape(BRICKS, 64, LANES)
    mean_g = group_mean(jnp.sum(g3, axis=1))
    mean_gn = group_mean(jnp.sum(g3 * n3, axis=1))
    result = per_brick(inverse) * (g3 - per_brick(mean_g) - n3 * per_brick(mean_gn))
    grad = cotangent_ref[...].astype(F32).reshape(ROWS, LANES)
    result = grad + result.reshape(ROWS, LANES)
    input_grad_held[...] = result.reshape(BRICKS, 8, 8, LANES).astype(BF16)
    input_grad_copy = pltpu.make_async_copy(input_grad_held, input_grad_ref, copy_sems.at[1])
    input_grad_copy.start()

    wait_arrived(others(coarse_mid, n_chip), 5, "chip")
    part = coarse_mid[0].astype(F32)
    for p in range(1, n_chip):
        part = part + coarse_mid[p].astype(F32)
    coarse_all[plane] = part.astype(BF16)
    exchange(lambda p: coarse_all.at[plane], coarse_all.at[plane], 6, "plane")

    coarse_values = dot(hot_target, back).astype(BF16)
    i, j = spread_index((64, LANES))
    up_wide = dot_tn(up_weight_ref[...], one_hot(i == (j & 63))).astype(BF16)
    upward = jnp.where(half_mask, dot(coarse_values, up_wide), 0.0)
    upward_high = upward.astype(BF16)
    upward_low = (upward - upward_high.astype(F32)).astype(BF16)
    upward = dot(unpool, upward_high) + dot(unpool, upward_low)
    features = features_ref[...].astype(F32).reshape(ROWS, LANES)
    conv_ref[...] = features + conv_ref[...] + upward
    i, j = spread_index((ROWS, 256))
    x, y = (i >> 3) & 7, i & 7
    by_x = (j & 63) == ((i >> 6) * 8 + y)
    by_y = (j & 63) == (i >> 3)
    way = j >> 6
    edges = one_hot(
        ((way == 0) & (x == 0) & by_x)
        | ((way == 1) & (x == 7) & by_x)
        | ((way == 2) & (y == 0) & by_y)
        | ((way == 3) & (y == 7) & by_y)
    )

    wait_arrived(others(brick_all, n_dev), 9, "dev")
    embeddings = small_in[...].astype(F32)[:, 8:16, :].reshape(n_dev * BRICKS, 128)
    time_grad = lax.dot_general(
        embeddings,
        brick_all[...].reshape(n_dev * BRICKS, 128),
        (((0,), (0,)), ((), ())),
        precision=lax.Precision.HIGHEST,
        preferred_element_type=F32,
    )
    time_all[grp] = time_grad[0:64].astype(BF16)
    exchange(lambda p: time_all.at[grp], time_all.at[grp], 11, "grp")

    wait_arrived(others(fine_mid, n_dev), 8, "dev")
    part = fine_mid[0].astype(F32)
    for p in range(1, n_dev):
        part = part + fine_mid[p].astype(F32)
    fine_all[grp] = part.astype(BF16)
    exchange(lambda p: fine_all.at[grp], fine_all.at[grp], 10, "grp")

    wait_arrived(others(face_in, n_dev), 1, "dev")
    halo = dot_tn(hot_halo[640 : 640 + n_dev * SLOT_ROWS, :], face_in[...].reshape(-1, LANES))
    halo = halo.astype(BF16)
    sides = []
    for k in range(6):
        band = band_ref[256 * k : 256 * (k + 1), :]
        piece = halo[64 * k : 64 * k + 64]
        sides.append(
            jnp.concatenate([dot(piece[:, 0:256], band), dot(piece[:, 256:512], band)], axis=1)
            .astype(BF16)
        )
    mixed = conv_ref[...] + dot(edges, jnp.concatenate(sides[0:4], axis=0))
    first = fold_lanes(jnp.where(y_mask, dot(repeat_y, sides[4]), 0.0))
    last = fold_lanes(jnp.where(y_mask, dot(repeat_y, sides[5]), 0.0))
    mixed = jnp.concatenate(
        [
            mixed[:, 0:128] + jnp.where(low_rows, first, 0.0),
            mixed[:, 128:384],
            mixed[:, 384:512] + jnp.where(low_rows, 0.0, last),
        ],
        axis=1,
    )
    mixed_held[...] = mixed.reshape(BRICKS, 8, 8, LANES).astype(BF16)
    mixed_copy = pltpu.make_async_copy(mixed_held, mixed_ref, copy_sems.at[0])
    mixed_copy.start()

    wait_arrived(others(coarse_all, 2 * n_grp), 6, "plane")
    coarse_sum_ref[...] = coarse_all[...].reshape(COARSE_ROWS, 128)
    wait_arrived(others(fine_all, n_grp), 10, "grp")
    fine_sum_ref[...] = fine_all[...].reshape(FINE_ROWS, 128)
    wait_arrived(others(time_all, n_grp), 11, "grp")
    part = time_all[0].astype(F32)
    for p in range(1, n_grp):
        part = part + time_all[p].astype(F32)
    time_sum_ref[...] = part

    wait_sent(others(small_out, n_dev), 0, "dev")
    wait_sent(others(face_out, n_dev), 1, "dev")
    wait_sent(others(layer_out, n_dev), 2, "dev")
    wait_sent(others(back_out, n_dev), 3, "dev")
    wait_sent(others(coarse_part, 2 * n_grp), 4, "plane")
    wait_sent(others(coarse_mid, n_chip), 5, "chip")
    wait_sent(others(coarse_all, 2 * n_grp), 6, "plane")
    wait_sent(others(fine_out, n_grp), 7, "grp")
    wait_sent(others(fine_mid, n_dev), 8, "dev")
    wait_sent(others(brick_all, n_dev), 9, "dev")
    wait_sent(others(fine_all, n_grp), 10, "grp")
    wait_sent(others(time_all, n_grp), 11, "grp")
    mixed_copy.wait()
    input_grad_copy.wait()


def finish(
    mixed_in,
    input_grad_in,
    coarse_sum_ref,
    fine_sum_ref,
    time_sum_ref,
    mixed_ref,
    input_grad_ref,
    fine_grad_ref,
    down_grad_ref,
    coarse_grad_ref,
    up_grad_ref,
    time_grad_ref,
):
    mixed_ref[...] = mixed_in[...]
    input_grad_ref[...] = input_grad_in[...]
    coarse_grad_ref[...] = coarse_sum_ref[0:896, :].astype(F32).reshape(7, 128, 128)
    down_grad_ref[...] = coarse_sum_ref[896:960, :].astype(F32)
    up_grad_ref[...] = coarse_sum_ref[960:1024, :].astype(F32)
    for t in range(4):
        piece = fine_sum_ref[64 * t : 64 * t + 64, :].astype(F32)
        fine_grad_ref[t] = piece[:, 0:64]
        if t < 3:
            fine_grad_ref[t + 4] = pltpu.roll(piece, 64, 1)[:, 0:64]
    time_grad_ref[...] = time_sum_ref[...]


def body(n_grp, n_dev, *args):
    half = 32
    frequency = np.exp(-math.log(10000.0) * np.arange(half) / half).astype(np.float32)
    frequency = jnp.asarray(np.concatenate([frequency, frequency])[None, :])
    args = list(args)
    args[4] = jnp.swapaxes(args[4], 1, 2)
    args[6] = args[6].reshape(1, n_dev)
    args[11] = args[11].T
    args.append(frequency)
    vmem = pl.BlockSpec(memory_space=pltpu.VMEM)
    free = pl.BlockSpec(memory_space=pl.ANY)
    packed = jax.ShapeDtypeStruct((BRICKS, 8, 8, LANES), BF16)
    slots = (n_dev, SLOT_ROWS)
    coarse_chunk = COARSE_ROWS // 2 // n_grp
    fine_chunk = FINE_ROWS // n_grp
    held = pl.pallas_call(
        functools.partial(kernel, n_grp, n_dev),
        out_shape=(
            packed,
            packed,
            jax.ShapeDtypeStruct((COARSE_ROWS, 128), BF16),
            jax.ShapeDtypeStruct((FINE_ROWS, 128), BF16),
            jax.ShapeDtypeStruct((64, 128), F32),
        ),
        in_specs=[free] * 13,
        out_specs=(free, free, vmem, vmem, vmem),
        scratch_shapes=[
            pltpu.VMEM(slots + (128,), BF16),
            pltpu.VMEM(slots + (128,), BF16),
            pltpu.VMEM(slots + (LANES,), BF16),
            pltpu.VMEM(slots + (LANES,), BF16),
            pltpu.VMEM(slots + (LANES,), BF16),
            pltpu.VMEM(slots + (LANES,), BF16),
            pltpu.VMEM(slots + (128,), BF16),
            pltpu.VMEM(slots + (128,), BF16),
            pltpu.VMEM((2 * n_grp, coarse_chunk, 128), BF16),
            pltpu.VMEM((2 * n_grp, coarse_chunk, 128), BF16),
            pltpu.VMEM((n_dev // 2, coarse_chunk, 128), BF16),
            pltpu.VMEM((2 * n_grp, coarse_chunk, 128), BF16),
            pltpu.VMEM((n_grp, fine_chunk, 128), BF16),
            pltpu.VMEM((n_grp, fine_chunk, 128), BF16),
            pltpu.VMEM((n_dev, fine_chunk, 128), BF16),
            pltpu.VMEM((n_grp, fine_chunk, 128), BF16),
            pltpu.VMEM((n_dev, BRICKS, 128), F32),
            pltpu.VMEM((n_grp, 64, 128), BF16),
            pltpu.VMEM((BRICKS, 8, 8, LANES), BF16),
            pltpu.VMEM((BRICKS, 8, 8, LANES), BF16),
            pltpu.VMEM((6 * LANES, n_dev * SLOT_ROWS), BF16),
            pltpu.VMEM((640 + n_dev * SLOT_ROWS, 384), BF16),
            pltpu.VMEM((640, n_dev * SLOT_ROWS), BF16),
            pltpu.VMEM((640, LANES), BF16),
            pltpu.VMEM((ROWS, LANES), F32),
            pltpu.VMEM((ROWS, LANES), F32),
            pltpu.VMEM((ROWS, LANES), F32),
            pltpu.VMEM((ROWS, LANES), F32),
            pltpu.VMEM((448, LANES), F32),
            pltpu.VMEM((1536, 256), BF16),
            pltpu.SemaphoreType.DMA((12,)),
            pltpu.SemaphoreType.DMA((12,)),
            pltpu.SemaphoreType.DMA((2,)),
        ]
        + [pltpu.VMEM(a.shape, a.dtype) for a in args]
        + [pltpu.SemaphoreType.DMA((13,))],
        compiler_params=pltpu.CompilerParams(
            collective_id=0, has_side_effects=True, vmem_limit_bytes=56 * 1024 * 1024
        ),
    )(*args)
    outs = pl.pallas_call(
        finish,
        out_shape=(
            packed,
            packed,
            jax.ShapeDtypeStruct((7, 64, 64), F32),
            jax.ShapeDtypeStruct((64, 128), F32),
            jax.ShapeDtypeStruct((7, 128, 128), F32),
            jax.ShapeDtypeStruct((64, 128), F32),
            jax.ShapeDtypeStruct((64, 128), F32),
        ),
        in_specs=[vmem] * 5,
        out_specs=(vmem,) * 7,
        compiler_params=pltpu.CompilerParams(vmem_limit_bytes=56 * 1024 * 1024),
    )(*held)
    return outs[0], outs[1], outs[2], outs[3], outs[4], outs[5].T, outs[6]


def solution(mesh):
    split = ("grp", "dev")
    in_specs = (
        P(split, None, None, None),
        P(split, None, None, None),
        P(split),
        P(split, None),
        P(split, None, None),
        P(split),
        P(split, None, None),
        P(),
        P(),
        P(),
        P(),
        P(),
    )
    out_specs = (
        P(split, None, None, None),
        P(split, None, None, None),
        P(),
        P(),
        P(),
        P(),
        P(),
    )
    return jax.shard_map(
        functools.partial(body, mesh.shape["grp"], mesh.shape["dev"]),
        mesh=mesh,
        in_specs=in_specs,
        out_specs=out_specs,
        check_vma=False,
    )
```

```python
import functools
import math

import jax
import jax.numpy as jnp
import numpy as np
from jax import lax
from jax.experimental import pallas as pl
from jax.experimental.pallas import tpu as pltpu
from jax.sharding import PartitionSpec as P

EPSILON = 1e-05
F32 = jnp.float32
BF16 = jnp.bfloat16
BRICKS = 8
ROWS = 512
LANES = 512
SLOT_ROWS = 16
COARSE_ROWS = 1024
FINE_ROWS = 256


def iota(shape, axis):
    return lax.broadcasted_iota(jnp.int32, shape, axis)


def dot(a, b):
    return jnp.dot(a, b, preferred_element_type=F32)


def dot_nt(a, b):
    return lax.dot_general(a, b, (((1,), (1,)), ((), ())), preferred_element_type=F32)


def dot_tn(a, b):
    return lax.dot_general(a, b, (((0,), (0,)), ((), ())), preferred_element_type=F32)


def exact_dot(a, b):
    return jnp.dot(a, b, precision=lax.Precision.HIGHEST, preferred_element_type=F32)


def one_hot(condition):
    return jnp.where(condition, 1.0, 0.0).astype(BF16)


def lanes_four(v):
    return jnp.concatenate([v, v, v, v], axis=1)


def fold_lanes(v):
    s = (v[:, 0:128] + v[:, 128:256]) + (v[:, 256:384] + v[:, 384:512])
    return s + pltpu.roll(s, 64, 1)


def group_mean(sums):
    s = fold_lanes(sums)
    lane = iota(s.shape, 1)
    pair = jnp.where((lane & 1) == 0, pltpu.roll(s, 127, 1), pltpu.roll(s, 1, 1))
    return lanes_four((s + pair) * (1.0 / 1024.0))


def brick_sum(v):
    return jnp.sum(v.reshape(BRICKS, 64, LANES), axis=1)


def per_brick(v):
    return v[:, None, :]


def face_index(brick, side, r):
    base = brick * 64
    xy = jnp.where(
        side < 0.5,
        base + r,
        jnp.where(
            side < 1.5,
            base + 56 + r,
            jnp.where(side < 2.5, base + 8 * r, base + 8 * r + 7),
        ),
    )
    zz = 512 + brick * 8 + r + jnp.where(side > 4.5, 64, 0)
    return jnp.where(side < 3.5, xy, zz)


def shift_rows(v, amount):
    return pltpu.roll(v, amount % v.shape[0], 0)


def z_table(v, mask, select):
    i, j = iota((128, LANES), 0), iota((128, LANES), 1)
    low = one_hot(i == (j & 63))
    high = one_hot(i - 64 == (j & 63))
    first = jnp.where(mask, dot(v[:, 0:128], low), 0.0).astype(BF16)
    last = jnp.where(mask, dot(v[:, 384:512], high), 0.0).astype(BF16)
    return dot(select, first).astype(BF16), dot(select, last).astype(BF16)


def diagonal_sum(blocks, low_shift, high_shift, count):
    even = odd = None
    for z in range(count):
        zr, zc = z + low_shift, z + high_shift
        if not (0 <= zr < count and 0 <= zc < count):
            continue
        piece = blocks[64 * zr : 64 * zr + 64, 128 * (zc // 2) : 128 * (zc // 2) + 128]
        if zc % 2 == 0:
            even = piece if even is None else even + piece
        else:
            odd = piece if odd is None else odd + piece
    return even + pltpu.roll(odd, 64, 1)


def kernel(
    n_grp,
    n_dev,
    features_far,
    cotangent_far,
    steps_far,
    links_far,
    sources_far,
    targets_far,
    places_far,
    time_weight_far,
    fine_weight_far,
    down_weight_far,
    coarse_weight_far,
    up_weight_far,
    frequency_far,
    mixed_ref,
    input_grad_ref,
    coarse_sum_ref,
    fine_sum_ref,
    time_sum_ref,
    small_out,
    small_in,
    face_out,
    face_in,
    layer_out,
    layer_in,
    back_out,
    back_in,
    coarse_part,
    coarse_in,
    coarse_mid,
    coarse_all,
    fine_out,
    fine_in,
    fine_mid,
    fine_all,
    brick_all,
    time_all,
    mixed_held,
    input_grad_held,
    own_faces,
    hot_halo,
    hot_out,
    table,
    normed_ref,
    slope_ref,
    conv_ref,
    grad_ref,
    weight_ref,
    band_ref,
    send_sems,
    recv_sems,
    copy_sems,
    features_ref,
    cotangent_ref,
    steps_ref,
    links_ref,
    sources_ref,
    targets_ref,
    places_ref,
    time_weight_ref,
    fine_weight_ref,
    down_weight_ref,
    coarse_weight_ref,
    up_weight_ref,
    frequency_ref,
    load_sems,
):
    grp = lax.axis_index("grp")
    dev = lax.axis_index("dev")
    chip = dev // 2
    core = dev % 2
    n_chip = n_dev // 2
    coarse_chunk = COARSE_ROWS // 2 // n_grp

    rings = {
        "dev": (dev, n_dev, lambda p: (grp, p)),
        "chip": (chip, n_chip, lambda p: (grp, 2 * p + core)),
        "grp": (grp, n_grp, lambda p: (p, dev)),
        "cross": (grp, n_grp, lambda p: (p, 2 * chip + 1 - core)),
        "plane": (2 * grp + core, 2 * n_grp, lambda p: (p // 2, 2 * chip + p % 2)),
    }

    def device_at(along, p):
        grp_at, dev_at = rings[along][2](p)
        return {"grp": grp_at, "dev": dev_at}

    def entry_signal():
        barrier = pltpu.get_barrier_semaphore()
        for along in ("dev", "grp", "cross"):
            me, count, _ = rings[along]

            def step(j, carry, along=along, me=me, count=count):
                pl.semaphore_signal(
                    barrier,
                    inc=1,
                    device_id=device_at(along, lax.rem(me + j, count)),
                    device_id_type=pl.DeviceIdType.MESH,
                )
                return carry

            lax.fori_loop(1, count, step, 0)

    def entry_wait():
        pl.semaphore_wait(pltpu.get_barrier_semaphore(), n_dev - 1 + 2 * (n_grp - 1))

    def remote(src, dst, index, along, p):
        return pltpu.make_async_remote_copy(
            src_ref=src,
            dst_ref=dst,
            send_sem=send_sems.at[index],
            recv_sem=recv_sems.at[index],
            device_id=device_at(along, p),
            device_id_type=pl.DeviceIdType.MESH,
        )

    def exchange(src, dst, index, along):
        me, count, _ = rings[along]

        def step(j, carry):
            p = lax.rem(me + j, count)
            remote(src(p), dst, index, along, p).start()
            return carry

        lax.fori_loop(1, count, step, 0)

    def wait_arrived(part, index, along):
        me, count, _ = rings[along]
        if count > 1:
            remote(part, part, index, along, lax.rem(me + 1, count)).wait_recv()

    def wait_sent(part, index, along):
        me, count, _ = rings[along]
        if count > 1:
            remote(part, part, index, along, lax.rem(me + 1, count)).wait_send()

    def others(ref, count):
        return ref.at[pl.ds(0, max(count - 1, 1))]

    loads = [
        pltpu.make_async_copy(far, near, load_sems.at[index])
        for index, (far, near) in enumerate(
            (
                (features_far, features_ref),
                (cotangent_far, cotangent_ref),
                (steps_far, steps_ref),
                (links_far, links_ref),
                (sources_far, sources_ref),
                (targets_far, targets_ref),
                (places_far, places_ref),
                (time_weight_far, time_weight_ref),
                (fine_weight_far, fine_weight_ref),
                (down_weight_far, down_weight_ref),
                (coarse_weight_far, coarse_weight_ref),
                (up_weight_far, up_weight_ref),
                (frequency_far, frequency_ref),
            )
        )
    ]
    for load in loads:
        load.start()
    entry_signal()
    for load in loads:
        load.wait()

    row = iota((ROWS, LANES), 0)
    lane = iota((ROWS, LANES), 1)
    y_mask = (lane >> 6) == (row & 7)

    def spread_index(shape):
        return iota(shape, 0), iota(shape, 1)

    i, j = spread_index((n_dev, n_dev * SLOT_ROWS))
    by_slot = (j >> 4) == i
    spread_slot = jnp.where(by_slot, 1.0, 0.0)
    sources = exact_dot(sources_ref[0].astype(F32), spread_slot)
    j = iota((1, n_dev * SLOT_ROWS), 1)
    code = jnp.where(((j >> 3) & 1) == 0, sources[0:1], sources[1:2])
    brick = jnp.zeros_like(code)
    for m in range(1, BRICKS):
        brick = brick + jnp.where(code > 6.0 * m - 0.5, 1.0, 0.0)
    r = (iota(code.shape, 1) & 7).astype(F32)
    out_index = jnp.where(code < -0.5, -1.0, face_index(brick, code - 6.0 * brick, r))
    out_index = out_index.astype(jnp.int32)
    hot_out[...] = one_hot(iota((640, n_dev * SLOT_ROWS), 0) == out_index)

    i, j = spread_index((BRICKS, 384))
    links = links_ref[...].astype(F32)
    link = jnp.zeros((BRICKS, 384), F32)
    for k in range(6):
        link = link + jnp.where((j >> 6) == k, links[:, k : k + 1], 0.0)
    link = jnp.sum(jnp.where(((j >> 3) & 7) == i, link, 0.0), axis=0, keepdims=True)
    k_row = iota((1, 384), 1) >> 6
    side = (k_row + 1 - 2 * (k_row & 1)).astype(F32)
    r = (iota((1, 384), 1) & 7).astype(F32)
    halo_index = jnp.where(
        link < -0.5,
        -1.0,
        jnp.where(link < 7.5, face_index(link, side, r), 640 + (link - 8.0) * 8 + r),
    ).astype(jnp.int32)
    hot_halo[...] = one_hot(iota((640 + n_dev * SLOT_ROWS, 384), 0) == halo_index)

    i, j = spread_index((64, BRICKS))
    targets = targets_ref[...].astype(F32).reshape(1, BRICKS)
    target = jnp.sum(jnp.where((i >> 3) == j, targets, 0.0), axis=1, keepdims=True)
    child = (iota((64, 1), 0) & 7).astype(F32)
    target_code = (target * 16 + child).astype(jnp.int32)
    slot_lane = iota((64, n_dev * SLOT_ROWS), 1)
    hot_target = one_hot(slot_lane == target_code)
    hot_target_grad = one_hot(slot_lane == target_code + 8)

    i, j = spread_index((64, ROWS))
    pool = one_hot(
        ((i >> 3) == (j >> 6))
        & (((i >> 2) & 1) == ((j >> 5) & 1))
        & (((i >> 1) & 1) == ((j >> 2) & 1))
    )
    i, j = spread_index((64, LANES))
    half_mask = (i & 1) == (j >> 8)
    select_x = one_hot(i == (j >> 3))
    i, j = spread_index((ROWS, 64))
    unpool = one_hot(
        ((j >> 3) == (i >> 6))
        & (((j >> 2) & 1) == ((i >> 5) & 1))
        & (((j >> 1) & 1) == ((i >> 2) & 1))
    )
    repeat_y = one_hot(j == (i >> 3))
    repeat_x = one_hot(j == ((i >> 6) * 8 + (i & 7)))
    low_half = iota((64, 128), 1) < 64

    grad = cotangent_ref[...].astype(F32)
    grad_b = grad.astype(BF16)
    i, j = spread_index((64, ROWS))
    g4 = grad.reshape(BRICKS, 8, 8, LANES)
    grad_z = z_table(grad_b, y_mask, select_x)
    layers = [
        g4[:, 0].reshape(64, LANES).astype(BF16),
        g4[:, 7].reshape(64, LANES).astype(BF16),
        dot(one_hot(j == i * 8), grad_b).astype(BF16),
        dot(one_hot(j == i * 8 + 7), grad_b).astype(BF16),
        grad_z[0],
        grad_z[1],
    ]
    hot_slots = hot_halo[640 : 640 + n_dev * SLOT_ROWS, :]
    layer_out[...] = (
        dot(hot_slots, jnp.concatenate(layers, axis=0))
        .astype(BF16)
        .reshape(n_dev, SLOT_ROWS, LANES)
    )
    layer_in[dev] = layer_out[dev]
    directions = dot(hot_slots, (iota((384, 128), 0) >> 6).astype(F32).astype(BF16))

    features = features_ref[...].astype(F32)
    f3 = features.reshape(BRICKS, 64, LANES)
    centred = f3 - per_brick(group_mean(jnp.sum(f3, axis=1)))
    variance = group_mean(jnp.sum(centred * centred, axis=1))
    inverse = lax.rsqrt(variance + EPSILON)
    normed = (centred * per_brick(inverse)).reshape(ROWS, LANES)
    normed_ref[...] = normed
    i, j = spread_index((BRICKS, BRICKS))
    steps = steps_ref[...].astype(F32).reshape(1, BRICKS)
    step_column = jnp.sum(jnp.where(i == j, steps, 0.0), axis=1, keepdims=True)
    angles = step_column * frequency_ref[...]
    embedding = jnp.where(iota((BRICKS, 64), 1) < 32, jnp.cos(angles), jnp.sin(angles))
    modulate = exact_dot(embedding, time_weight_ref[...])
    swapped = pltpu.roll(modulate, 64, 1)
    low_b = iota((BRICKS, 128), 1) < 64
    scale = lanes_four(jnp.where(low_b, modulate, swapped))
    shift = lanes_four(jnp.where(low_b, swapped, modulate))
    gain = 1.0 + scale
    before = (
        normed.reshape(BRICKS, 64, LANES) * per_brick(gain) + per_brick(shift)
    ).reshape(ROWS, LANES)
    sigmoid = 1.0 / (1.0 + jnp.exp(-before))
    slope_ref[...] = sigmoid * (1.0 + before * (1.0 - sigmoid))
    active = (before * sigmoid).astype(BF16)
    table[0:512, :] = active

    pooled = fold_lanes(jnp.where(half_mask, dot(pool, active), 0.0)) * (1.0 / 64.0)
    grad_up = fold_lanes(jnp.where(half_mask, dot(pool, grad_b), 0.0))
    small = jnp.where(low_half, pooled, grad_up).astype(BF16)
    wide = jnp.concatenate([embedding, embedding], axis=1)
    wide = jnp.concatenate([jnp.zeros((8, 128), F32), wide] * n_dev, axis=0)
    i, j = spread_index((n_dev * SLOT_ROWS, 128))
    codes = jnp.where(j < 96, shift_rows(directions, 8), directions)
    codes = jnp.where((i & 8) == 8, codes, 0.0)
    small = dot_tn(hot_target, small) + jnp.where(j < 64, wide, codes)
    small_out[...] = small.astype(BF16).reshape(n_dev, SLOT_ROWS, 128)
    small_in[dev] = small_out[dev]

    entry_wait()
    exchange(lambda p: small_out.at[p], small_in.at[dev], 0, "dev")
    exchange(lambda p: layer_out.at[p], layer_in.at[dev], 2, "dev")

    z_first, z_last = z_table(active, y_mask, select_x)
    table[512:576, :] = z_first
    table[576:640, :] = z_last
    face_out[...] = (
        dot_tn(hot_out[...], table[...]).astype(BF16).reshape(n_dev, SLOT_ROWS, LANES)
    )
    face_in[dev] = face_out[dev]

    i, j = spread_index((64, LANES))
    wide = dot(fine_weight_ref[...].reshape(448, 64), one_hot(i == (j & 63)))
    weight_ref[...] = wide
    i, j = spread_index((256, 256))
    block = (i >> 6) == (j >> 6)
    for k in range(6):
        piece = weight_ref[64 * (k + 1) : 64 * (k + 2), 0:256]
        band_ref[256 * k : 256 * (k + 1), :] = jnp.where(
            block, jnp.concatenate([piece] * 4, axis=0), 0.0
        ).astype(BF16)
    z_step = (lane >> 6) - (row >> 6)
    middle = jnp.where(
        z_step == 0,
        jnp.concatenate([weight_ref[0:64, :]] * 8, axis=0),
        jnp.where(
            z_step == 1,
            jnp.concatenate([weight_ref[320:384, :]] * 8, axis=0),
            jnp.where(
                z_step == -1, jnp.concatenate([weight_ref[384:448, :]] * 8, axis=0), 0.0
            ),
        ),
    ).astype(BF16)

    def times_band(v, k):
        band = band_ref[256 * k : 256 * (k + 1), :]
        return jnp.concatenate([dot_nt(v[:, 0:256], band), dot_nt(v[:, 256:512], band)], axis=1)

    rim = jnp.concatenate([times_band(layers[k], k).astype(BF16) for k in range(6)], axis=0)

    x_at, y_at = (row >> 3) & 7, row & 7

    def shifted(v, k, edge):
        amount, at, end = ((8, x_at, 0), (-8, x_at, 7), (1, y_at, 0), (-1, y_at, 7))[k]
        return jnp.where(at == end, edge, shift_rows(v, amount))

    total = dot_nt(grad_b, middle)
    left, right = total[:, 0:256], total[:, 256:512]
    for k in range(4):
        moved = shifted(grad, k ^ 1, 0.0).astype(BF16)
        band = band_ref[256 * k : 256 * (k + 1), :]
        left = left + dot_nt(moved[:, 0:256], band)
        right = right + dot_nt(moved[:, 256:512], band)
    total = jnp.concatenate([left, right], axis=1)
    total = total + dot(hot_halo[0:512, :], rim)
    z_rows = dot(hot_halo[512:640, :], rim)
    grad_ref[...] = total

    active_f = active.astype(F32)
    halo = dot_tn(hot_halo[0:640, :], table[...]).astype(BF16)
    grad_t = grad.T.astype(BF16)
    center = dot(grad_t, active)
    conv = dot(active, middle)
    left, right = conv[:, 0:256], conv[:, 256:512]
    tap_grads = [diagonal_sum(center, 0, 0, 8)]
    for k in range(4):
        repeat = repeat_x if k < 2 else repeat_y
        moved = shifted(active_f, k, dot(repeat, halo[64 * k : 64 * k + 64])).astype(BF16)
        band = band_ref[256 * k : 256 * (k + 1), :]
        left = left + dot(moved[:, 0:256], band)
        right = right + dot(moved[:, 256:512], band)
        tap_grads.append(
            diagonal_sum(dot(grad_t[0:256], moved[:, 0:256]), 0, 0, 4)
            + diagonal_sum(dot(grad_t[256:512], moved[:, 256:512]), 0, 0, 4)
        )
    low_z = jnp.where(y_mask, dot(repeat_y, halo[256:320]), 0.0).astype(BF16)
    high_z = jnp.where(y_mask, dot(repeat_y, halo[320:384]), 0.0).astype(BF16)
    end = jnp.where(low_half, weight_ref[320:384, 0:128], 0.0).astype(BF16)
    first = dot(low_z, jnp.concatenate([end] * 8, axis=0))
    end = jnp.where(low_half, 0.0, weight_ref[384:448, 0:128]).astype(BF16)
    last = dot(high_z, jnp.concatenate([end] * 8, axis=0))
    conv_ref[...] = jnp.concatenate(
        [left[:, 0:128] + first, left[:, 128:256], right[:, 0:128], right[:, 128:256] + last],
        axis=1,
    )
    tap_grads.append(diagonal_sum(center, 0, -1, 8) + fold_lanes(dot(grad_t[0:64], low_z)))
    tap_grads.append(diagonal_sum(center, 0, 1, 8) + fold_lanes(dot(grad_t[448:512], high_z)))

    place = exact_dot(places_ref[...].astype(F32), spread_slot)
    j = iota((1, n_dev * SLOT_ROWS), 1)
    place_code = (place * 8 + (j & 7).astype(F32)).astype(jnp.int32)
    i = iota((ROWS, 1), 0)
    voxel_code = (
        ((i >> 7) * 16 + ((i >> 4) & 3) * 4 + ((i >> 1) & 3)) * 8
        + ((i >> 6) & 1) * 4
        + ((i >> 3) & 1) * 2
        + (i & 1)
    )
    first_kind = (j & 8) == 0
    hot_place = one_hot(voxel_code == jnp.where(first_kind, place_code, -1))
    hot_place_grad = one_hot(voxel_code == jnp.where(first_kind, -1, place_code))
    wait_arrived(others(small_in, n_dev), 0, "dev")
    grid = dot(hot_place, small_in[...].reshape(n_dev * SLOT_ROWS, 128)).astype(BF16)
    down = jnp.concatenate([down_weight_ref[...], jnp.zeros((64, 128), BF16)], axis=0)
    up = jnp.concatenate([jnp.zeros((64, 128), BF16), up_weight_ref[...]], axis=0)
    coarse_pre = dot(grid, down)
    coarse_sig = 1.0 / (1.0 + jnp.exp(-coarse_pre))
    coarse_act = coarse_pre * coarse_sig
    row_c = iota((ROWS, 128), 0)
    at_c = (row_c >> 6, (row_c >> 3) & 7, row_c & 7)

    def coarse_shifted(v, k):
        amount = (64, -64, 8, -8, 1, -1)[k]
        return jnp.where(at_c[k // 2] == 7 * (k % 2), 0.0, shift_rows(v, amount))

    coarse_act_f = coarse_act.astype(BF16).astype(F32)
    stack = jnp.concatenate(
        [coarse_act_f.astype(BF16)]
        + [coarse_shifted(coarse_act_f, k).astype(BF16) for k in range(6)],
        axis=1,
    )
    coarse_out = dot(stack, coarse_weight_ref[...].reshape(896, 128)).astype(BF16)
    grad_out = dot(grid, up)
    grad_out_b = grad_out.astype(BF16)
    grad_act = dot_nt(grad_out_b, coarse_weight_ref[0])
    for k in range(6):
        grad_act = grad_act + dot_nt(
            coarse_shifted(grad_out, k ^ 1).astype(BF16), coarse_weight_ref[k + 1]
        )
    grad_pre = grad_act * coarse_sig * (1.0 + coarse_pre * (1.0 - coarse_sig))
    grad_pre = grad_pre.astype(BF16)
    grad_pooled = dot_nt(grad_pre, down).astype(BF16)
    back_out[...] = (
        (dot_tn(hot_place, coarse_out) + dot_tn(hot_place_grad, grad_pooled))
        .astype(BF16)
        .reshape(n_dev, SLOT_ROWS, 128)
    )
    back_in[dev] = back_out[dev]
    exchange(lambda p: back_out.at[p], back_in.at[dev], 3, "dev")

    coarse_grad = dot_tn(stack, grad_out_b)
    down_grad = dot_tn(grid, grad_pre)
    up_grad = dot_tn(grid, coarse_out)
    part = jnp.concatenate([coarse_grad, down_grad[0:64], up_grad[64:128]], axis=0)
    coarse_part[...] = part.astype(BF16).reshape(2 * n_grp, coarse_chunk, 128)
    plane = rings["plane"][0]
    coarse_in[plane] = coarse_part[plane]
    exchange(lambda p: coarse_part.at[p], coarse_in.at[plane], 4, "plane")

    exchange(lambda p: face_out.at[p], face_in.at[dev], 1, "dev")

    marks = small_in[...].reshape(n_dev * SLOT_ROWS, 128).astype(F32)
    odd_slot = (iota((n_dev * SLOT_ROWS, 1), 0) & 8) == 8
    way = jnp.where(odd_slot, marks[:, 96:97], shift_rows(marks, -8)[:, 64:65])
    way_row = jnp.broadcast_to(way, (n_dev * SLOT_ROWS, 128)).T[0:1]
    faces_t = face_out[...].reshape(n_dev * SLOT_ROWS, LANES).astype(F32).T
    for k in range(6):
        own_faces[LANES * k : LANES * (k + 1), :] = jnp.where(
            way_row == float(k), faces_t, 0.0
        ).astype(BF16)
    tap_grads = [jnp.concatenate([t, t], axis=0).T[0:64] for t in tap_grads]
    wait_arrived(others(layer_in, n_dev), 2, "dev")
    came = layer_in[...].reshape(n_dev * SLOT_ROWS, LANES)
    for k in range(6):
        base = LANES * k
        tap_grads[k + 1] = (
            tap_grads[k + 1]
            + diagonal_sum(dot(own_faces[base : base + 256, :], came[:, 0:256]), 0, 0, 4)
            + diagonal_sum(dot(own_faces[base + 256 : base + 512, :], came[:, 256:512]), 0, 0, 4)
        )
    fine_rows = []
    for t in range(4):
        high = pltpu.roll(tap_grads[t + 4], 64, 1) if t < 3 else 0.0
        fine_rows.append(jnp.where(low_half, tap_grads[t], high))
    part = jnp.concatenate(fine_rows, axis=0)
    fine_out[...] = part.astype(BF16).reshape(n_grp, FINE_ROWS // n_grp, 128)
    fine_in[grp] = fine_out[grp]
    exchange(lambda p: fine_out.at[p], fine_in.at[grp], 7, "grp")

    rim_back = times_band(came, 0)
    for k in range(1, 6):
        rim_back = jnp.where(way == float(k), times_band(came, k), rim_back)
    rim_back = rim_back.astype(BF16)
    total = grad_ref[...] + dot(hot_out[0:512, :], rim_back)
    z_rows = (z_rows + dot(hot_out[512:640, :], rim_back)).astype(BF16)
    low_rows = lane[:, 0:128] < 64
    first = fold_lanes(jnp.where(y_mask, dot(repeat_y, z_rows[0:64]), 0.0))
    last = fold_lanes(jnp.where(y_mask, dot(repeat_y, z_rows[64:128]), 0.0))
    grad_ref[...] = jnp.concatenate(
        [
            total[:, 0:128] + jnp.where(low_rows, first, 0.0),
            total[:, 128:384],
            total[:, 384:512] + jnp.where(low_rows, 0.0, last),
        ],
        axis=1,
    )

    wait_arrived(others(coarse_in, 2 * n_grp), 4, "plane")
    part = coarse_in[0].astype(F32)
    for p in range(1, 2 * n_grp):
        part = part + coarse_in[p].astype(F32)
    coarse_mid[chip] = part.astype(BF16)
    exchange(lambda p: coarse_mid.at[chip], coarse_mid.at[chip], 5, "chip")

    wait_arrived(others(back_in, n_dev), 3, "dev")
    back = back_in[...].reshape(n_dev * SLOT_ROWS, 128)
    back_grad = dot(hot_target_grad, back).astype(BF16)
    i, j = spread_index((128, LANES))
    back_wide = jnp.where(half_mask, dot(back_grad, one_hot(i == (j & 63))), 0.0)
    total = grad_ref[...] + dot(unpool, (back_wide * (1.0 / 64.0)).astype(BF16))
    normed = normed_ref[...]
    grad_before = total * slope_ref[...]
    grad_ref[...] = grad_before
    grad_scale = fold_lanes(brick_sum(grad_before * normed))
    grad_shift = fold_lanes(brick_sum(grad_before))
    brick_all[dev] = jnp.where(low_b, grad_scale, grad_shift)
    exchange(lambda p: brick_all.at[dev], brick_all.at[dev], 9, "dev")

    wait_arrived(others(fine_in, n_grp), 7, "grp")
    part = fine_in[0].astype(F32)
    for p in range(1, n_grp):
        part = part + fine_in[p].astype(F32)
    fine_mid[dev] = part.astype(BF16)
    exchange(lambda p: fine_mid.at[dev], fine_mid.at[dev], 8, "dev")

    grad_before = grad_ref[...]
    g3 = grad_before.reshape(BRICKS, 64, LANES) * per_brick(gain)
    n3 = normed_ref[...].reshape(BRICKS, 64, LANES)
    mean_g = group_mean(jnp.sum(g3, axis=1))
    mean_gn = group_mean(jnp.sum(g3 * n3, axis=1))
    result = per_brick(inverse) * (g3 - per_brick(mean_g) - n3 * per_brick(mean_gn))
    grad = cotangent_ref[...].astype(F32)
    result = grad + result.reshape(ROWS, LANES)
    input_grad_held[...] = result.astype(BF16)
    input_grad_copy = pltpu.make_async_copy(input_grad_held, input_grad_ref, copy_sems.at[1])
    input_grad_copy.start()

    wait_arrived(others(coarse_mid, n_chip), 5, "chip")
    part = coarse_mid[0].astype(F32)
    for p in range(1, n_chip):
        part = part + coarse_mid[p].astype(F32)
    coarse_all[plane] = part.astype(BF16)
    exchange(lambda p: coarse_all.at[plane], coarse_all.at[plane], 6, "plane")

    coarse_values = dot(hot_target, back).astype(BF16)
    i, j = spread_index((64, LANES))
    up_wide = dot_tn(up_weight_ref[...], one_hot(i == (j & 63))).astype(BF16)
    upward = jnp.where(half_mask, dot(coarse_values, up_wide), 0.0)
    upward_high = upward.astype(BF16)
    upward_low = (upward - upward_high.astype(F32)).astype(BF16)
    upward = dot(unpool, upward_high) + dot(unpool, upward_low)
    features = features_ref[...].astype(F32)
    conv_ref[...] = features + conv_ref[...] + upward
    i, j = spread_index((ROWS, 256))
    x, y = (i >> 3) & 7, i & 7
    by_x = (j & 63) == ((i >> 6) * 8 + y)
    by_y = (j & 63) == (i >> 3)
    way = j >> 6
    edges = one_hot(
        ((way == 0) & (x == 0) & by_x)
        | ((way == 1) & (x == 7) & by_x)
        | ((way == 2) & (y == 0) & by_y)
        | ((way == 3) & (y == 7) & by_y)
    )

    wait_arrived(others(brick_all, n_dev), 9, "dev")
    embeddings = small_in[...].astype(F32)[:, 8:16, :].reshape(n_dev * BRICKS, 128)
    time_grad = lax.dot_general(
        embeddings,
        brick_all[...].reshape(n_dev * BRICKS, 128),
        (((0,), (0,)), ((), ())),
        precision=lax.Precision.HIGHEST,
        preferred_element_type=F32,
    )
    time_all[grp] = time_grad[0:64].astype(BF16)
    exchange(lambda p: time_all.at[grp], time_all.at[grp], 11, "grp")

    wait_arrived(others(fine_mid, n_dev), 8, "dev")
    part = fine_mid[0].astype(F32)
    for p in range(1, n_dev):
        part = part + fine_mid[p].astype(F32)
    fine_all[grp] = part.astype(BF16)
    exchange(lambda p: fine_all.at[grp], fine_all.at[grp], 10, "grp")

    wait_arrived(others(face_in, n_dev), 1, "dev")
    halo = dot_tn(hot_halo[640 : 640 + n_dev * SLOT_ROWS, :], face_in[...].reshape(-1, LANES))
    halo = halo.astype(BF16)
    sides = []
    for k in range(6):
        band = band_ref[256 * k : 256 * (k + 1), :]
        piece = halo[64 * k : 64 * k + 64]
        sides.append(
            jnp.concatenate([dot(piece[:, 0:256], band), dot(piece[:, 256:512], band)], axis=1)
            .astype(BF16)
        )
    mixed = conv_ref[...] + dot(edges, jnp.concatenate(sides[0:4], axis=0))
    first = fold_lanes(jnp.where(y_mask, dot(repeat_y, sides[4]), 0.0))
    last = fold_lanes(jnp.where(y_mask, dot(repeat_y, sides[5]), 0.0))
    mixed = jnp.concatenate(
        [
            mixed[:, 0:128] + jnp.where(low_rows, first, 0.0),
            mixed[:, 128:384],
            mixed[:, 384:512] + jnp.where(low_rows, 0.0, last),
        ],
        axis=1,
    )
    mixed_held[...] = mixed.astype(BF16)
    mixed_copy = pltpu.make_async_copy(mixed_held, mixed_ref, copy_sems.at[0])
    mixed_copy.start()

    wait_arrived(others(coarse_all, 2 * n_grp), 6, "plane")
    coarse_sum_ref[...] = coarse_all[...].reshape(COARSE_ROWS, 128)
    wait_arrived(others(fine_all, n_grp), 10, "grp")
    fine_sum_ref[...] = fine_all[...].reshape(FINE_ROWS, 128)
    wait_arrived(others(time_all, n_grp), 11, "grp")
    part = time_all[0].astype(F32)
    for p in range(1, n_grp):
        part = part + time_all[p].astype(F32)
    time_sum_ref[...] = part

    wait_sent(others(small_out, n_dev), 0, "dev")
    wait_sent(others(face_out, n_dev), 1, "dev")
    wait_sent(others(layer_out, n_dev), 2, "dev")
    wait_sent(others(back_out, n_dev), 3, "dev")
    wait_sent(others(coarse_part, 2 * n_grp), 4, "plane")
    wait_sent(others(coarse_mid, n_chip), 5, "chip")
    wait_sent(others(coarse_all, 2 * n_grp), 6, "plane")
    wait_sent(others(fine_out, n_grp), 7, "grp")
    wait_sent(others(fine_mid, n_dev), 8, "dev")
    wait_sent(others(brick_all, n_dev), 9, "dev")
    wait_sent(others(fine_all, n_grp), 10, "grp")
    wait_sent(others(time_all, n_grp), 11, "grp")
    mixed_copy.wait()
    input_grad_copy.wait()


def finish(
    mixed_in,
    input_grad_in,
    coarse_sum_ref,
    fine_sum_ref,
    time_sum_ref,
    mixed_ref,
    input_grad_ref,
    fine_grad_ref,
    down_grad_ref,
    coarse_grad_ref,
    up_grad_ref,
    time_grad_ref,
):
    mixed_ref[...] = mixed_in[...]
    input_grad_ref[...] = input_grad_in[...]
    coarse_grad_ref[...] = coarse_sum_ref[0:896, :].astype(F32).reshape(7, 128, 128)
    down_grad_ref[...] = coarse_sum_ref[896:960, :].astype(F32)
    up_grad_ref[...] = coarse_sum_ref[960:1024, :].astype(F32)
    for t in range(4):
        piece = fine_sum_ref[64 * t : 64 * t + 64, :].astype(F32)
        fine_grad_ref[t] = piece[:, 0:64]
        if t < 3:
            fine_grad_ref[t + 4] = pltpu.roll(piece, 64, 1)[:, 0:64]
    time_grad_ref[...] = time_sum_ref[...]


def body(n_grp, n_dev, *args):
    half = 32
    frequency = np.exp(-math.log(10000.0) * np.arange(half) / half).astype(np.float32)
    frequency = jnp.asarray(np.concatenate([frequency, frequency])[None, :])
    args = list(args)
    whole = args[0].shape
    args[0] = args[0].reshape(ROWS, LANES)
    args[1] = args[1].reshape(ROWS, LANES)
    args[4] = jnp.swapaxes(args[4], 1, 2)
    args[6] = args[6].reshape(1, n_dev)
    args[11] = args[11].T
    args.append(frequency)
    vmem = pl.BlockSpec(memory_space=pltpu.VMEM)
    free = pl.BlockSpec(memory_space=pl.ANY)
    packed = jax.ShapeDtypeStruct((ROWS, LANES), BF16)
    slots = (n_dev, SLOT_ROWS)
    coarse_chunk = COARSE_ROWS // 2 // n_grp
    fine_chunk = FINE_ROWS // n_grp
    held = pl.pallas_call(
        functools.partial(kernel, n_grp, n_dev),
        out_shape=(
            packed,
            packed,
            jax.ShapeDtypeStruct((COARSE_ROWS, 128), BF16),
            jax.ShapeDtypeStruct((FINE_ROWS, 128), BF16),
            jax.ShapeDtypeStruct((64, 128), F32),
        ),
        in_specs=[free] * 13,
        out_specs=(free, free, vmem, vmem, vmem),
        scratch_shapes=[
            pltpu.VMEM(slots + (128,), BF16),
            pltpu.VMEM(slots + (128,), BF16),
            pltpu.VMEM(slots + (LANES,), BF16),
            pltpu.VMEM(slots + (LANES,), BF16),
            pltpu.VMEM(slots + (LANES,), BF16),
            pltpu.VMEM(slots + (LANES,), BF16),
            pltpu.VMEM(slots + (128,), BF16),
            pltpu.VMEM(slots + (128,), BF16),
            pltpu.VMEM((2 * n_grp, coarse_chunk, 128), BF16),
            pltpu.VMEM((2 * n_grp, coarse_chunk, 128), BF16),
            pltpu.VMEM((n_dev // 2, coarse_chunk, 128), BF16),
            pltpu.VMEM((2 * n_grp, coarse_chunk, 128), BF16),
            pltpu.VMEM((n_grp, fine_chunk, 128), BF16),
            pltpu.VMEM((n_grp, fine_chunk, 128), BF16),
            pltpu.VMEM((n_dev, fine_chunk, 128), BF16),
            pltpu.VMEM((n_grp, fine_chunk, 128), BF16),
            pltpu.VMEM((n_dev, BRICKS, 128), F32),
            pltpu.VMEM((n_grp, 64, 128), BF16),
            pltpu.VMEM((ROWS, LANES), BF16),
            pltpu.VMEM((ROWS, LANES), BF16),
            pltpu.VMEM((6 * LANES, n_dev * SLOT_ROWS), BF16),
            pltpu.VMEM((640 + n_dev * SLOT_ROWS, 384), BF16),
            pltpu.VMEM((640, n_dev * SLOT_ROWS), BF16),
            pltpu.VMEM((640, LANES), BF16),
            pltpu.VMEM((ROWS, LANES), F32),
            pltpu.VMEM((ROWS, LANES), F32),
            pltpu.VMEM((ROWS, LANES), F32),
            pltpu.VMEM((ROWS, LANES), F32),
            pltpu.VMEM((448, LANES), F32),
            pltpu.VMEM((1536, 256), BF16),
            pltpu.SemaphoreType.DMA((12,)),
            pltpu.SemaphoreType.DMA((12,)),
            pltpu.SemaphoreType.DMA((2,)),
        ]
        + [pltpu.VMEM(a.shape, a.dtype) for a in args]
        + [pltpu.SemaphoreType.DMA((13,))],
        compiler_params=pltpu.CompilerParams(
            collective_id=0, has_side_effects=True, vmem_limit_bytes=56 * 1024 * 1024
        ),
    )(*args)
    outs = pl.pallas_call(
        finish,
        out_shape=(
            packed,
            packed,
            jax.ShapeDtypeStruct((7, 64, 64), F32),
            jax.ShapeDtypeStruct((64, 128), F32),
            jax.ShapeDtypeStruct((7, 128, 128), F32),
            jax.ShapeDtypeStruct((64, 128), F32),
            jax.ShapeDtypeStruct((64, 128), F32),
        ),
        in_specs=[vmem] * 5,
        out_specs=(vmem,) * 7,
        compiler_params=pltpu.CompilerParams(vmem_limit_bytes=56 * 1024 * 1024),
    )(*held)
    return outs[0].reshape(whole), outs[1].reshape(whole), outs[2], outs[3], outs[4], outs[5].T, outs[6]


def solution(mesh):
    split = ("grp", "dev")
    in_specs = (
        P(split, None, None, None),
        P(split, None, None, None),
        P(split),
        P(split, None),
        P(split, None, None),
        P(split),
        P(split, None, None),
        P(),
        P(),
        P(),
        P(),
        P(),
    )
    out_specs = (
        P(split, None, None, None),
        P(split, None, None, None),
        P(),
        P(),
        P(),
        P(),
        P(),
    )
    return jax.shard_map(
        functools.partial(body, mesh.shape["grp"], mesh.shape["dev"]),
        mesh=mesh,
        in_specs=in_specs,
        out_specs=out_specs,
        check_vma=False,
    )
```
